128 devices in a mesh: patch: 8 (over y, core), bulk: 16 (over z, x).
Axes of the slice: x: 4, y: 4, z: 4, core: 2. Of those that a mesh axis runs over, the one named last changes fastest.
Arguments:
- positions: float32 [3, 2097152], P(None, ('patch', 'bulk')), may hold values from -4 to 4
- masses: float32 [2097152], P(('patch', 'bulk')), may hold values from 0.004 to 0.04
- smoothing: float32 [2097152], P(('patch', 'bulk')), may hold values from 0.8 to 1.6
- energy: float32 [2097152], P(('patch', 'bulk')), may hold values from 0.3 to 3
- level_ids: int32 [16384], P(('patch', 'bulk')), may hold values from 0 to 2
- send_list: int32 [128, 20, 8], P(('patch', 'bulk')), may hold values from 0 to 127
- pair_list: int32 [128, 2, 672], P(('patch', 'bulk')), may hold values from 0 to 287, as said below
- pair_count: int32 [128], P(('patch', 'bulk')), may hold values from 416 to 672, as said below
Outputs:
- density: float32 [2097152], P(('patch', 'bulk'))
- accel: float32 [3, 2097152], P(None, ('patch', 'bulk'))
The draws below stay inside these ranges and needn't reach their ends.
Inputs may be any that keep to these rules, and one draw needn't show every extreme that they name: `send_list`: each entry names one of the sending device's own blocks. `pair_list`: row 0 names own blocks, row 1 names blocks of the extended set, never the pair's own block a itself by the same index; the first 160 pairs of each device join extended block 128 + k, for k in order, with some own block. `pair_count`: some device has all slots live.
All inputs are finite; a program needn't handle non-finite values.
Results may differ from the reference program's by a relative error of at most 0.0003.
Values sent between devices are 32-bit elements; how exact they have to be, the bound alone decides.
A program may use at most 64 MiB of HBM per device.

```python
import math
import jax
import jax.numpy as jnp
from jax import lax

B = 128
NB = 128
G = 8
NEIGH = 20
LEVELS = 3
GHOSTS = 160
EXT = 288
NPAIR = 672
BLOCKS = 16384
PARTS_SIZE = 2097152
N_BULK = 16
DEVICES = 128


def draw_pair_list(key, part):
    key = jax.random.fold_in(key, 11)
    key_one, key_two, key_three = jax.random.split(key, 3)
    cover_a = jax.random.randint(key_one, (DEVICES, GHOSTS), 0, NB)
    cover_b = jnp.broadcast_to(NB + jnp.arange(GHOSTS, dtype=jnp.int32), (DEVICES, GHOSTS))
    rest_a = jax.random.randint(key_two, (DEVICES, 4 * NB), 0, NB)
    offset = jax.random.randint(key_three, (DEVICES, 4 * NB), 1, EXT)
    rest_b = (rest_a + offset) % EXT
    first = jnp.concatenate([cover_a, rest_a], 1)
    second = jnp.concatenate([cover_b, rest_b], 1)
    return jnp.stack([first, second], 1).astype(jnp.int32)


def draw_pair_count(key, part):
    key = jax.random.fold_in(key, 12)
    key_one, key_two = jax.random.split(key)
    counts = GHOSTS + jax.random.randint(key_one, (DEVICES,), 2 * NB, 4 * NB + 1)
    fullest = jax.random.randint(key_two, (), 0, DEVICES)
    return counts.at[fullest].set(NPAIR).astype(jnp.int32)


def with_ends(drawn, key, least, high):
    dims = drawn.shape
    spot = [jax.random.randint(jax.random.fold_in(key, axis), (), 0, dims[axis]) for axis in range(len(dims))]
    drawn = drawn.at[tuple(spot)].set(least)
    longest = dims.index(max(dims))
    spot[longest] = (spot[longest] + 1) % dims[longest]
    return drawn.at[tuple(spot)].set(high)


def block_levels(stream_key, dims, cuts, low, high):
    factor_of = 1.0
    for dim, shards_of in cuts:
        draws = jax.random.uniform(jax.random.fold_in(jax.random.fold_in(stream_key, 6), dim), (shards_of,), jnp.float32, low / len(cuts), high / len(cuts))
        factor_of = factor_of * jnp.repeat(jnp.exp(draws), dims[dim] // shards_of).reshape((-1,) + (1,) * (len(dims) - 1 - dim))
    return factor_of


def centred(key, shape, width, reach, pieces=(), kind=jnp.bfloat16):
    values = jax.random.normal(key, shape, jnp.float32) * width
    if len(pieces) > 0:
        values = block_levels(key, shape, pieces, -0.22, 0.18) * values
    return jnp.clip(values, min=-reach, max=reach).astype(kind)


def setup_inputs(seed: int = 0) -> dict:
    splits = jax.random.split(jax.random.key(seed), 9)
    positions = centred(splits[0], (3, PARTS_SIZE), 0.6, 4.0, ((1, 128),), jnp.float32)
    masses = jnp.clip(jnp.exp(math.log(0.04) - 2.30258502 * jax.random.uniform(splits[1], (PARTS_SIZE,), jnp.float32) ** block_levels(splits[1], (PARTS_SIZE,), ((0, 128),), -0.2, 0.2)), 0.004, 0.04)
    smoothing = jnp.clip(jnp.exp(math.log(1.6) - 0.6931472 * jax.random.uniform(splits[2], (PARTS_SIZE,), jnp.float32) ** block_levels(splits[2], (PARTS_SIZE,), ((0, 128),), -0.2, 0.2)), 0.8, 1.6)
    energy = jnp.clip(jnp.exp(math.log(3.0) - 2.3025851 * jax.random.uniform(splits[3], (PARTS_SIZE,), jnp.float32) ** block_levels(splits[3], (PARTS_SIZE,), ((0, 128),), -0.2, 0.2)), 0.3, 3.0)
    level_ids = with_ends(jax.random.randint(splits[4], (BLOCKS,), 0, LEVELS), jax.random.fold_in(splits[4], 1), 0, LEVELS - 1).astype(jnp.int32)
    send_list = with_ends(jax.random.randint(splits[5], (DEVICES, NEIGH, G), 0, NB), jax.random.fold_in(splits[5], 1), 0, NB - 1).astype(jnp.int32)
    pair_list = draw_pair_list(jax.random.fold_in(splits[8], 71), 0)
    pair_count = draw_pair_count(jax.random.fold_in(splits[8], 71), 0)
    return {"positions": positions, "masses": masses, "smoothing": smoothing, "energy": energy, "level_ids": level_ids, "send_list": send_list, "pair_list": pair_list, "pair_count": pair_count}


NORM = 21.0 / (2.0 * math.pi)
GAMMA_LESS = 2.0 / 3.0
SHRINK = 0.8

def neighbour_offsets(bulk_count):
    return [step_patch * bulk_count + step_bulk for step_patch in (-1, 0, 1) for step_bulk in range(-3, 4) if (step_patch, step_bulk) != (0, 0)]

def kernel_terms(xa, xb, ha, hb):
    dx = xa[:, :, None] - xb[:, None, :]
    dist = jnp.sqrt(lax.optimization_barrier(jnp.sum(dx * dx, axis=0)))
    hij = 0.5 * (ha[:, None] + hb[None, :])
    qval = dist / hij
    tail = jnp.maximum(1.0 - qval, 0.0)
    inverse = 1.0 / hij
    weight = NORM * inverse ** 3 * tail ** 4 * (1.0 + 4.0 * qval)
    slope = -20.0 * NORM * inverse ** 5 * tail ** 3
    return (dx, weight, slope)

def density_pair(rec_a, rec_b):
    dx, weight, slope = kernel_terms(rec_a[0:3], rec_b[0:3], rec_a[4], rec_b[4])
    return (lax.optimization_barrier(jnp.sum(weight * rec_b[3][None, :], axis=1)), lax.optimization_barrier(jnp.sum(weight * rec_a[3][:, None], axis=0)))

def force_pair(rec_a, rec_b, press_a, press_b):
    dx, weight, slope = kernel_terms(rec_a[0:3], rec_b[0:3], rec_a[4], rec_b[4])
    coef = slope * (press_a[:, None] + press_b[None, :])
    to_a = -lax.optimization_barrier(jnp.sum((coef * rec_b[3][None, :])[None] * dx, axis=2))
    to_b = lax.optimization_barrier(jnp.sum((coef * rec_a[3][:, None])[None] * dx, axis=1))
    return (to_a, to_b)

def self_density(rec):
    return density_pair(rec, rec)[0]

def self_force(rec, press):
    return force_pair(rec, rec, press, press)[0]

def reference(positions, masses, smoothing, energy, level_ids, send_list, pair_list, pair_count):
    pos = positions.reshape(3, BLOCKS, B)
    smooth = smoothing.reshape(BLOCKS, B) * SHRINK ** level_ids.astype(jnp.float32)[:, None]
    record = jnp.concatenate([pos, masses.reshape(1, BLOCKS, B), smooth[None], energy.reshape(1, BLOCKS, B)], 0)
    offsets = jnp.array(neighbour_offsets(N_BULK), dtype=jnp.int32)
    devices = jnp.arange(DEVICES, dtype=jnp.int32)
    sources = ((devices[:, None] - offsets[None, :]) % DEVICES).astype(jnp.int32)
    which = jnp.arange(NEIGH, dtype=jnp.int32)[None, :]
    chosen = send_list[sources, which]
    flat_targets = (sources[:, :, None] * NB + chosen).astype(jnp.int32).reshape(DEVICES, GHOSTS)

    def setup(device):
        start = (device * NB).astype(jnp.int32)
        local = lax.dynamic_slice_in_dim(record, start, NB, 1)
        extended = jnp.concatenate([local, record[:, flat_targets[device]]], 1)
        first = pair_list[device, 0]
        second = pair_list[device, 1]
        live = (jnp.arange(NPAIR, dtype=jnp.int32) < pair_count[device]).astype(jnp.float32)
        return (start, local, extended, first, second, live)

    def pass_one(device):
        start, local, extended, first, second, live = setup(device)
        rows_a = jnp.moveaxis(extended[:, first], 1, 0)
        rows_b = jnp.moveaxis(extended[:, second], 1, 0)
        to_a, to_b = jax.vmap(density_pair)(rows_a, rows_b)
        dens_ext = jax.ops.segment_sum(to_a * live[:, None], first, EXT) + jax.ops.segment_sum(to_b * live[:, None], second, EXT)
        own = jax.vmap(self_density)(jnp.moveaxis(local, 1, 0))
        return (own + dens_ext[:NB], dens_ext[NB:])
    local_dens, ghost_dens = lax.map(pass_one, devices)
    density = local_dens.reshape(BLOCKS, B) + jax.ops.segment_sum(ghost_dens.reshape(DEVICES * GHOSTS, B), flat_targets.reshape(-1), BLOCKS)
    press = GAMMA_LESS * energy.reshape(BLOCKS, B) / density

    def pass_two(device):
        start, local, extended, first, second, live = setup(device)
        local_press = lax.dynamic_slice_in_dim(press, start, NB, 0)
        ext_press = jnp.concatenate([local_press, press[flat_targets[device]]], 0)
        rows_a = jnp.moveaxis(extended[:, first], 1, 0)
        rows_b = jnp.moveaxis(extended[:, second], 1, 0)
        to_a, to_b = jax.vmap(force_pair)(rows_a, rows_b, ext_press[first], ext_press[second])
        acc_ext = jax.ops.segment_sum(to_a * live[:, None, None], first, EXT) + jax.ops.segment_sum(to_b * live[:, None, None], second, EXT)
        own = jax.vmap(self_force)(jnp.moveaxis(local, 1, 0), local_press)
        return (own + acc_ext[:NB], acc_ext[NB:])
    local_acc, ghost_acc = lax.map(pass_two, devices)
    accel = local_acc.reshape(BLOCKS, 3, B) + jax.ops.segment_sum(ghost_acc.reshape(DEVICES * GHOSTS, 3, B), flat_targets.reshape(-1), BLOCKS)
    return (density.reshape(PARTS_SIZE), jnp.moveaxis(accel, 1, 0).reshape(3, PARTS_SIZE))
```

```python
import functools
import math

import jax
import jax.numpy as jnp
from jax import lax
from jax.experimental import pallas as pl
from jax.experimental.pallas import tpu as pltpu
from jax.sharding import PartitionSpec as P

SHRINK = 0.8
NORM = 21.0 / (2.0 * math.pi)
bf16=jnp.bfloat16; f32=jnp.float32
CH8=[(0,0),(0,1),(1,0),(1,1),(0,2),(2,0),(1,2),(2,1)]
E=288

def split3(v):
    a=v.astype(bf16).astype(f32); r=v-a
    b=r.astype(bf16).astype(f32)
    return a,b,r-b
def hilo(v):
    hi=v.astype(bf16)
    return hi,(v-hi.astype(f32)).astype(bf16)

def tile_math(r2,hs):
    r2=jnp.maximum(r2,1e-30)
    s=pl.reciprocal(hs,approx=True)
    d=r2*lax.rsqrt(r2)
    q=d*s
    t=jnp.maximum(1.0-q,0.0)
    st=s*t
    c=st*st*st
    S=c*(s*s)
    W=c*(t*(q+0.25))
    return W,S

def k2(opt, G, U, pairs, count, own_ref, gh_ref, dens_ref, s_ref, C, CA, AF, BF, MM, GB, WB, acc):
    step=pl.program_id(0)
    NP=pairs.shape[1]; TOT=NP+128
    def ab(k):
        kk=jnp.maximum(k-128,0)
        a=jnp.where(k<128,k,pairs[0,kk]); b=jnp.where(k<128,k,pairs[1,kk])
        return a,b
    def targets(k):
        a,b=ab(k)
        live=k<128+count[0]
        return a,b,jnp.where(live,a,E),jnp.where(live&(k>=128),b,E)
    def first_stage(k,j):
        a,b=ab(k)
        GB[j]=jnp.dot(AF[a],BF[b],preferred_element_type=f32)
    def last_stage(k,j):
        a,b,ta,tb=targets(k)
        pa=lax.dot_general(MM[b],jnp.concatenate([WB[j,0],WB[j,1]],1),(((1,),(1,)),((),())),preferred_element_type=f32)
        pb=jnp.dot(MM[a],jnp.concatenate([WB[j,0],WB[j,1]],0),preferred_element_type=f32)
        if opt.get('only')=='a': return [(ta,pa)]
        if opt.get('only')=='b': return [(tb,pb)]
        if opt.get('only')=='m':
            return [(ta,jnp.dot(jnp.concatenate([WB[j,0],WB[j,1]],1),AF[b,:,:].reshape(128,64) if 0 else jnp.concatenate([MM[b,:,:128].astype(f32).T.astype(bf16)]*2,0),preferred_element_type=f32)[:16].reshape(16,16)),(tb,pb)]
        return [(ta,pa),(tb,pb)]
    def add(res):
        for i,r in res:
            acc[i]+=r[:8]+r[8:]
    @pl.when(step==0)
    def _():
        one=jnp.ones((E,128),f32); zero=jnp.zeros((E,128),f32)
        C[3*E:4*E]=one; C[10*E:11*E]=one
        for i in (5,6,7,8,11,12,17,18,19,20): C[i*E:(i+1)*E]=zero
        CA[4*128:5*128]=one[:128]
        for i in (6,7): CA[i*128:(i+1)*128]=zero[:128]
        x,y,z,m,h=[own_ref[c] for c in range(5)]
        n=x*x+y*y+z*z; hh=0.5*h
        for i,v in ((0,x),(1,y),(2,z),(4,n),(9,hh),(13,m),(14,m*x),(15,m*y),(16,m*z)):
            C[i*E:i*E+128]=v
        for i,v in ((0,-2*x),(1,-2*y),(2,-2*z),(3,n),(5,hh)):
            CA[i*128:(i+1)*128]=v
        for k in range(20):
            x,y,z,m,h=[gh_ref[k,c] for c in range(5)]
            n=x*x+y*y+z*z; hh=0.5*h
            for i,v in ((0,x),(1,y),(2,z),(4,n),(9,hh),(13,m),(14,m*x),(15,m*y),(16,m*z)):
                o=i*E+128+k*8
                C[o:o+8]=v
        acc[...]=jnp.zeros_like(acc)
        WB[...]=jnp.zeros_like(WB)
        def blk(i,_):
            for j in range(4):
                b=i*4+j
                for w,c in ((0,0),(5,128)):
                    p=split3(C[pl.ds(w*E+b,8,stride=E),:])
                    f=jnp.concatenate([p[q] for _,q in CH8],0).astype(bf16)
                    BF[b,:,c:c+128]=f
                mv=C[pl.ds(13*E+b,8,stride=E),:]
                hi=mv.astype(bf16).astype(f32)
                mm=jnp.concatenate([hi,mv-hi],0).astype(bf16)
                MM[b,:,:128]=mm; MM[b,:,128:]=mm
            return 0
        lax.fori_loop(0,E//4,blk,0)
        def blka(i,_):
            for j in range(4):
                b=i*4+j
                p=split3(CA[pl.ds(b,8,stride=128),:])
                f=jnp.concatenate([p[q] for q,_ in CH8],0)
                if opt.get('bt'):
                    AF[b]=f.astype(bf16).T
                else:
                    AF[b]=f.T.astype(bf16)
            return 0
        lax.fori_loop(0,32,blka,0)
        for j in range(U): first_stage(j,j)
    def body(u,_):
        k0=step*G+u*U
        res=[]
        for j in range(U):
            if not opt.get('no3'): res+=last_stage(jnp.maximum(k0-U+j,0),j)
        for j in range(U):
            for r in range(0,0 if opt.get('no2') else 128,opt.get('rows',32)):
                rows=opt.get('rows',32)
                W,S=tile_math(GB[j,r:r+rows,:128],GB[j,r:r+rows,128:])
                Shi,Slo=hilo(S)
                s_ref[u*U+j,r:r+rows]=Shi; s_ref[u*U+j,128+r:128+r+rows]=Slo
                Whi,Wlo=hilo(W)
                WB[j,0,r:r+rows]=Whi; WB[j,1,r:r+rows]=Wlo
            if not opt.get('no1'): first_stage(jnp.minimum(k0+U+j,TOT-1),j)
        add(res)
        return 0
    lax.fori_loop(0,0 if opt.get('no') else G//U,body,0)
    @pl.when(step==pl.num_programs(0)-1)
    def _():
        res=[]
        for j in range(U): res+=last_stage(TOT-U+j,j)
        add(res)
        for i in range(E//8):
            dens_ref[i*8:i*8+8]=acc[i*8:i*8+8,0,:]*(4*NORM)

def run_k2(pairs,count,own,gh,opt,G=16,U=2):
    NP=pairs.shape[1]
    n=(NP+128)//G
    return pl.pallas_call(functools.partial(k2,opt,G,U),
      grid_spec=pltpu.PrefetchScalarGridSpec(num_scalar_prefetch=2,grid=(n,),
        in_specs=[pl.BlockSpec(memory_space=pltpu.VMEM)]*2,
        out_specs=[pl.BlockSpec(memory_space=pltpu.VMEM),pl.BlockSpec((G,256,128),lambda i,*_:(0 if opt.get('nodma') else i,0,0))],
        scratch_shapes=[pltpu.VMEM((21*E,128),f32),pltpu.VMEM((8*128,128),f32),
          pltpu.VMEM((128,128,64),bf16),pltpu.VMEM((E,64,256),bf16),pltpu.VMEM((E,16,256),bf16),
          pltpu.VMEM((U,128,256),f32),pltpu.VMEM((U,2,128,128),bf16),pltpu.VMEM((E+1,8,128),f32)]),
      out_shape=[jax.ShapeDtypeStruct((E,128),f32),jax.ShapeDtypeStruct((NP+128,256,128),bf16)],
      compiler_params=pltpu.CompilerParams(vmem_limit_bytes=60*2**20),
      name="k2")(pairs,count,own,gh)

def k4(opt, G, U, pairs, count, own_ref, gh_ref, press_ref, gpress_ref, s_ref, acc_o, acc_g, C, MM, acc, accA):
    step=pl.program_id(0)
    NP=pairs.shape[1]; TOT=NP+128
    def targets(k):
        kk=jnp.maximum(k-128,0)
        a=jnp.where(k<128,k,pairs[0,kk]); b=jnp.where(k<128,k,pairs[1,kk])
        live=k<128+count[0]
        return a,b,jnp.where(live,a,128 if opt.get('astream') else E),jnp.where(live&(k>=128),b,E)
    @pl.when(step==0)
    def _():
        x,y,z,m=[own_ref[c] for c in range(4)]
        p=press_ref[...]; pm=p*m
        for i,v in enumerate((m,m*x,m*y,m*z,pm,pm*x,pm*y,pm*z)): C[i*E:i*E+128]=v
        for k in range(20):
            x,y,z,m=[gh_ref[k,c] for c in range(4)]
            p=gpress_ref[k*8:k*8+8]; pm=p*m
            o=128+k*8
            for i,v in enumerate((m,m*x,m*y,m*z,pm,pm*x,pm*y,pm*z)): C[i*E+o:i*E+o+8]=v
        acc[...]=jnp.zeros_like(acc)
        if opt.get('astream'): accA[...]=jnp.zeros_like(accA)
        def blk(i,_):
            for j in range(4):
                b=i*4+j
                mv=C[pl.ds(b,8,stride=E),:]
                hi=mv.astype(bf16).astype(f32)
                mm=jnp.concatenate([hi,mv-hi],0).astype(bf16)
                MM[b,:,:128]=mm; MM[b,:,128:]=mm
            return 0
        lax.fori_loop(0,E//4,blk,0)
    def body(u,_):
        resa=[];resb=[]
        for j in range(U):
            k=step*G+u*U+j
            a,b,ta,tb=targets(k)
            hi=s_ref[u*U+j,:128]; lo=s_ref[u*U+j,128:]
            if not opt.get('nob'):
                resb.append((tb,jnp.dot(MM[a],s_ref[u*U+j],preferred_element_type=f32)))
            if not opt.get('noa'):
                cat=jnp.concatenate([hi,lo],1)
                if opt.get('astream'):
                    resa.append((ta,lax.dot_general(cat,MM[b],(((1,),(1,)),((),())),preferred_element_type=f32)))
                else:
                    resb.append((ta,lax.dot_general(MM[b],cat,(((1,),(1,)),((),())),preferred_element_type=f32)))
        for i,r in resb: acc[i]+=r[:8]+r[8:]
        for i,r in resa: accA[i]+=r
        return 0
    lax.fori_loop(0,G//U,body,0)
    @pl.when(step==pl.num_programs(0)-1)
    def _():
        if opt.get('astream'):
            def fin(i,_):
                t=jnp.concatenate([accA[i],jnp.zeros((128,112),f32)],1).T
                acc[i]+=t[:8]+t[8:16]
                return 0
            lax.fori_loop(0,128,fin,0)
        def final(x,y,z,p,A):
            m0=p*A[0]+A[4]
            return [p*A[c+1]+A[c+5]-v*m0 for c,v in enumerate((x,y,z))]
        K=-20.0*NORM
        for i in range(16):
            r=slice(i*8,i*8+8)
            x,y,z=[own_ref[c,r] for c in range(3)]
            A=[acc[r,c,:] for c in range(8)]
            o=final(x,y,z,press_ref[r],A)
            for c in range(3): acc_o[c,r]=o[c]*K
        for i in range(20):
            x,y,z=[gh_ref[i,c] for c in range(3)]
            A=[acc[128+i*8:136+i*8,c,:] for c in range(8)]
            o=final(x,y,z,gpress_ref[i*8:i*8+8],A)
            for c in range(3): acc_g[i,c]=o[c]*K

def run_k4(pairs,count,own,gh,press,gpress,S,opt,G=16,U=2):
    NP=pairs.shape[1]
    n=(NP+128)//G
    V=pl.BlockSpec(memory_space=pltpu.VMEM)
    return pl.pallas_call(functools.partial(k4,opt,G,U),
      grid_spec=pltpu.PrefetchScalarGridSpec(num_scalar_prefetch=2,grid=(n,),
        in_specs=[V]*4+[pl.BlockSpec((G,256,128),lambda i,*_:(0 if opt.get('nodma') else i,0,0))],
        out_specs=[V,V],
        scratch_shapes=[pltpu.VMEM((8*E,128),f32),pltpu.VMEM((E,16,256),bf16),pltpu.VMEM((E+1,8,128),f32),pltpu.VMEM((129 if opt.get('astream') else 1,128,16),f32)]),
      out_shape=[jax.ShapeDtypeStruct((3,128,128),f32),jax.ShapeDtypeStruct((20,3,8,128),f32)],
      compiler_params=pltpu.CompilerParams(vmem_limit_bytes=60*2**20),
      name="k4")(pairs,count,own,gh,press,gpress,S)


MESH = pl.DeviceIdType.MESH
NB = 128
NEIGH = 20
G8 = 8


def neighbour_steps():
    return [
        (step_patch, step_bulk)
        for step_patch in (-1, 0, 1)
        for step_bulk in range(-3, 4)
        if (step_patch, step_bulk) != (0, 0)
    ]


def place(offset):
    rows, columns = lax.axis_size("patch"), lax.axis_size("bulk")
    count = rows * columns
    me = lax.axis_index("patch") * columns + lax.axis_index("bulk")
    other = lax.rem(me + (offset + count), count)
    return (lax.div(other, columns), lax.rem(other, columns))


def offsets():
    columns = lax.axis_size("bulk")
    return [u * columns + v for u, v in neighbour_steps()]


def meet():
    barrier = pltpu.get_barrier_semaphore()
    for o in offsets():
        pl.semaphore_signal(barrier, inc=1, device_id=place(o), device_id_type=MESH)
    pl.semaphore_wait(barrier, NEIGH)


def start_all(src, dst, send_sem, recv_sem, sign):
    copies = []
    for n, o in enumerate(offsets()):
        copy = pltpu.make_async_remote_copy(
            src_ref=src.at[n], dst_ref=dst.at[n], send_sem=send_sem.at[n], recv_sem=recv_sem.at[n],
            device_id=place(sign * o), device_id_type=MESH)
        copy.start()
        copies.append(copy)
    return copies


def split_dot(hot, v):
    a = v.astype(bf16)
    r = v - a.astype(f32)
    b = r.astype(bf16)
    c = (r - b.astype(f32)).astype(bf16)
    dot = functools.partial(jnp.dot, preferred_element_type=f32)
    return dot(hot, a) + (dot(hot, b) + dot(hot, c))


def one_hot(which_ref):
    rows = lax.broadcasted_iota(jnp.int32, (NB, NEIGH * G8), 0)
    return (rows == which_ref[...]).astype(f32).astype(bf16)


def forward_kernel(send_list, rec, out, buf, send_sem, recv_sem):
    meet()

    def gather(n, _):
        for g in range(G8):
            t = send_list[n * G8 + g]
            for c in range(5):
                buf[n, c, g:g + 1, :] = rec[c, pl.ds(t, 1), :]
        return 0

    lax.fori_loop(0, NEIGH, gather, 0)
    for copy in start_all(buf, out, send_sem, recv_sem, 1):
        copy.wait()


def density_kernel(send_list, which, part, gpart, energy, dens_o, press_o, gpress_o, ret, buf, s1, r1, s2, r2):
    meet()
    for copy in start_all(gpart, ret, s1, r1, -1):
        copy.wait()
    hot = one_hot(which)
    dens = part[...] + split_dot(hot, ret[...].reshape(NEIGH * G8, 128))
    dens_o[...] = dens
    press_o[...] = (2.0 / 3.0) * energy[...] / dens

    def gather(n, _):
        for g in range(G8):
            t = send_list[n * G8 + g]
            buf[n, g:g + 1, :] = press_o[pl.ds(t, 1), :]
        return 0

    lax.fori_loop(0, NEIGH, gather, 0)
    for copy in start_all(buf, gpress_o, s2, r2, 1):
        copy.wait()


def force_kernel(which, part, gpart, acc_o, ret, s1, r1):
    meet()
    for copy in start_all(gpart, ret, s1, r1, -1):
        copy.wait()
    hot = one_hot(which)
    for c in range(3):
        acc_o[c] = part[c] + split_dot(hot, ret[:, c].reshape(NEIGH * G8, 128))


def per_device(positions, masses, smoothing, energy, level_ids, send_list, pair_list, pair_count):
    V = pl.BlockSpec(memory_space=pltpu.VMEM)
    S = pl.BlockSpec(memory_space=pltpu.SMEM)
    D = pltpu.SemaphoreType.DMA((NEIGH,))
    sds = jax.ShapeDtypeStruct
    pos = positions.reshape(3, NB, 128)
    mass = masses.reshape(NB, 128)
    en = energy.reshape(NB, 128)
    level = level_ids[:, None]
    scale = jnp.where(level == 0, 1.0, jnp.where(level == 1, SHRINK, SHRINK * SHRINK))
    h = smoothing.reshape(NB, 128) * scale.astype(f32)
    rec = jnp.concatenate([pos, mass[None], h[None]], 0)
    flat = send_list.reshape(NEIGH * G8)
    which = send_list.reshape(1, NEIGH * G8)
    pairs = pair_list[0]
    gh = pl.pallas_call(
        forward_kernel, out_shape=sds((NEIGH, 5, G8, 128), f32), in_specs=[S, V], out_specs=V,
        scratch_shapes=[pltpu.VMEM((NEIGH, 5, G8, 128), f32), D, D],
        compiler_params=pltpu.CompilerParams(collective_id=0, has_side_effects=True), name="forward")(flat, rec)
    dens, tiles = run_k2(pairs, pair_count, rec, gh, {}, G=32, U=8)
    density, press, gpress = pl.pallas_call(
        density_kernel,
        out_shape=[sds((NB, 128), f32), sds((NB, 128), f32), sds((NEIGH, G8, 128), f32)],
        in_specs=[S, V, V, V, V], out_specs=[V, V, V],
        scratch_shapes=[pltpu.VMEM((NEIGH, G8, 128), f32), pltpu.VMEM((NEIGH, G8, 128), f32), D, D, D, D],
        compiler_params=pltpu.CompilerParams(collective_id=1, has_side_effects=True), name="density")(
            flat, which, dens[:NB], dens[NB:].reshape(NEIGH, G8, 128), en)
    acc, gacc = run_k4(pairs, pair_count, rec, gh, press, gpress.reshape(NEIGH * G8, 128), tiles, {}, G=16, U=16)
    accel = pl.pallas_call(
        force_kernel, out_shape=sds((3, NB, 128), f32), in_specs=[V, V, V], out_specs=V,
        scratch_shapes=[pltpu.VMEM((NEIGH, 3, G8, 128), f32), D, D],
        compiler_params=pltpu.CompilerParams(collective_id=2, has_side_effects=True), name="force")(which, acc, gacc)
    return density.reshape(NB * 128), accel.reshape(3, NB * 128)


def solution(mesh):
    both = ("patch", "bulk")
    placed = (P(None, both), P(both), P(both), P(both), P(both), P(both, None, None), P(both, None, None), P(both))
    return jax.shard_map(per_device, mesh=mesh, in_specs=placed, out_specs=(P(both), P(None, both)), check_vma=False)
```

```python
import functools
import math

import jax
import jax.numpy as jnp
from jax import lax
from jax.experimental import pallas as pl
from jax.experimental.pallas import tpu as pltpu
from jax.sharding import PartitionSpec as P

MESH = pl.DeviceIdType.MESH
f32 = jnp.float32
bf16 = jnp.bfloat16
NORM = 21.0 / (2.0 * math.pi)
GAMMA_LESS = 2.0 / 3.0
SHRINK = 0.8
NB = 128
W128 = 128
NEIGH = 20
SLOTS = 8
GHOSTS = NEIGH * SLOTS
EXT = NB + GHOSTS
CHUNKS = [(0, 0), (0, 1), (1, 0), (1, 1), (0, 2), (2, 0), (1, 2), (2, 1)]
UNITS_STEP = 32
UNROLL = 16
FORCE_STEP = 80
FORCE_UNROLL = 16


def neighbour_steps():
    return [
        (step_patch, step_bulk)
        for step_patch in (-1, 0, 1)
        for step_bulk in range(-3, 4)
        if (step_patch, step_bulk) != (0, 0)
    ]


def place(offset):
    rows, columns = lax.axis_size("patch"), lax.axis_size("bulk")
    count = rows * columns
    me = lax.axis_index("patch") * columns + lax.axis_index("bulk")
    other = lax.rem(me + (offset + count), count)
    return (lax.div(other, columns), lax.rem(other, columns))


def offsets():
    columns = lax.axis_size("bulk")
    return [u * columns + v for u, v in neighbour_steps()]


def meet():
    barrier = pltpu.get_barrier_semaphore()
    for o in offsets():
        pl.semaphore_signal(barrier, inc=1, device_id=place(o), device_id_type=MESH)
    pl.semaphore_wait(barrier, NEIGH)


def start_all(src, dst, send_sem, recv_sem, sign):
    copies = []
    for n, o in enumerate(offsets()):
        copy = pltpu.make_async_remote_copy(
            src_ref=src.at[n], dst_ref=dst.at[n], send_sem=send_sem.at[n], recv_sem=recv_sem.at[n],
            device_id=place(sign * o), device_id_type=MESH)
        copy.start()
        copies.append(copy)
    return copies


def split3(v):
    a = v.astype(bf16).astype(f32)
    r = v - a
    b = r.astype(bf16).astype(f32)
    return a, b, r - b


def hilo(v):
    hi = v.astype(bf16)
    return hi, (v - hi.astype(f32)).astype(bf16)


def split_dot(hot, v):
    a, b, c = [p.astype(bf16) for p in split3(v)]
    dot = functools.partial(jnp.dot, preferred_element_type=f32)
    return dot(hot, a) + (dot(hot, b) + dot(hot, c))


def one_hot(which_ref):
    rows = lax.broadcasted_iota(jnp.int32, (NB, GHOSTS), 0)
    return (rows == which_ref[...]).astype(f32).astype(bf16)


def inverse_cube_root(m):
    k = jnp.exp(jnp.log(m) * (-1.0 / 3.0))
    return k * (4.0 - m * (k * k * k)) * (1.0 / 3.0)


def forward_kernel(send_list, pairs, count, pos, mass, smooth, out, idx, buf, send_sem, recv_sem):
    def gather(n, _):
        for g in range(SLOTS):
            t = send_list[0, n, g]
            for c in range(3):
                buf[n, c, g:g + 1, :] = pos[c, pl.ds(t, 1), :]
            buf[n, 3, g:g + 1, :] = mass[pl.ds(t, 1), :]
            buf[n, 4, g:g + 1, :] = smooth[pl.ds(t, 1), :]
        return 0

    meet()
    lax.fori_loop(0, NEIGH, gather, 0)
    copies = start_all(buf, out, send_sem, recv_sem, 1)
    total = NB + pairs.shape[2]
    lane = lax.broadcasted_iota(jnp.int32, (1, total - NB), 1)
    live = lane < count[0]
    own = lax.broadcasted_iota(jnp.int32, (1, NB), 1)
    idx[...] = jnp.zeros_like(idx)
    for r in range(4):
        idx[r:r + 1, :NB] = own if r < 3 else jnp.full((1, NB), EXT, jnp.int32)
    first = pairs[0, 0:1, :]
    second = pairs[0, 1:2, :]
    idx[0:1, NB:total] = first
    idx[1:2, NB:total] = second
    idx[2:3, NB:total] = jnp.where(live, first, NB)
    idx[3:4, NB:total] = jnp.where(live, second, EXT)
    for copy in copies:
        copy.wait()


def tile_math(r2, hs):
    r2 = jnp.maximum(r2, 1e-30)
    s = pl.reciprocal(hs, approx=True)
    q = r2 * lax.rsqrt(r2) * s
    t = jnp.maximum(1.0 - q, 0.0)
    st = s * t
    c = st * st * st
    return c * (t * (q + 0.25)), c * (s * s)


def density_pairs(idx, pos, mass, smooth, ghost, dens_o, dens_g, tiles, C, CA, AF, BF, GB, acc_a, acc_b):
    step = pl.program_id(0)

    def first_stage(k, j):
        GB[j] = jnp.dot(AF[idx[0, k]], BF[idx[1, k]], preferred_element_type=f32)

    @pl.when(step == 0)
    def _():
        zero = jnp.zeros((EXT, W128), f32)
        for i in (5, 6, 7, 8, 9, 12):
            C[i * EXT:(i + 1) * EXT] = zero
        CA[7 * NB:8 * NB] = zero[:NB]

        def columns(x, y, z, m, h):
            k = inverse_cube_root(m)
            k2 = k * k
            return x * k2, y * k2, z * k2, k2, (x * x + y * y + z * z) * k2, (0.5 * h) * k, k

        def fill(at, rows, v):
            for i, c in ((0, 0), (1, 1), (2, 2), (3, 3), (4, 4), (10, 5), (11, 6)):
                C[i * EXT + at:i * EXT + at + rows] = v[c]

        v = columns(pos[0], pos[1], pos[2], mass[...], smooth[...])
        fill(0, NB, v)
        for i, w in enumerate((-2.0 * v[0], -2.0 * v[1], -2.0 * v[2], v[4], v[3])):
            CA[i * NB:(i + 1) * NB] = w
        CA[5 * NB:6 * NB] = v[6]
        CA[6 * NB:7 * NB] = v[5]
        for n in range(NEIGH):
            fill(NB + n * SLOTS, SLOTS, columns(*[ghost[n, c] for c in range(5)]))
        acc_b[...] = jnp.zeros_like(acc_b)

        def right_side(i, _):
            for j in range(4):
                b = i * 4 + j
                for w, c in ((0, 0), (5, W128)):
                    p = split3(C[pl.ds(w * EXT + b, 8, stride=EXT), :])
                    BF[b, :, c:c + W128] = jnp.concatenate([p[q] for _, q in CHUNKS], 0).astype(bf16)
            return 0

        lax.fori_loop(0, EXT // 4, right_side, 0)

        def left_side(i, _):
            for j in range(8):
                b = i * 8 + j
                p = split3(CA[pl.ds(b, 8, stride=NB), :])
                AF[b] = jnp.concatenate([p[q] for q, _ in CHUNKS], 0).T.astype(bf16)
                acc_a[b] = jnp.zeros((W128, W128), f32)
            return 0

        lax.fori_loop(0, NB // 8, left_side, 0)
        for j in range(UNROLL):
            first_stage(j, j)

    def body(u, _):
        k0 = step * UNITS_STEP + u * UNROLL
        sums = []
        for j in range(UNROLL):
            ta = idx[2, k0 + j]
            part = jnp.zeros((8, W128), f32)
            for r in range(0, W128, 8):
                W, S = tile_math(GB[j, r:r + 8, :W128], GB[j, r:r + 8, W128:])
                tiles[u * UNROLL + j, r:r + 8] = S
                part = part + W
                acc_a[ta, r:r + 8] += W
            first_stage(k0 + UNROLL + j, j)
            sums.append((idx[3, k0 + j], part))
        for tb, part in sums:
            acc_b[pl.ds(pl.multiple_of(tb * 8, 8), 8), :] += part
        return 0

    lax.fori_loop(0, UNITS_STEP // UNROLL, body, 0)

    @pl.when(step == pl.num_programs(0) - 1)
    def _():
        ones = jnp.ones((16, 2 * W128), bf16)

        def fold(i, _):
            rows = []
            for j in range(4):
                hi, lo = hilo(acc_a[i * 4 + j])
                rows.append(lax.dot_general(ones, jnp.concatenate([hi, lo], 1), (((1,), (1,)), ((), ())),
                                            preferred_element_type=f32))
            for j in range(4):
                dens_o[pl.ds(i * 4 + j, 1), :] = rows[j][:1]
            return 0

        lax.fori_loop(0, NB // 4, fold, 0)
        for i in range(EXT // 8):
            v = acc_b[pl.ds(i * 64, 8, stride=8), :]
            for s in range(1, 8):
                v = v + acc_b[pl.ds(i * 64 + s, 8, stride=8), :]
            if i < NB // 8:
                r = slice(i * 8, i * 8 + 8)
                dens_o[r] = (dens_o[r] + v) * (4.0 * NORM) / mass[r]
            else:
                n = i - NB // 8
                dens_g[n] = v * (4.0 * NORM) / ghost[n, 3]


def density_kernel(send_list, which, part, gpart, energy, dens_o, press_o, gpress_o, ret, buf, s1, r1, s2, r2):
    meet()
    copies = start_all(gpart, ret, s1, r1, -1)
    hot = one_hot(which)
    for copy in copies:
        copy.wait()
    dens = part[...] + split_dot(hot, ret[...].reshape(GHOSTS, W128))
    dens_o[...] = dens
    press_o[...] = GAMMA_LESS * energy[...] / dens

    def gather(n, _):
        for g in range(SLOTS):
            buf[n, g:g + 1, :] = press_o[pl.ds(send_list[0, n, g], 1), :]
        return 0

    lax.fori_loop(0, NEIGH, gather, 0)
    for copy in start_all(buf, gpress_o, s2, r2, 1):
        copy.wait()


def force_pairs(idx, pos, mass, ghost, press, gpress, tiles, acc_o, acc_g, C, MM, acc):
    step = pl.program_id(0)

    @pl.when(step == 0)
    def _():
        def fill(at, rows, x, y, z, m, p):
            k = inverse_cube_root(m)
            w = k * k
            pw = p * w
            for i, v in enumerate((w, w * x, w * y, w * z, pw, pw * x, pw * y, pw * z)):
                C[i * EXT + at:i * EXT + at + rows] = v

        fill(0, NB, pos[0], pos[1], pos[2], mass[...], press[...])
        for n in range(NEIGH):
            fill(NB + n * SLOTS, SLOTS, *[ghost[n, c] for c in range(4)], gpress[n])
        acc[...] = jnp.zeros_like(acc)

        def columns(i, _):
            for j in range(4):
                b = i * 4 + j
                v = C[pl.ds(b, 8, stride=EXT), :]
                hi = v.astype(bf16).astype(f32)
                mm = jnp.concatenate([hi, v - hi], 0).astype(bf16)
                MM[b, :, :W128] = mm
                MM[b, :, W128:] = mm
            return 0

        lax.fori_loop(0, EXT // 4, columns, 0)

    def body(u, _):
        sums = []
        for j in range(FORCE_UNROLL):
            k = step * FORCE_STEP + u * FORCE_UNROLL + j
            hi, lo = hilo(tiles[u * FORCE_UNROLL + j])
            to_b = jnp.dot(MM[idx[0, k]], jnp.concatenate([hi, lo], 0), preferred_element_type=f32)
            to_a = lax.dot_general(MM[idx[1, k]], jnp.concatenate([hi, lo], 1), (((1,), (1,)), ((), ())),
                                   preferred_element_type=f32)
            sums.append((idx[2, k], to_a))
            sums.append((idx[3, k], to_b))
        for n, (i, v) in enumerate(sums):
            if n % 2 == 0:
                i = jnp.where(i == NB, EXT, i)
            acc[i] += v[:8] + v[8:]
        return 0

    lax.fori_loop(0, FORCE_STEP // FORCE_UNROLL, body, 0)

    @pl.when(step == pl.num_programs(0) - 1)
    def _():
        def final(p, m, spot, A):
            k = inverse_cube_root(m)
            k2 = k * k
            scale = (-20.0 * NORM) * (k2 * k2 * k)
            own = p * A[0] + A[4]
            return [(p * A[c + 1] + A[c + 5] - v * own) * scale for c, v in enumerate(spot)]

        for i in range(EXT // 8):
            r = slice(i * 8, i * 8 + 8)
            A = [acc[r, c, :] for c in range(8)]
            if i < NB // 8:
                for c, v in enumerate(final(press[r], mass[r], [pos[c, r] for c in range(3)], A)):
                    acc_o[c, r] = v
            else:
                n = i - NB // 8
                for c, v in enumerate(final(gpress[n], ghost[n, 3], [ghost[n, c] for c in range(3)], A)):
                    acc_g[n, c] = v


def force_kernel(which, part, gpart, acc_o, ret, s1, r1):
    meet()
    copies = start_all(gpart, ret, s1, r1, -1)
    hot = one_hot(which)
    for copy in copies:
        copy.wait()
    for c in range(3):
        acc_o[c] = part[c] + split_dot(hot, ret[:, c].reshape(GHOSTS, W128))


V = pl.BlockSpec(memory_space=pltpu.VMEM)
SM = pl.BlockSpec(memory_space=pltpu.SMEM)
sds = jax.ShapeDtypeStruct


def exchange_params(number):
    return pltpu.CompilerParams(collective_id=number, has_side_effects=True)


def run_density(idx, pos, mass, smooth, ghost, units):
    return pl.pallas_call(
        density_pairs,
        grid_spec=pltpu.PrefetchScalarGridSpec(
            num_scalar_prefetch=1, grid=(units // UNITS_STEP,), in_specs=[V] * 4,
            out_specs=[V, V, pl.BlockSpec((UNITS_STEP, W128, W128), lambda i, *_: (i, 0, 0))],
            scratch_shapes=[
                pltpu.VMEM((13 * EXT, W128), f32), pltpu.VMEM((8 * NB, W128), f32),
                pltpu.VMEM((NB, W128, 64), bf16), pltpu.VMEM((EXT, 64, 2 * W128), bf16),
                pltpu.VMEM((UNROLL, W128, 2 * W128), f32), pltpu.VMEM((NB + 1, W128, W128), f32),
                pltpu.VMEM(((EXT + 1) * 8, W128), f32)]),
        out_shape=[sds((NB, W128), f32), sds((NEIGH, SLOTS, W128), f32), sds((units, W128, W128), f32)],
        compiler_params=pltpu.CompilerParams(vmem_limit_bytes=60 * 2**20),
        name="density_pairs")(idx, pos, mass, smooth, ghost)


def run_force(idx, pos, mass, ghost, press, gpress, tiles):
    return pl.pallas_call(
        force_pairs,
        grid_spec=pltpu.PrefetchScalarGridSpec(
            num_scalar_prefetch=1, grid=(tiles.shape[0] // FORCE_STEP,),
            in_specs=[V] * 5 + [pl.BlockSpec((FORCE_STEP, W128, W128), lambda i, *_: (i, 0, 0))],
            out_specs=[V, V],
            scratch_shapes=[
                pltpu.VMEM((8 * EXT, W128), f32), pltpu.VMEM((EXT, 16, 2 * W128), bf16),
                pltpu.VMEM((EXT + 1, 8, W128), f32)]),
        out_shape=[sds((3, NB, W128), f32), sds((NEIGH, 3, SLOTS, W128), f32)],
        compiler_params=pltpu.CompilerParams(vmem_limit_bytes=60 * 2**20),
        name="force_pairs")(idx, pos, mass, ghost, press, gpress, tiles)


def per_device(positions, masses, smoothing, energy, level_ids, send_list, pair_list, pair_count):
    D = pltpu.SemaphoreType.DMA((NEIGH,))
    units = NB + pair_list.shape[2]
    pos = positions.reshape(3, NB, W128)
    mass = masses.reshape(NB, W128)
    level = level_ids[:, None]
    scale = jnp.where(level == 0, 1.0, jnp.where(level == 1, SHRINK, SHRINK * SHRINK)).astype(f32)
    smooth = smoothing.reshape(NB, W128) * scale
    which = send_list.reshape(1, GHOSTS)
    ghost, idx = pl.pallas_call(
        forward_kernel,
        out_shape=[sds((NEIGH, 5, SLOTS, W128), f32), sds((4, units + 2 * W128 - units % W128), jnp.int32)],
        in_specs=[SM, V, SM, V, V, V], out_specs=[V, V],
        scratch_shapes=[pltpu.VMEM((NEIGH, 5, SLOTS, W128), f32), D, D],
        compiler_params=exchange_params(0), name="forward")(send_list, pair_list, pair_count, pos, mass, smooth)
    dens, gdens, tiles = run_density(idx, pos, mass, smooth, ghost, units)
    density, press, gpress = pl.pallas_call(
        density_kernel,
        out_shape=[sds((NB, W128), f32), sds((NB, W128), f32), sds((NEIGH, SLOTS, W128), f32)],
        in_specs=[SM, V, V, V, V], out_specs=[V, V, V],
        scratch_shapes=[pltpu.VMEM((NEIGH, SLOTS, W128), f32), pltpu.VMEM((NEIGH, SLOTS, W128), f32), D, D, D, D],
        compiler_params=exchange_params(1), name="density")(
            send_list, which, dens, gdens, energy.reshape(NB, W128))
    acc, gacc = run_force(idx, pos, mass, ghost, press, gpress, tiles)
    accel = pl.pallas_call(
        force_kernel, out_shape=sds((3, NB, W128), f32), in_specs=[V, V, V], out_specs=V,
        scratch_shapes=[pltpu.VMEM((NEIGH, 3, SLOTS, W128), f32), D, D],
        compiler_params=exchange_params(2), name="force")(which, acc, gacc)
    return density.reshape(NB * W128), accel.reshape(3, NB * W128)


def solution(mesh):
    both = ("patch", "bulk")
    placed = (P(None, both), P(both), P(both), P(both), P(both), P(both, None, None), P(both, None, None), P(both))
    return jax.shard_map(per_device, mesh=mesh, in_specs=placed, out_specs=(P(both), P(None, both)), check_vma=False)
```

```python
import functools
import math

import jax
import jax.numpy as jnp
from jax import lax
from jax.experimental import pallas as pl
from jax.experimental.pallas import tpu as pltpu
from jax.sharding import PartitionSpec as P

MESH = pl.DeviceIdType.MESH
f32 = jnp.float32
bf16 = jnp.bfloat16
NORM = 21.0 / (2.0 * math.pi)
GAMMA_LESS = 2.0 / 3.0
SHRINK = 0.8
NB = 128
W128 = 128
NEIGH = 20
SLOTS = 8
GHOSTS = NEIGH * SLOTS
EXT = NB + GHOSTS
CHUNKS = [(0, 0), (0, 1), (1, 0), (1, 1), (0, 2), (2, 0), (1, 2), (2, 1)]
UNITS_STEP = 32
UNROLL = 16
FORCE_STEP = 84
FORCE_UNROLL = 14
SELF = 8
VMEM = 63 * 2**20


def neighbour_steps():
    return [
        (step_patch, step_bulk)
        for step_patch in (-1, 0, 1)
        for step_bulk in range(-3, 4)
        if (step_patch, step_bulk) != (0, 0)
    ]


def place(offset):
    rows, columns = lax.axis_size("patch"), lax.axis_size("bulk")
    count = rows * columns
    me = lax.axis_index("patch") * columns + lax.axis_index("bulk")
    other = lax.rem(me + (offset + count), count)
    return (lax.div(other, columns), lax.rem(other, columns))


def offsets():
    columns = lax.axis_size("bulk")
    return [u * columns + v for u, v in neighbour_steps()]


def meet():
    barrier = pltpu.get_barrier_semaphore()
    for o in offsets():
        pl.semaphore_signal(barrier, inc=1, device_id=place(o), device_id_type=MESH)
    pl.semaphore_wait(barrier, NEIGH)


def start_all(src, dst, send_sem, recv_sem, sign):
    copies = []
    for n, o in enumerate(offsets()):
        copy = pltpu.make_async_remote_copy(
            src_ref=src.at[n], dst_ref=dst.at[n], send_sem=send_sem.at[n], recv_sem=recv_sem.at[n],
            device_id=place(sign * o), device_id_type=MESH)
        copy.start()
        copies.append(copy)
    return copies


def split3(v):
    a = v.astype(bf16).astype(f32)
    r = v - a
    b = r.astype(bf16).astype(f32)
    return a, b, r - b


def hilo(v):
    hi = v.astype(bf16)
    return hi, (v - hi.astype(f32)).astype(bf16)


def split_dot(hot, v):
    a, b, c = [p.astype(bf16) for p in split3(v)]
    dot = functools.partial(jnp.dot, preferred_element_type=f32)
    return dot(hot, a) + (dot(hot, b) + dot(hot, c))


def inverse_cube_root(m):
    k = jnp.exp(jnp.log(m) * (-1.0 / 3.0))
    return k * (4.0 - m * (k * k * k)) * (1.0 / 3.0)


def tile_math(r2, hs):
    r2 = jnp.maximum(r2, 1e-30)
    s = pl.reciprocal(hs, approx=True)
    q = r2 * lax.rsqrt(r2) * s
    t = jnp.maximum(1.0 - q, 0.0)
    st = s * t
    c = st * st * st
    return c * (t * (q + 0.25)), c * (s * s)


def scaled_columns(x, y, z, m, h):
    k = inverse_cube_root(m)
    k2 = k * k
    return x * k2, y * k2, z * k2, k2, (x * x + y * y + z * z) * k2, (0.5 * h) * k, k


def fill_right(C, total, at, rows, v):
    for i, c in ((0, 0), (1, 1), (2, 2), (3, 3), (4, 4), (10, 5), (11, 6)):
        C[i * total + at:i * total + at + rows] = v[c]


def clear_right(C, total):
    zero = jnp.zeros((total, W128), f32)
    for i in (5, 6, 7, 8, 9, 12):
        C[i * total:(i + 1) * total] = zero


def fill_left(CA, v):
    for i, w in enumerate((-2.0 * v[0], -2.0 * v[1], -2.0 * v[2], v[4], v[3], v[6], v[5], jnp.zeros_like(v[0]))):
        CA[i * NB:(i + 1) * NB] = w


def right_features(C, total, b, BF, at):
    for w, c in ((0, 0), (5, W128)):
        p = split3(C[pl.ds(w * total + b, 8, stride=total), :])
        BF[at, :, c:c + W128] = jnp.concatenate([p[q] for _, q in CHUNKS], 0).astype(bf16)


def left_features(CA, b, AF, at):
    p = split3(CA[pl.ds(b, 8, stride=NB), :])
    AF[at] = jnp.concatenate([p[q] for q, _ in CHUNKS], 0).T.astype(bf16)


def forward_kernel(send_list, count, pairs, pos, mass, smoothing, level, ghost_o, idx, hot_o, pos_o, smooth_o, self_o, tiles_o,
                   buf, hot, C, CA, AF, BF, GB, tiles, send_sem, recv_sem, tile_sem):
    lev = level[...]
    scale = jnp.where(lev == 0, 1.0, jnp.where(lev == 1, SHRINK, SHRINK * SHRINK)).astype(f32)
    smooth_o[...] = smoothing[...] * jnp.broadcast_to(scale, (NB, W128)).T
    for c in range(3):
        pos_o[c] = pos[:, c, :]
    lane = lax.broadcasted_iota(jnp.int32, (1, NB), 1)

    def gather(n, _):
        for g in range(SLOTS):
            t = send_list[0, n, g]
            for c in range(3):
                buf[n, c, g:g + 1, :] = pos_o[c, pl.ds(t, 1), :]
            buf[n, 3, g:g + 1, :] = mass[pl.ds(t, 1), :]
            buf[n, 4, g:g + 1, :] = smooth_o[pl.ds(t, 1), :]
            hot[pl.ds(n * SLOTS + g, 1), :] = jnp.where(lane == t, 1.0, 0.0)
        return 0

    hot[GHOSTS:] = jnp.zeros((2 * W128 - GHOSTS, W128), f32)
    lax.fori_loop(0, NEIGH, gather, 0)
    meet()
    copies = start_all(buf, ghost_o, send_sem, recv_sem, 1)
    count_pairs = pairs.shape[2]
    live = lax.broadcasted_iota(jnp.int32, (1, count_pairs), 1) < count[0]
    idx[...] = jnp.zeros_like(idx)
    first = pairs[0, 0:1, :]
    second = pairs[0, 1:2, :]
    idx[0:1, :count_pairs] = first
    idx[1:2, :count_pairs] = second
    idx[2:3, :count_pairs] = jnp.where(live, first, NB)
    idx[3:4, :count_pairs] = jnp.where(live, second, EXT)
    for i in range(2):
        hot_o[:, i * W128:(i + 1) * W128] = hot[i * W128:(i + 1) * W128].T.astype(bf16)
    v = scaled_columns(pos_o[0], pos_o[1], pos_o[2], mass[...], smooth_o[...])
    clear_right(C, NB)
    fill_right(C, NB, 0, NB, v)
    fill_left(CA, v)

    def features(g):
        for j in range(SELF):
            right_features(C, NB, g * SELF + j, BF, j)
            left_features(CA, g * SELF + j, AF, j)

    def products():
        for j in range(SELF):
            GB[j] = jnp.dot(AF[j], BF[j], preferred_element_type=f32)

    features(0)
    products()
    features(1)

    def body(g, _):
        for j in range(SELF):
            part = jnp.zeros((8, W128), f32)
            for r in range(0, W128, 8):
                W, S = tile_math(GB[j, r:r + 8, :W128], GB[j, r:r + 8, W128:])
                tiles[g * SELF + j, r:r + 8] = S
                part = part + W
            self_o[pl.ds(g * SELF + j, 1), :] = jnp.sum(part, axis=0, keepdims=True)
        pltpu.make_async_copy(tiles.at[pl.ds(g * SELF, SELF)], tiles_o.at[pl.ds(g * SELF, SELF)], tile_sem.at[g]).start()
        products()
        features(jnp.minimum(g + 2, NB // SELF - 1))
        return 0

    lax.fori_loop(0, NB // SELF, body, 0)

    def landed(g, _):
        pltpu.make_async_copy(tiles.at[pl.ds(g * SELF, SELF)], tiles_o.at[pl.ds(g * SELF, SELF)], tile_sem.at[g]).wait()
        return 0

    lax.fori_loop(0, NB // SELF, landed, 0)
    for copy in copies:
        copy.wait()


def density_pairs(idx, pos, mass, smooth, ghost, self_sum, dens_o, dens_g, tiles, C, CA, AF, BF, GB, acc_a, acc_b):
    step = pl.program_id(0)

    def first_stage(k, j):
        GB[j] = jnp.dot(AF[idx[0, k]], BF[idx[1, k]], preferred_element_type=f32)

    @pl.when(step == 0)
    def _():
        v = scaled_columns(pos[0], pos[1], pos[2], mass[...], smooth[...])
        clear_right(C, EXT)
        fill_right(C, EXT, 0, NB, v)
        fill_left(CA, v)
        for n in range(NEIGH):
            fill_right(C, EXT, NB + n * SLOTS, SLOTS, scaled_columns(*[ghost[n, c] for c in range(5)]))
        acc_b[...] = jnp.zeros_like(acc_b)

        def right_side(i, _):
            for j in range(4):
                right_features(C, EXT, i * 4 + j, BF, i * 4 + j)
            return 0

        lax.fori_loop(0, EXT // 4, right_side, 0)

        def left_side(i, _):
            for j in range(8):
                b = i * 8 + j
                left_features(CA, b, AF, b)
                acc_a[b] = jnp.zeros((W128, W128), f32)
            return 0

        lax.fori_loop(0, NB // 8, left_side, 0)
        for j in range(UNROLL):
            first_stage(j, j)

    def body(u, _):
        k0 = step * UNITS_STEP + u * UNROLL
        sums = []
        for j in range(UNROLL):
            ta = idx[2, k0 + j]
            part = jnp.zeros((8, W128), f32)
            for r in range(0, W128, 8):
                W, S = tile_math(GB[j, r:r + 8, :W128], GB[j, r:r + 8, W128:])
                tiles[u * UNROLL + j, r:r + 8] = S
                part = part + W
                acc_a[ta, r:r + 8] += W
            first_stage(k0 + UNROLL + j, j)
            sums.append((idx[3, k0 + j], part))
        for tb, part in sums:
            acc_b[pl.ds(pl.multiple_of(tb * 8, 8), 8), :] += part
        return 0

    lax.fori_loop(0, UNITS_STEP // UNROLL, body, 0)

    @pl.when(step == pl.num_programs(0) - 1)
    def _():
        ones = jnp.ones((16, 2 * W128), bf16)

        def fold(i, _):
            rows = []
            for j in range(4):
                hi, lo = hilo(acc_a[i * 4 + j])
                rows.append(lax.dot_general(ones, jnp.concatenate([hi, lo], 1), (((1,), (1,)), ((), ())),
                                            preferred_element_type=f32))
            for j in range(4):
                dens_o[pl.ds(i * 4 + j, 1), :] = rows[j][:1]
            return 0

        lax.fori_loop(0, NB // 4, fold, 0)
        for i in range(EXT // 8):
            v = acc_b[pl.ds(i * 64, 8, stride=8), :]
            for s in range(1, 8):
                v = v + acc_b[pl.ds(i * 64 + s, 8, stride=8), :]
            if i < NB // 8:
                r = slice(i * 8, i * 8 + 8)
                dens_o[r] = (dens_o[r] + (v + self_sum[r])) * (4.0 * NORM) / mass[r]
            else:
                n = i - NB // 8
                dens_g[n] = v * (4.0 * NORM) / ghost[n, 3]


def density_kernel(send_list, hot, part, gpart, energy, dens_o, press_o, gpress_o, ret, buf, s1, r1, s2, r2):
    meet()
    copies = start_all(gpart, ret, s1, r1, -1)
    for copy in copies:
        copy.wait()
    dens = part[...] + split_dot(hot[:, :GHOSTS], ret[...].reshape(GHOSTS, W128))
    dens_o[...] = dens
    press_o[...] = GAMMA_LESS * energy[...] / dens

    def gather(n, _):
        for g in range(SLOTS):
            buf[n, g:g + 1, :] = press_o[pl.ds(send_list[0, n, g], 1), :]
        return 0

    lax.fori_loop(0, NEIGH, gather, 0)
    for copy in start_all(buf, gpress_o, s2, r2, 1):
        copy.wait()


def force_pairs(idx, pos, mass, ghost, press, gpress, tiles, own_tiles, acc_o, acc_g, C, MM, acc):
    step = pl.program_id(0)

    @pl.when(step == 0)
    def _():
        def fill(at, rows, x, y, z, m, p):
            k = inverse_cube_root(m)
            w = k * k
            pw = p * w
            for i, v in enumerate((w, w * x, w * y, w * z, pw, pw * x, pw * y, pw * z)):
                C[i * EXT + at:i * EXT + at + rows] = v

        fill(0, NB, pos[0], pos[1], pos[2], mass[...], press[...])
        for n in range(NEIGH):
            fill(NB + n * SLOTS, SLOTS, *[ghost[n, c] for c in range(4)], gpress[n])
        acc[...] = jnp.zeros_like(acc)

        def columns(i, _):
            for j in range(4):
                b = i * 4 + j
                v = C[pl.ds(b, 8, stride=EXT), :]
                hi = v.astype(bf16).astype(f32)
                mm = jnp.concatenate([hi, v - hi], 0).astype(bf16)
                MM[b, :, :W128] = mm
                MM[b, :, W128:] = mm
            return 0

        lax.fori_loop(0, EXT // 4, columns, 0)

    def body(u, _):
        sums = []
        for j in range(FORCE_UNROLL):
            k = step * FORCE_STEP + u * FORCE_UNROLL + j
            hi, lo = hilo(tiles[u * FORCE_UNROLL + j])
            to_b = jnp.dot(MM[idx[0, k]], jnp.concatenate([hi, lo], 0), preferred_element_type=f32)
            to_a = lax.dot_general(MM[idx[1, k]], jnp.concatenate([hi, lo], 1), (((1,), (1,)), ((), ())),
                                   preferred_element_type=f32)
            sums.append((idx[2, k], to_a))
            sums.append((idx[3, k], to_b))
        for n, (i, v) in enumerate(sums):
            if n % 2 == 0:
                i = jnp.where(i == NB, EXT, i)
            acc[i] += v[:8] + v[8:]
        return 0

    def own_body(u, _):
        sums = []
        for j in range(SELF):
            a = step * own_tiles.shape[0] + u * SELF + j
            hi, lo = hilo(own_tiles[u * SELF + j])
            sums.append((a, jnp.dot(MM[a], jnp.concatenate([hi, lo], 0), preferred_element_type=f32)))
        for a, v in sums:
            acc[a] += v[:8] + v[8:]
        return 0

    lax.fori_loop(0, own_tiles.shape[0] // SELF, own_body, 0)
    lax.fori_loop(0, FORCE_STEP // FORCE_UNROLL, body, 0)

    @pl.when(step == pl.num_programs(0) - 1)
    def _():
        def final(p, m, spot, A):
            k = inverse_cube_root(m)
            k2 = k * k
            scale = (-20.0 * NORM) * (k2 * k2 * k)
            own = p * A[0] + A[4]
            return [(p * A[c + 1] + A[c + 5] - v * own) * scale for c, v in enumerate(spot)]

        for i in range(EXT // 8):
            r = slice(i * 8, i * 8 + 8)
            A = [acc[r, c, :] for c in range(8)]
            if i < NB // 8:
                for c, v in enumerate(final(press[r], mass[r], [pos[c, r] for c in range(3)], A)):
                    acc_o[c, r] = v
            else:
                n = i - NB // 8
                for c, v in enumerate(final(gpress[n], ghost[n, 3], [ghost[n, c] for c in range(3)], A)):
                    acc_g[n, c] = v


def force_kernel(hot, part, gpart, acc_o, ret, s1, r1):
    meet()
    copies = start_all(gpart, ret, s1, r1, -1)
    for copy in copies:
        copy.wait()
    for c in range(3):
        acc_o[:, c, :] = part[c] + split_dot(hot[:, :GHOSTS], ret[:, c].reshape(GHOSTS, W128))


V = pl.BlockSpec(memory_space=pltpu.VMEM)
SM = pl.BlockSpec(memory_space=pltpu.SMEM)
sds = jax.ShapeDtypeStruct


def exchange_params(number):
    return pltpu.CompilerParams(collective_id=number, has_side_effects=True, vmem_limit_bytes=VMEM)


def run_forward(send_list, pair_count, pair_list, pos, mass, smoothing, level):
    D = pltpu.SemaphoreType.DMA((NEIGH,))
    slots = pair_list.shape[2] + 2 * W128 - pair_list.shape[2] % W128
    vm = pltpu.VMEM
    return pl.pallas_call(
        forward_kernel,
        out_shape=[
            sds((NEIGH, 5, SLOTS, W128), f32), sds((4, slots), jnp.int32), sds((NB, 2 * W128), bf16),
            sds((3, NB, W128), f32), sds((NB, W128), f32), sds((NB, W128), f32), sds((NB, W128, W128), f32)],
        in_specs=[SM, SM, V, V, V, V, V], out_specs=[V] * 6 + [pl.BlockSpec(memory_space=pl.ANY)],
        scratch_shapes=[
            vm((NEIGH, 5, SLOTS, W128), f32), vm((2 * W128, W128), f32), vm((13 * NB, W128), f32), vm((8 * NB, W128), f32),
            vm((SELF, W128, 64), bf16), vm((SELF, 64, 2 * W128), bf16), vm((SELF, W128, 2 * W128), f32),
            vm((NB, W128, W128), f32), D, D, pltpu.SemaphoreType.DMA((NB // SELF,))],
        compiler_params=pltpu.CompilerParams(collective_id=0, has_side_effects=True, vmem_limit_bytes=VMEM),
        name="forward")(send_list, pair_count, pair_list, pos, mass, smoothing, level)


def run_density(idx, pos, mass, smooth, ghost, self_sum, pairs):
    vm = pltpu.VMEM
    return pl.pallas_call(
        density_pairs,
        grid_spec=pltpu.PrefetchScalarGridSpec(
            num_scalar_prefetch=1, grid=(pairs // UNITS_STEP,), in_specs=[V] * 5,
            out_specs=[V, V, pl.BlockSpec((UNITS_STEP, W128, W128), lambda i, *_: (i, 0, 0))],
            scratch_shapes=[
                vm((13 * EXT, W128), f32), vm((8 * NB, W128), f32), vm((NB, W128, 64), bf16), vm((EXT, 64, 2 * W128), bf16),
                vm((UNROLL, W128, 2 * W128), f32), vm((NB + 1, W128, W128), f32), vm(((EXT + 1) * 8, W128), f32)]),
        out_shape=[sds((NB, W128), f32), sds((NEIGH, SLOTS, W128), f32), sds((pairs, W128, W128), f32)],
        compiler_params=pltpu.CompilerParams(vmem_limit_bytes=VMEM),
        name="density_pairs")(idx, pos, mass, smooth, ghost, self_sum)


def run_force(idx, pos, mass, ghost, press, gpress, tiles, own_tiles):
    steps = tiles.shape[0] // FORCE_STEP
    vm = pltpu.VMEM
    return pl.pallas_call(
        force_pairs,
        grid_spec=pltpu.PrefetchScalarGridSpec(
            num_scalar_prefetch=1, grid=(steps,),
            in_specs=[V] * 5 + [pl.BlockSpec((FORCE_STEP, W128, W128), lambda i, *_: (i, 0, 0)),
                                pl.BlockSpec((NB // steps, W128, W128), lambda i, *_: (i, 0, 0))],
            out_specs=[V, V],
            scratch_shapes=[vm((8 * EXT, W128), f32), vm((EXT, 16, 2 * W128), bf16), vm((EXT + 1, 8, W128), f32)]),
        out_shape=[sds((3, NB, W128), f32), sds((NEIGH, 3, SLOTS, W128), f32)],
        compiler_params=pltpu.CompilerParams(vmem_limit_bytes=VMEM),
        name="force_pairs")(idx, pos, mass, ghost, press, gpress, tiles, own_tiles)


def per_device(positions, masses, smoothing, energy, level_ids, send_list, pair_list, pair_count):
    D = pltpu.SemaphoreType.DMA((NEIGH,))
    vm = pltpu.VMEM
    mass = masses.reshape(NB, W128)
    ghost, idx, hot, pos, smooth, self_sum, own_tiles = run_forward(
        send_list, pair_count, pair_list, positions.reshape(3, NB, W128).transpose(1, 0, 2), mass,
        smoothing.reshape(NB, W128), level_ids.reshape(1, NB))
    dens, gdens, tiles = run_density(idx, pos, mass, smooth, ghost, self_sum, pair_list.shape[2])
    density, press, gpress = pl.pallas_call(
        density_kernel,
        out_shape=[sds((NB, W128), f32), sds((NB, W128), f32), sds((NEIGH, SLOTS, W128), f32)],
        in_specs=[SM, V, V, V, V], out_specs=[V, V, V],
        scratch_shapes=[vm((NEIGH, SLOTS, W128), f32), vm((NEIGH, SLOTS, W128), f32), D, D, D, D],
        compiler_params=exchange_params(1), name="density")(
            send_list, hot, dens, gdens, energy.reshape(NB, W128))
    acc, gacc = run_force(idx, pos, mass, ghost, press, gpress, tiles, own_tiles)
    accel = pl.pallas_call(
        force_kernel, out_shape=sds((NB, 3, W128), f32), in_specs=[V, V, V], out_specs=V,
        scratch_shapes=[vm((NEIGH, 3, SLOTS, W128), f32), D, D],
        compiler_params=exchange_params(2), name="force")(hot, acc, gacc)
    return density.reshape(NB * W128), accel.transpose(1, 0, 2).reshape(3, NB * W128)


def solution(mesh):
    both = ("patch", "bulk")
    placed = (P(None, both), P(both), P(both), P(both), P(both), P(both, None, None), P(both, None, None), P(both))
    return jax.shard_map(per_device, mesh=mesh, in_specs=placed, out_specs=(P(both), P(None, both)), check_vma=False)
```

```python
import functools
import math

import jax
import jax.numpy as jnp
from jax import lax
from jax.experimental import pallas as pl
from jax.experimental.pallas import tpu as pltpu
from jax.sharding import PartitionSpec as P

MESH = pl.DeviceIdType.MESH
f32 = jnp.float32
bf16 = jnp.bfloat16
NORM = 21.0 / (2.0 * math.pi)
GAMMA_LESS = 2.0 / 3.0
SHRINK = 0.8
NB = 128
W128 = 128
NEIGH = 20
SLOTS = 8
GHOSTS = NEIGH * SLOTS
EXT = NB + GHOSTS
CHUNKS = [(0, 0), (0, 1), (1, 0), (1, 1), (0, 2), (2, 0), (1, 2), (2, 1)]
UNITS_STEP = 32
UNROLL = 16
CHUNK = 84
FORCE_UNROLL = 14
EARLY = 2
SELF = 8
VMEM = 63 * 2**20


def neighbour_steps():
    return [
        (step_patch, step_bulk)
        for step_patch in (-1, 0, 1)
        for step_bulk in range(-3, 4)
        if (step_patch, step_bulk) != (0, 0)
    ]


def place(offset):
    rows, columns = lax.axis_size("patch"), lax.axis_size("bulk")
    count = rows * columns
    me = lax.axis_index("patch") * columns + lax.axis_index("bulk")
    other = lax.rem(me + (offset + count), count)
    return (lax.div(other, columns), lax.rem(other, columns))


def offsets():
    columns = lax.axis_size("bulk")
    return [u * columns + v for u, v in neighbour_steps()]


def meet():
    barrier = pltpu.get_barrier_semaphore()
    for o in offsets():
        pl.semaphore_signal(barrier, inc=1, device_id=place(o), device_id_type=MESH)
    pl.semaphore_wait(barrier, NEIGH)


def start_all(src, dst, send_sem, recv_sem, sign):
    copies = []
    for n, o in enumerate(offsets()):
        copy = pltpu.make_async_remote_copy(
            src_ref=src.at[n], dst_ref=dst.at[n], send_sem=send_sem.at[n], recv_sem=recv_sem.at[n],
            device_id=place(sign * o), device_id_type=MESH)
        copy.start()
        copies.append(copy)
    return copies


def split3(v):
    a = v.astype(bf16).astype(f32)
    r = v - a
    b = r.astype(bf16).astype(f32)
    return a, b, r - b


def hilo(v):
    hi = v.astype(bf16)
    return hi, (v - hi.astype(f32)).astype(bf16)


def split_dot(hot, v):
    a, b, c = [p.astype(bf16) for p in split3(v)]
    dot = functools.partial(jnp.dot, preferred_element_type=f32)
    return dot(hot, a) + (dot(hot, b) + dot(hot, c))


def inverse_cube_root(m):
    k = jnp.exp(jnp.log(m) * (-1.0 / 3.0))
    return k * (4.0 - m * (k * k * k)) * (1.0 / 3.0)


def tile_math(r2, hs):
    r2 = jnp.maximum(r2, 1e-30)
    s = pl.reciprocal(hs, approx=True)
    q = r2 * lax.rsqrt(r2) * s
    t = jnp.maximum(1.0 - q, 0.0)
    st = s * t
    c = st * st * st
    return c * (t * (q + 0.25)), c * (s * s)


def scaled_columns(x, y, z, m, h):
    k = inverse_cube_root(m)
    k2 = k * k
    return x * k2, y * k2, z * k2, k2, (x * x + y * y + z * z) * k2, (0.5 * h) * k, k


def fill_right(C, total, at, rows, v):
    for i, c in ((0, 0), (1, 1), (2, 2), (3, 3), (4, 4), (10, 5), (11, 6)):
        C[i * total + at:i * total + at + rows] = v[c]


def clear_right(C, total):
    zero = jnp.zeros((total, W128), f32)
    for i in (5, 6, 7, 8, 9, 12):
        C[i * total:(i + 1) * total] = zero


def fill_left(CA, v):
    for i, w in enumerate((-2.0 * v[0], -2.0 * v[1], -2.0 * v[2], v[4], v[3], v[6], v[5], jnp.zeros_like(v[0]))):
        CA[i * NB:(i + 1) * NB] = w


def right_features(C, total, b, BF, at):
    for w, c in ((0, 0), (5, W128)):
        p = split3(C[pl.ds(w * total + b, 8, stride=total), :])
        BF[at, :, c:c + W128] = jnp.concatenate([p[q] for _, q in CHUNKS], 0).astype(bf16)


def left_features(CA, b, AF, at):
    p = split3(CA[pl.ds(b, 8, stride=NB), :])
    AF[at] = jnp.concatenate([p[q] for q, _ in CHUNKS], 0).T.astype(bf16)


def forward_kernel(send_list, count, pairs, pos, mass, smoothing, level, ghost_o, idx, hot_o, pos_o, smooth_o, self_o, tiles_o,
                   buf, hot, C, CA, AF, BF, GB, tiles, send_sem, recv_sem, tile_sem):
    lev = level[...]
    scale = jnp.where(lev == 0, 1.0, jnp.where(lev == 1, SHRINK, SHRINK * SHRINK)).astype(f32)
    smooth_o[...] = smoothing[...] * jnp.broadcast_to(scale, (NB, W128)).T
    for c in range(3):
        pos_o[c] = pos[:, c, :]
    lane = lax.broadcasted_iota(jnp.int32, (1, NB), 1)

    def gather(n, _):
        for g in range(SLOTS):
            t = send_list[0, n, g]
            for c in range(3):
                buf[n, c, g:g + 1, :] = pos_o[c, pl.ds(t, 1), :]
            buf[n, 3, g:g + 1, :] = mass[pl.ds(t, 1), :]
            buf[n, 4, g:g + 1, :] = smooth_o[pl.ds(t, 1), :]
            hot[pl.ds(n * SLOTS + g, 1), :] = jnp.where(lane == t, 1.0, 0.0)
        return 0

    hot[GHOSTS:] = jnp.zeros((2 * W128 - GHOSTS, W128), f32)
    lax.fori_loop(0, NEIGH, gather, 0)
    meet()
    copies = start_all(buf, ghost_o, send_sem, recv_sem, 1)
    count_pairs = pairs.shape[2]
    live = lax.broadcasted_iota(jnp.int32, (1, count_pairs), 1) < count[0]
    idx[...] = jnp.zeros_like(idx)
    idx[2:4, :] = jnp.full((2, idx.shape[1]), EXT, jnp.int32)
    first = pairs[0, 0:1, :]
    second = pairs[0, 1:2, :]
    idx[0:1, :count_pairs] = first
    idx[1:2, :count_pairs] = second
    idx[2:3, :count_pairs] = jnp.where(live, first, NB)
    idx[3:4, :count_pairs] = jnp.where(live, second, EXT)
    for i in range(2):
        hot_o[:, i * W128:(i + 1) * W128] = hot[i * W128:(i + 1) * W128].T.astype(bf16)
    v = scaled_columns(pos_o[0], pos_o[1], pos_o[2], mass[...], smooth_o[...])
    clear_right(C, NB)
    fill_right(C, NB, 0, NB, v)
    fill_left(CA, v)

    def features(g):
        for j in range(SELF):
            right_features(C, NB, g * SELF + j, BF, j)
            left_features(CA, g * SELF + j, AF, j)

    def products():
        for j in range(SELF):
            GB[j] = jnp.dot(AF[j], BF[j], preferred_element_type=f32)

    features(0)
    products()
    features(1)

    def body(g, _):
        for j in range(SELF):
            part = jnp.zeros((8, W128), f32)
            for r in range(0, W128, 8):
                W, S = tile_math(GB[j, r:r + 8, :W128], GB[j, r:r + 8, W128:])
                tiles[g * SELF + j, r:r + 8] = S
                part = part + W
            self_o[pl.ds(g * SELF + j, 1), :] = jnp.sum(part, axis=0, keepdims=True)
        pltpu.make_async_copy(tiles.at[pl.ds(g * SELF, SELF)], tiles_o.at[pl.ds(g * SELF, SELF)], tile_sem.at[g]).start()
        products()
        features(jnp.minimum(g + 2, NB // SELF - 1))
        return 0

    lax.fori_loop(0, NB // SELF, body, 0)

    def landed(g, _):
        pltpu.make_async_copy(tiles.at[pl.ds(g * SELF, SELF)], tiles_o.at[pl.ds(g * SELF, SELF)], tile_sem.at[g]).wait()
        return 0

    lax.fori_loop(0, NB // SELF, landed, 0)
    for copy in copies:
        copy.wait()


def density_pairs(idx, pos, mass, smooth, ghost, self_sum, dens_o, dens_g, tiles, C, CA, AF, BF, GB, acc_a, acc_b):
    step = pl.program_id(0)

    def first_stage(k, j):
        GB[j] = jnp.dot(AF[idx[0, k]], BF[idx[1, k]], preferred_element_type=f32)

    @pl.when(step == 0)
    def _():
        v = scaled_columns(pos[0], pos[1], pos[2], mass[...], smooth[...])
        clear_right(C, EXT)
        fill_right(C, EXT, 0, NB, v)
        fill_left(CA, v)
        for n in range(NEIGH):
            fill_right(C, EXT, NB + n * SLOTS, SLOTS, scaled_columns(*[ghost[n, c] for c in range(5)]))
        acc_b[...] = jnp.zeros_like(acc_b)

        def right_side(i, _):
            for j in range(4):
                right_features(C, EXT, i * 4 + j, BF, i * 4 + j)
            return 0

        lax.fori_loop(0, EXT // 4, right_side, 0)

        def left_side(i, _):
            for j in range(8):
                b = i * 8 + j
                left_features(CA, b, AF, b)
                acc_a[b] = jnp.zeros((W128, W128), f32)
            return 0

        lax.fori_loop(0, NB // 8, left_side, 0)
        for j in range(UNROLL):
            first_stage(j, j)

    def body(u, _):
        k0 = step * UNITS_STEP + u * UNROLL
        sums = []
        for j in range(UNROLL):
            ta = idx[2, k0 + j]
            part = jnp.zeros((8, W128), f32)
            for r in range(0, W128, 8):
                W, S = tile_math(GB[j, r:r + 8, :W128], GB[j, r:r + 8, W128:])
                tiles[u * UNROLL + j, r:r + 8] = S
                part = part + W
                acc_a[ta, r:r + 8] += W
            first_stage(k0 + UNROLL + j, j)
            sums.append((idx[3, k0 + j], part))
        for tb, part in sums:
            acc_b[pl.ds(pl.multiple_of(tb * 8, 8), 8), :] += part
        return 0

    lax.fori_loop(0, UNITS_STEP // UNROLL, body, 0)

    @pl.when(step == pl.num_programs(0) - 1)
    def _():
        ones = jnp.ones((16, 2 * W128), bf16)

        def fold(i, _):
            rows = []
            for j in range(4):
                hi, lo = hilo(acc_a[i * 4 + j])
                rows.append(lax.dot_general(ones, jnp.concatenate([hi, lo], 1), (((1,), (1,)), ((), ())),
                                            preferred_element_type=f32))
            for j in range(4):
                dens_o[pl.ds(i * 4 + j, 1), :] = rows[j][:1]
            return 0

        lax.fori_loop(0, NB // 4, fold, 0)
        for i in range(EXT // 8):
            v = acc_b[pl.ds(i * 64, 8, stride=8), :]
            for s in range(1, 8):
                v = v + acc_b[pl.ds(i * 64 + s, 8, stride=8), :]
            if i < NB // 8:
                r = slice(i * 8, i * 8 + 8)
                dens_o[r] = (dens_o[r] + (v + self_sum[r])) * (4.0 * NORM) / mass[r]
            else:
                n = i - NB // 8
                dens_g[n] = v * (4.0 * NORM) / ghost[n, 3]


def back_kernel(idx, send_list, idx_v, hot, pos, mass, ghost, part, gpart, energy, tiles_h, own_h, dens_o, acc_o,
                T, R, RS, MM, C, hot_a, hot_b, press, gpress, ret, buf, gacc, racc,
                tile_sem, s1, r1, s2, r2, s3, r3):
    pairs = tiles_h.shape[0]
    chunks = pairs // CHUNK
    tail = chunks - 2

    def tile_copy(c):
        at = pl.ds(c * CHUNK, CHUNK)
        return pltpu.make_async_copy(tiles_h.at[at], T.at[at], tile_sem.at[c])

    own_at = pl.ds(tail * CHUNK, NB)
    own_copy = pltpu.make_async_copy(own_h, T.at[own_at], tile_sem.at[chunks])
    own_copy.start()
    for c in range(tail):
        tile_copy(c).start()
    meet()
    copies = start_all(gpart, ret, s1, r1, -1)

    slots = R.shape[0] // 16
    R[pairs * 8:slots * 8] = jnp.zeros(((slots - pairs) * 8, W128), f32)
    R[(slots + pairs) * 8:] = jnp.zeros(((slots - pairs) * 8, W128), f32)
    for w in range(slots // W128):
        at = slice(w * W128, (w + 1) * W128)
        for matrix, row in ((hot_a, 2), (hot_b, 3)):
            rows = matrix.shape[0]
            which = idx_v[row:row + 1, at]
            blocks = lax.broadcasted_iota(jnp.int32, (rows, W128), 0)
            matrix[:, at] = jnp.where(blocks == which, 1.0, 0.0).astype(bf16)

    def weights(at, rows, x, y, z, m, p):
        k = inverse_cube_root(m)
        w = k * k
        pw = p * w
        for i, v in enumerate((w, w * x, w * y, w * z, pw, pw * x, pw * y, pw * z)):
            C[i * EXT + at:i * EXT + at + rows] = v

    def columns(i, _):
        for j in range(4):
            b = i * 4 + j
            v = C[pl.ds(b, 8, stride=EXT), :]
            hi = v.astype(bf16).astype(f32)
            mm = jnp.concatenate([hi, v - hi], 0).astype(bf16)
            MM[b, :, :W128] = mm
            MM[b, :, W128:] = mm
        return 0

    for copy in copies:
        copy.wait()
    dens = part[...] + split_dot(hot[:, :GHOSTS], ret[...].reshape(GHOSTS, W128))
    dens_o[...] = dens
    press[...] = GAMMA_LESS * energy[...] / dens

    def gather(n, _):
        for g in range(SLOTS):
            buf[n, g:g + 1, :] = press[pl.ds(send_list[0, n, g], 1), :]
        return 0

    lax.fori_loop(0, NEIGH, gather, 0)
    copies = start_all(buf, gpress, s2, r2, 1)

    weights(0, NB, pos[0], pos[1], pos[2], mass[...], press[...])
    lax.fori_loop(0, NB // 4, columns, 0)

    def to_b(k, hi, lo):
        return jnp.dot(MM[idx[0, k]], jnp.concatenate([hi, lo], 0), preferred_element_type=f32)

    def to_a(k, hi, lo):
        return lax.dot_general(MM[idx[1, k]], jnp.concatenate([hi, lo], 1), (((1,), (1,)), ((), ())),
                               preferred_element_type=f32)

    def put(ref, k, v):
        ref[pl.ds(pl.multiple_of(k * 8, 8), 8), :] = v[:8] + v[8:]

    def own_body(u, _):
        out = []
        for j in range(16):
            a = u * 16 + j
            hi, lo = hilo(T[tail * CHUNK + a])
            out.append((a, jnp.dot(MM[a], jnp.concatenate([hi, lo], 0), preferred_element_type=f32)))
        for a, v in out:
            put(RS, a, v)
        return 0

    def pair_body(do_a, do_b, u, _):
        out = []
        for j in range(FORCE_UNROLL):
            k = u * FORCE_UNROLL + j
            hi, lo = hilo(T[k])
            if do_b:
                out.append((slots + k, to_b(k, hi, lo)))
            if do_a:
                out.append((k, to_a(k, hi, lo)))
        for k, v in out:
            put(R, k, v)
        return 0

    per = CHUNK // FORCE_UNROLL
    own_copy.wait()
    lax.fori_loop(0, NB // 16, own_body, 0)
    for c in range(tail, chunks):
        tile_copy(c).start()
    for c in range(EARLY):
        tile_copy(c).wait()
    lax.fori_loop(0, EARLY * per, functools.partial(pair_body, False, True), 0)
    for copy in copies:
        copy.wait()
    for n in range(NEIGH):
        weights(NB + n * SLOTS, SLOTS, *[ghost[n, c] for c in range(4)], gpress[n])
    lax.fori_loop(NB // 4, EXT // 4, columns, 0)
    lax.fori_loop(0, EARLY * per, functools.partial(pair_body, True, False), 0)

    def chunk_body(c, _):
        tile_copy(c).wait()
        lax.fori_loop(c * per, (c + 1) * per, functools.partial(pair_body, True, True), 0)
        return 0

    lax.fori_loop(EARLY, chunks, chunk_body, 0)

    dot = functools.partial(jnp.dot, preferred_element_type=f32)
    A = []
    for c in range(0, 8, 2):
        total = []
        for half, matrix in ((0, hot_a), (1, hot_b)):
            v = [R[pl.ds(half * slots * 8 + c + i, slots, stride=8), :] for i in range(2)]
            hi, lo = hilo(jnp.concatenate(v, 1))
            total.append(dot(matrix[...], hi) + dot(matrix[...], lo))
        own = total[1][:NB] + total[0]
        for i in range(2):
            at = slice(i * W128, (i + 1) * W128)
            A.append((own[:, at] + RS[pl.ds(c + i, NB, stride=8), :], total[1][NB:, at]))
    scale = -20.0 * NORM

    def final(p, m, spot, A):
        k = inverse_cube_root(m)
        k2 = k * k
        own = p * A[0] + A[4]
        return [(p * A[c + 1] + A[c + 5] - v * own) * (scale * (k2 * k2 * k)) for c, v in enumerate(spot)]

    for n in range(NEIGH):
        r = slice(n * SLOTS, (n + 1) * SLOTS)
        for c, v in enumerate(final(gpress[n], ghost[n, 3], [ghost[n, c] for c in range(3)], [x[1][r] for x in A])):
            gacc[n, c] = v
    copies = start_all(gacc, racc, s3, r3, -1)
    mine = final(press[...], mass[...], [pos[c] for c in range(3)], [x[0] for x in A])
    for copy in copies:
        copy.wait()
    for c in range(3):
        acc_o[:, c, :] = mine[c] + split_dot(hot[:, :GHOSTS], racc[:, c].reshape(GHOSTS, W128))


V = pl.BlockSpec(memory_space=pltpu.VMEM)
SM = pl.BlockSpec(memory_space=pltpu.SMEM)
sds = jax.ShapeDtypeStruct


def run_forward(send_list, pair_count, pair_list, pos, mass, smoothing, level):
    D = pltpu.SemaphoreType.DMA((NEIGH,))
    slots = pair_list.shape[2] + 2 * W128 - pair_list.shape[2] % W128
    vm = pltpu.VMEM
    return pl.pallas_call(
        forward_kernel,
        out_shape=[
            sds((NEIGH, 5, SLOTS, W128), f32), sds((4, slots), jnp.int32), sds((NB, 2 * W128), bf16),
            sds((3, NB, W128), f32), sds((NB, W128), f32), sds((NB, W128), f32), sds((NB, W128, W128), f32)],
        in_specs=[SM, SM, V, V, V, V, V], out_specs=[V] * 6 + [pl.BlockSpec(memory_space=pl.ANY)],
        scratch_shapes=[
            vm((NEIGH, 5, SLOTS, W128), f32), vm((2 * W128, W128), f32), vm((13 * NB, W128), f32), vm((8 * NB, W128), f32),
            vm((SELF, W128, 64), bf16), vm((SELF, 64, 2 * W128), bf16), vm((SELF, W128, 2 * W128), f32),
            vm((NB, W128, W128), f32), D, D, pltpu.SemaphoreType.DMA((NB // SELF,))],
        compiler_params=pltpu.CompilerParams(collective_id=0, has_side_effects=True, vmem_limit_bytes=VMEM),
        name="forward")(send_list, pair_count, pair_list, pos, mass, smoothing, level)


def run_density(idx, pos, mass, smooth, ghost, self_sum, pairs):
    vm = pltpu.VMEM
    return pl.pallas_call(
        density_pairs,
        grid_spec=pltpu.PrefetchScalarGridSpec(
            num_scalar_prefetch=1, grid=(pairs // UNITS_STEP,), in_specs=[V] * 5,
            out_specs=[V, V, pl.BlockSpec((UNITS_STEP, W128, W128), lambda i, *_: (i, 0, 0))],
            scratch_shapes=[
                vm((13 * EXT, W128), f32), vm((8 * NB, W128), f32), vm((NB, W128, 64), bf16), vm((EXT, 64, 2 * W128), bf16),
                vm((UNROLL, W128, 2 * W128), f32), vm((NB + 1, W128, W128), f32), vm(((EXT + 1) * 8, W128), f32)]),
        out_shape=[sds((NB, W128), f32), sds((NEIGH, SLOTS, W128), f32), sds((pairs, W128, W128), f32)],
        compiler_params=pltpu.CompilerParams(vmem_limit_bytes=VMEM),
        name="density_pairs")(idx, pos, mass, smooth, ghost, self_sum)


def run_back(idx, send_list, hot, pos, mass, ghost, part, gpart, energy, tiles, own_tiles):
    D = pltpu.SemaphoreType.DMA((NEIGH,))
    vm = pltpu.VMEM
    pairs = tiles.shape[0]
    slots = pairs + (-pairs) % (2 * W128)
    A = pl.BlockSpec(memory_space=pl.ANY)
    return pl.pallas_call(
        back_kernel,
        out_shape=[sds((NB, W128), f32), sds((NB, 3, W128), f32)],
        in_specs=[SM, SM] + [V] * 8 + [A, A], out_specs=[V, V],
        scratch_shapes=[
            vm((pairs, W128, W128), f32), vm((2 * slots * 8, W128), f32), vm((NB * 8, W128), f32),
            vm((EXT, 16, 2 * W128), bf16), vm((8 * EXT, W128), f32), vm((NB, slots), bf16), vm((EXT, slots), bf16),
            vm((NB, W128), f32), vm((NEIGH, SLOTS, W128), f32), vm((NEIGH, SLOTS, W128), f32), vm((NEIGH, SLOTS, W128), f32),
            vm((NEIGH, 3, SLOTS, W128), f32), vm((NEIGH, 3, SLOTS, W128), f32),
            pltpu.SemaphoreType.DMA((pairs // CHUNK + 1,)), D, D, D, D, D, D],
        compiler_params=pltpu.CompilerParams(collective_id=1, has_side_effects=True, vmem_limit_bytes=VMEM),
        name="back")(idx, send_list, idx, hot, pos, mass, ghost, part, gpart, energy, tiles, own_tiles)


def per_device(positions, masses, smoothing, energy, level_ids, send_list, pair_list, pair_count):
    mass = masses.reshape(NB, W128)
    ghost, idx, hot, pos, smooth, self_sum, own_tiles = run_forward(
        send_list, pair_count, pair_list, positions.reshape(3, NB, W128).transpose(1, 0, 2), mass,
        smoothing.reshape(NB, W128), level_ids.reshape(1, NB))
    dens, gdens, tiles = run_density(idx, pos, mass, smooth, ghost, self_sum, pair_list.shape[2])
    density, accel = run_back(
        idx, send_list, hot, pos, mass, ghost, dens, gdens, energy.reshape(NB, W128), tiles, own_tiles)
    return density.reshape(NB * W128), accel.transpose(1, 0, 2).reshape(3, NB * W128)


def solution(mesh):
    both = ("patch", "bulk")
    placed = (P(None, both), P(both), P(both), P(both), P(both), P(both, None, None), P(both, None, None), P(both))
    return jax.shard_map(per_device, mesh=mesh, in_specs=placed, out_specs=(P(both), P(None, both)), check_vma=False)
```

```python
import functools
import math

import jax
import jax.numpy as jnp
from jax import lax
from jax.experimental import pallas as pl
from jax.experimental.pallas import tpu as pltpu
from jax.sharding import PartitionSpec as P

MESH = pl.DeviceIdType.MESH
f32 = jnp.float32
bf16 = jnp.bfloat16
NORM = 21.0 / (2.0 * math.pi)
GAMMA_LESS = 2.0 / 3.0
SHRINK = 0.8
NB = 128
W128 = 128
NEIGH = 20
SLOTS = 8
GHOSTS = NEIGH * SLOTS
EXT = NB + GHOSTS
CHUNKS = [(0, 0), (0, 1), (1, 0), (1, 1), (0, 2), (2, 0), (1, 2), (2, 1)]
UNROLL = 14
CHUNK = 84
FORCE_UNROLL = 14
EARLY = 2
SELF = 8
VMEM = 63 * 2**20


def neighbour_steps():
    return [
        (step_patch, step_bulk)
        for step_patch in (-1, 0, 1)
        for step_bulk in range(-3, 4)
        if (step_patch, step_bulk) != (0, 0)
    ]


def place(offset):
    rows, columns = lax.axis_size("patch"), lax.axis_size("bulk")
    count = rows * columns
    me = lax.axis_index("patch") * columns + lax.axis_index("bulk")
    other = lax.rem(me + (offset + count), count)
    return (lax.div(other, columns), lax.rem(other, columns))


def offsets():
    columns = lax.axis_size("bulk")
    return [u * columns + v for u, v in neighbour_steps()]


def meet():
    barrier = pltpu.get_barrier_semaphore()
    for o in offsets():
        pl.semaphore_signal(barrier, inc=1, device_id=place(o), device_id_type=MESH)
    pl.semaphore_wait(barrier, NEIGH)


def start_all(src, dst, send_sem, recv_sem, sign):
    copies = []
    for n, o in enumerate(offsets()):
        copy = pltpu.make_async_remote_copy(
            src_ref=src.at[n], dst_ref=dst.at[n], send_sem=send_sem.at[n], recv_sem=recv_sem.at[n],
            device_id=place(sign * o), device_id_type=MESH)
        copy.start()
        copies.append(copy)
    return copies


def split3(v):
    a = v.astype(bf16).astype(f32)
    r = v - a
    b = r.astype(bf16).astype(f32)
    return a, b, r - b


def hilo(v):
    hi = v.astype(bf16)
    return hi, (v - hi.astype(f32)).astype(bf16)


def split_dot(hot, v):
    a, b, c = [p.astype(bf16) for p in split3(v)]
    dot = functools.partial(jnp.dot, preferred_element_type=f32)
    return dot(hot, a) + (dot(hot, b) + dot(hot, c))


def inverse_cube_root(m):
    k = jnp.exp(jnp.log(m) * (-1.0 / 3.0))
    return k * (4.0 - m * (k * k * k)) * (1.0 / 3.0)


def tile_math(r2, hs):
    r2 = jnp.maximum(r2, 1e-30)
    s = pl.reciprocal(hs, approx=True)
    q = r2 * lax.rsqrt(r2) * s
    t = jnp.maximum(1.0 - q, 0.0)
    st = s * t
    c = st * st * st
    return c * (t * (q + 0.25)), c * (s * s)


def scaled_columns(x, y, z, m, h):
    k = inverse_cube_root(m)
    k2 = k * k
    return x * k2, y * k2, z * k2, k2, (x * x + y * y + z * z) * k2, (0.5 * h) * k, k


def fill_right(C, total, at, rows, v):
    for i, c in ((0, 0), (1, 1), (2, 2), (3, 3), (4, 4), (10, 5), (11, 6)):
        C[i * total + at:i * total + at + rows] = v[c]


def clear_right(C, total):
    zero = jnp.zeros((total, W128), f32)
    for i in (5, 6, 7, 8, 9, 12):
        C[i * total:(i + 1) * total] = zero


def fill_left(CA, v):
    for i, w in enumerate((-2.0 * v[0], -2.0 * v[1], -2.0 * v[2], v[4], v[3], v[6], v[5], jnp.zeros_like(v[0]))):
        CA[i * NB:(i + 1) * NB] = w


def right_features(C, total, b, BF, at):
    for w, c in ((0, 0), (5, W128)):
        p = split3(C[pl.ds(w * total + b, 8, stride=total), :])
        BF[at, :, c:c + W128] = jnp.concatenate([p[q] for _, q in CHUNKS], 0).astype(bf16)


def left_features(CA, b, AF, at):
    p = split3(CA[pl.ds(b, 8, stride=NB), :])
    AF[at] = jnp.concatenate([p[q] for q, _ in CHUNKS], 0).T.astype(bf16)


def pair_matrices(idx_v, hot_a, hot_b):
    for w in range(hot_a.shape[1] // W128):
        at = slice(w * W128, (w + 1) * W128)
        for matrix, row in ((hot_a, 2), (hot_b, 3)):
            which = idx_v[row:row + 1, at]
            blocks = lax.broadcasted_iota(jnp.int32, (matrix.shape[0], W128), 0)
            matrix[:, at] = jnp.where(blocks == which, 1.0, 0.0).astype(bf16)


def front_kernel(send_list, count, pair_ends, pairs, pos, mass, smoothing, level,
                 ghost_o, idx, hot_o, pos_o, dens_o, gdens_o, own_o, tiles_o,
                 smooth, self_sum, buf, hot, C, CA, AF, BF, GB, own_tiles, T, RT, PB, hot_a, hot_b,
                 send_sem, recv_sem, own_sem, tile_sem):
    lev = level[...]
    scale = jnp.where(lev == 0, 1.0, jnp.where(lev == 1, SHRINK, SHRINK * SHRINK)).astype(f32)
    smooth[...] = smoothing[...] * jnp.broadcast_to(scale, (NB, W128)).T
    for c in range(3):
        pos_o[c] = pos[:, c, :]
    lane = lax.broadcasted_iota(jnp.int32, (1, NB), 1)

    def gather(n, _):
        for g in range(SLOTS):
            t = send_list[0, n, g]
            for c in range(3):
                buf[n, c, g:g + 1, :] = pos_o[c, pl.ds(t, 1), :]
            buf[n, 3, g:g + 1, :] = mass[pl.ds(t, 1), :]
            buf[n, 4, g:g + 1, :] = smooth[pl.ds(t, 1), :]
            hot[pl.ds(n * SLOTS + g, 1), :] = jnp.where(lane == t, 1.0, 0.0)
        return 0

    hot[GHOSTS:] = jnp.zeros((2 * W128 - GHOSTS, W128), f32)
    lax.fori_loop(0, NEIGH, gather, 0)
    meet()
    copies = start_all(buf, ghost_o, send_sem, recv_sem, 1)

    npairs = pairs.shape[2]
    live = lax.broadcasted_iota(jnp.int32, (1, npairs), 1) < count[0]
    idx[...] = jnp.zeros_like(idx)
    idx[2:4, :] = jnp.full((2, idx.shape[1]), EXT, jnp.int32)
    first = pairs[0, 0:1, :]
    second = pairs[0, 1:2, :]
    idx[0:1, :npairs] = first
    idx[1:2, :npairs] = second
    idx[2:3, :npairs] = jnp.where(live, first, NB)
    idx[3:4, :npairs] = jnp.where(live, second, EXT)
    pair_matrices(idx, hot_a, hot_b)
    for i in range(2):
        hot_o[:, i * W128:(i + 1) * W128] = hot[i * W128:(i + 1) * W128].T.astype(bf16)
    PB[npairs * 8:] = jnp.zeros((PB.shape[0] - npairs * 8, W128), f32)
    RT[...] = jnp.zeros_like(RT)
    clear_right(C, EXT)
    v = scaled_columns(pos_o[0], pos_o[1], pos_o[2], mass[...], smooth[...])
    fill_right(C, EXT, 0, NB, v)
    fill_left(CA, v)

    def features(g):
        for j in range(SELF):
            b = g * SELF + j
            right_features(C, EXT, b, BF, b)
            left_features(CA, b, AF, b)

    def product(a, b, j):
        GB[j] = jnp.dot(AF[a], BF[b], preferred_element_type=f32)

    def own_copy(g):
        at = pl.ds(g * SELF, SELF)
        return pltpu.make_async_copy(own_tiles.at[at], own_o.at[at], own_sem.at[g])

    features(0)
    for j in range(SELF):
        product(j, j, j)
    features(1)

    def own_body(g, _):
        after = jnp.minimum(g + 1, NB // SELF - 1)
        for j in range(SELF):
            part = jnp.zeros((8, W128), f32)
            for r in range(0, W128, 8):
                W, S = tile_math(GB[j, r:r + 8, :W128], GB[j, r:r + 8, W128:])
                own_tiles[g * SELF + j, r:r + 8] = S
                part = part + W
            self_sum[pl.ds(g * SELF + j, 1), :] = jnp.sum(part, axis=0, keepdims=True)
        own_copy(g).start()
        for j in range(SELF):
            product(after * SELF + j, after * SELF + j, j)
        features(jnp.minimum(g + 2, NB // SELF - 1))
        return 0

    lax.fori_loop(0, NB // SELF, own_body, 0)
    for copy in copies:
        copy.wait()

    for n in range(NEIGH):
        fill_right(C, EXT, NB + n * SLOTS, SLOTS, scaled_columns(*[ghost_o[n, c] for c in range(5)]))

    def ghost_features(i, _):
        for j in range(8):
            right_features(C, EXT, i * 8 + j, BF, i * 8 + j)
        return 0

    lax.fori_loop(NB // 8, EXT // 8, ghost_features, 0)
    for j in range(UNROLL):
        product(pair_ends[0, 0, j], pair_ends[0, 1, j], j)
    lanes = lax.broadcasted_iota(jnp.int32, (8, W128), 1)

    def tile_copy(c):
        return pltpu.make_async_copy(T.at[lax.rem(c, 2)], tiles_o.at[pl.ds(c * CHUNK, CHUNK)], tile_sem.at[c])

    def pair_body(c, u, _):
        k0 = c * CHUNK + u * UNROLL
        slot = lax.rem(c, 2)
        for j in range(UNROLL):
            here = lanes == lax.rem(k0 + j, W128)
            column = lax.div(k0 + j, W128)
            part = jnp.zeros((8, W128), f32)
            for r in range(0, W128, 8):
                W, S = tile_math(GB[j, r:r + 8, :W128], GB[j, r:r + 8, W128:])
                T[slot, u * UNROLL + j, r:r + 8] = S
                part = part + W
                RT[column, r:r + 8] = jnp.where(here, jnp.sum(W, axis=1, keepdims=True), RT[column, r:r + 8])
            PB[pl.ds(pl.multiple_of((k0 + j) * 8, 8), 8), :] = part
            k = jnp.minimum(k0 + UNROLL + j, npairs - 1)
            product(pair_ends[0, 0, k], pair_ends[0, 1, k], j)
        return 0

    chunks = npairs // CHUNK

    def chunk_body(c, _):
        @pl.when(c >= 2)
        def _():
            tile_copy(c - 2).wait()

        lax.fori_loop(0, CHUNK // UNROLL, functools.partial(pair_body, c), 0)
        tile_copy(c).start()
        return 0

    lax.fori_loop(0, chunks, chunk_body, 0)

    dot = functools.partial(jnp.dot, preferred_element_type=f32)
    rows = jnp.zeros((W128, NB), f32)
    for w in range(RT.shape[0]):
        for p in hilo(RT[w]):
            rows = rows + lax.dot_general(p, hot_a[:, w * W128:(w + 1) * W128], (((1,), (1,)), ((), ())),
                                          preferred_element_type=f32)
    slots = PB.shape[0] // 8
    part = PB[pl.ds(0, slots, stride=8), :]
    for i in range(1, 8):
        part = part + PB[pl.ds(i, slots, stride=8), :]
    hi, lo = hilo(part)
    sums = dot(hot_b[...], hi) + dot(hot_b[...], lo)
    dens_o[...] = (sums[:NB] + rows.T + self_sum[...]) * (4.0 * NORM) / mass[...]
    for n in range(NEIGH):
        at = NB + n * SLOTS
        gdens_o[n] = sums[at:at + SLOTS] * (4.0 * NORM) / ghost_o[n, 3]

    def own_landed(g, _):
        own_copy(g).wait()
        return 0

    lax.fori_loop(0, NB // SELF, own_landed, 0)
    for c in range(chunks - 2, chunks):
        tile_copy(c).wait()


def back_kernel(idx, send_list, idx_v, hot, pos, mass, ghost, part, gpart, energy, tiles_h, own_h, dens_o, acc_o,
                T, R, RS, MM, C, hot_a, hot_b, press, gpress, ret, buf, gacc, racc,
                tile_sem, s1, r1, s2, r2, s3, r3):
    pairs = tiles_h.shape[0]
    chunks = pairs // CHUNK
    tail = chunks - 2

    def tile_copy(c):
        at = pl.ds(c * CHUNK, CHUNK)
        return pltpu.make_async_copy(tiles_h.at[at], T.at[at], tile_sem.at[c])

    own_at = pl.ds(tail * CHUNK, NB)
    own_copy = pltpu.make_async_copy(own_h, T.at[own_at], tile_sem.at[chunks])
    own_copy.start()
    for c in range(tail):
        tile_copy(c).start()
    meet()
    copies = start_all(gpart, ret, s1, r1, -1)

    slots = R.shape[0] // 16
    R[pairs * 8:slots * 8] = jnp.zeros(((slots - pairs) * 8, W128), f32)
    R[(slots + pairs) * 8:] = jnp.zeros(((slots - pairs) * 8, W128), f32)
    pair_matrices(idx_v, hot_a, hot_b)

    def weights(at, rows, x, y, z, m, p):
        k = inverse_cube_root(m)
        w = k * k
        pw = p * w
        for i, v in enumerate((w, w * x, w * y, w * z, pw, pw * x, pw * y, pw * z)):
            C[i * EXT + at:i * EXT + at + rows] = v

    def columns(i, _):
        for j in range(4):
            b = i * 4 + j
            v = C[pl.ds(b, 8, stride=EXT), :]
            hi = v.astype(bf16).astype(f32)
            mm = jnp.concatenate([hi, v - hi], 0).astype(bf16)
            MM[b, :, :W128] = mm
            MM[b, :, W128:] = mm
        return 0

    for copy in copies:
        copy.wait()
    dens = part[...] + split_dot(hot[:, :GHOSTS], ret[...].reshape(GHOSTS, W128))
    dens_o[...] = dens
    press[...] = GAMMA_LESS * energy[...] / dens

    def gather(n, _):
        for g in range(SLOTS):
            buf[n, g:g + 1, :] = press[pl.ds(send_list[0, n, g], 1), :]
        return 0

    lax.fori_loop(0, NEIGH, gather, 0)
    copies = start_all(buf, gpress, s2, r2, 1)

    weights(0, NB, pos[0], pos[1], pos[2], mass[...], press[...])
    lax.fori_loop(0, NB // 4, columns, 0)

    def to_b(k, hi, lo):
        return jnp.dot(MM[idx[0, k]], jnp.concatenate([hi, lo], 0), preferred_element_type=f32)

    def to_a(k, hi, lo):
        return lax.dot_general(MM[idx[1, k]], jnp.concatenate([hi, lo], 1), (((1,), (1,)), ((), ())),
                               preferred_element_type=f32)

    def put(ref, k, v):
        ref[pl.ds(pl.multiple_of(k * 8, 8), 8), :] = v[:8] + v[8:]

    def own_body(u, _):
        out = []
        for j in range(16):
            a = u * 16 + j
            hi, lo = hilo(T[tail * CHUNK + a])
            out.append((a, jnp.dot(MM[a], jnp.concatenate([hi, lo], 0), preferred_element_type=f32)))
        for a, v in out:
            put(RS, a, v)
        return 0

    def pair_body(do_a, do_b, u, _):
        out = []
        for j in range(FORCE_UNROLL):
            k = u * FORCE_UNROLL + j
            hi, lo = hilo(T[k])
            if do_b:
                out.append((slots + k, to_b(k, hi, lo)))
            if do_a:
                out.append((k, to_a(k, hi, lo)))
        for k, v in out:
            put(R, k, v)
        return 0

    per = CHUNK // FORCE_UNROLL
    own_copy.wait()
    lax.fori_loop(0, NB // 16, own_body, 0)
    for c in range(tail, chunks):
        tile_copy(c).start()
    for c in range(EARLY):
        tile_copy(c).wait()
    lax.fori_loop(0, EARLY * per, functools.partial(pair_body, False, True), 0)
    for copy in copies:
        copy.wait()
    for n in range(NEIGH):
        weights(NB + n * SLOTS, SLOTS, *[ghost[n, c] for c in range(4)], gpress[n])
    lax.fori_loop(NB // 4, EXT // 4, columns, 0)
    lax.fori_loop(0, EARLY * per, functools.partial(pair_body, True, False), 0)

    def chunk_body(c, _):
        tile_copy(c).wait()
        lax.fori_loop(c * per, (c + 1) * per, functools.partial(pair_body, True, True), 0)
        return 0

    lax.fori_loop(EARLY, chunks, chunk_body, 0)

    dot = functools.partial(jnp.dot, preferred_element_type=f32)
    A = []
    for c in range(0, 8, 2):
        total = []
        for half, matrix in ((0, hot_a), (1, hot_b)):
            v = [R[pl.ds(half * slots * 8 + c + i, slots, stride=8), :] for i in range(2)]
            hi, lo = hilo(jnp.concatenate(v, 1))
            total.append(dot(matrix[...], hi) + dot(matrix[...], lo))
        own = total[1][:NB] + total[0]
        for i in range(2):
            at = slice(i * W128, (i + 1) * W128)
            A.append((own[:, at] + RS[pl.ds(c + i, NB, stride=8), :], total[1][NB:, at]))
    scale = -20.0 * NORM

    def final(p, m, spot, A):
        k = inverse_cube_root(m)
        k2 = k * k
        own = p * A[0] + A[4]
        return [(p * A[c + 1] + A[c + 5] - v * own) * (scale * (k2 * k2 * k)) for c, v in enumerate(spot)]

    for n in range(NEIGH):
        r = slice(n * SLOTS, (n + 1) * SLOTS)
        for c, v in enumerate(final(gpress[n], ghost[n, 3], [ghost[n, c] for c in range(3)], [x[1][r] for x in A])):
            gacc[n, c] = v
    copies = start_all(gacc, racc, s3, r3, -1)
    mine = final(press[...], mass[...], [pos[c] for c in range(3)], [x[0] for x in A])
    for copy in copies:
        copy.wait()
    for c in range(3):
        acc_o[:, c, :] = mine[c] + split_dot(hot[:, :GHOSTS], racc[:, c].reshape(GHOSTS, W128))


V = pl.BlockSpec(memory_space=pltpu.VMEM)
SM = pl.BlockSpec(memory_space=pltpu.SMEM)
sds = jax.ShapeDtypeStruct


def run_front(send_list, pair_count, pair_list, pos, mass, smoothing, level):
    D = pltpu.SemaphoreType.DMA((NEIGH,))
    vm = pltpu.VMEM
    A = pl.BlockSpec(memory_space=pl.ANY)
    pairs = pair_list.shape[2]
    slots = pairs + (-pairs) % (2 * W128)
    return pl.pallas_call(
        front_kernel,
        out_shape=[
            sds((NEIGH, 5, SLOTS, W128), f32), sds((4, slots), jnp.int32), sds((NB, 2 * W128), bf16),
            sds((3, NB, W128), f32), sds((NB, W128), f32), sds((NEIGH, SLOTS, W128), f32),
            sds((NB, W128, W128), f32), sds((pairs, W128, W128), f32)],
        in_specs=[SM, SM, SM, V, V, V, V, V], out_specs=[V] * 6 + [A, A],
        scratch_shapes=[
            vm((NB, W128), f32), vm((NB, W128), f32), vm((NEIGH, 5, SLOTS, W128), f32), vm((2 * W128, W128), f32),
            vm((13 * EXT, W128), f32), vm((8 * NB, W128), f32), vm((NB, W128, 64), bf16), vm((EXT, 64, 2 * W128), bf16),
            vm((UNROLL, W128, 2 * W128), f32), vm((NB, W128, W128), f32), vm((2, CHUNK, W128, W128), f32),
            vm((slots // W128, W128, W128), f32), vm((slots * 8, W128), f32), vm((NB, slots), bf16), vm((EXT, slots), bf16),
            D, D, pltpu.SemaphoreType.DMA((NB // SELF,)), pltpu.SemaphoreType.DMA((pairs // CHUNK,))],
        compiler_params=pltpu.CompilerParams(collective_id=0, has_side_effects=True, vmem_limit_bytes=VMEM),
        name="front")(send_list, pair_count, pair_list, pair_list, pos, mass, smoothing, level)


def run_back(idx, send_list, hot, pos, mass, ghost, part, gpart, energy, tiles, own_tiles):
    D = pltpu.SemaphoreType.DMA((NEIGH,))
    vm = pltpu.VMEM
    pairs = tiles.shape[0]
    slots = pairs + (-pairs) % (2 * W128)
    A = pl.BlockSpec(memory_space=pl.ANY)
    return pl.pallas_call(
        back_kernel,
        out_shape=[sds((NB, W128), f32), sds((NB, 3, W128), f32)],
        in_specs=[SM, SM] + [V] * 8 + [A, A], out_specs=[V, V],
        scratch_shapes=[
            vm((pairs, W128, W128), f32), vm((2 * slots * 8, W128), f32), vm((NB * 8, W128), f32),
            vm((EXT, 16, 2 * W128), bf16), vm((8 * EXT, W128), f32), vm((NB, slots), bf16), vm((EXT, slots), bf16),
            vm((NB, W128), f32), vm((NEIGH, SLOTS, W128), f32), vm((NEIGH, SLOTS, W128), f32), vm((NEIGH, SLOTS, W128), f32),
            vm((NEIGH, 3, SLOTS, W128), f32), vm((NEIGH, 3, SLOTS, W128), f32),
            pltpu.SemaphoreType.DMA((pairs // CHUNK + 1,)), D, D, D, D, D, D],
        compiler_params=pltpu.CompilerParams(collective_id=1, has_side_effects=True, vmem_limit_bytes=VMEM),
        name="back")(idx, send_list, idx, hot, pos, mass, ghost, part, gpart, energy, tiles, own_tiles)


def per_device(positions, masses, smoothing, energy, level_ids, send_list, pair_list, pair_count):
    mass = masses.reshape(NB, W128)
    ghost, idx, hot, pos, dens, gdens, own_tiles, tiles = run_front(
        send_list, pair_count, pair_list, positions.reshape(3, NB, W128).transpose(1, 0, 2), mass,
        smoothing.reshape(NB, W128), level_ids.reshape(1, NB))
    density, accel = run_back(
        idx, send_list, hot, pos, mass, ghost, dens, gdens, energy.reshape(NB, W128), tiles, own_tiles)
    return density.reshape(NB * W128), accel.transpose(1, 0, 2).reshape(3, NB * W128)


def solution(mesh):
    both = ("patch", "bulk")
    placed = (P(None, both), P(both), P(both), P(both), P(both), P(both, None, None), P(both, None, None), P(both))
    return jax.shard_map(per_device, mesh=mesh, in_specs=placed, out_specs=(P(both), P(None, both)), check_vma=False)
```

```python
import functools
import math

import jax
import jax.numpy as jnp
from jax import lax
from jax.experimental import pallas as pl
from jax.experimental.pallas import tpu as pltpu
from jax.sharding import PartitionSpec as P

MESH = pl.DeviceIdType.MESH
f32 = jnp.float32
bf16 = jnp.bfloat16
NORM = 21.0 / (2.0 * math.pi)
GAMMA_LESS = 2.0 / 3.0
SHRINK = 0.8
NB = 128
W128 = 128
NEIGH = 20
SLOTS = 8
GHOSTS = NEIGH * SLOTS
EXT = NB + GHOSTS
CHUNKS = [(0, 0), (0, 1), (1, 0), (1, 1), (0, 2), (2, 0), (1, 2), (2, 1)]
UNROLL = 28
CHUNK = 84
FORCE_UNROLL = 28
KEEP = 5
SELF = 8
VMEM = 63 * 2**20


def neighbour_steps():
    return [
        (step_patch, step_bulk)
        for step_patch in (-1, 0, 1)
        for step_bulk in range(-3, 4)
        if (step_patch, step_bulk) != (0, 0)
    ]


def place(offset):
    rows, columns = lax.axis_size("patch"), lax.axis_size("bulk")
    count = rows * columns
    me = lax.axis_index("patch") * columns + lax.axis_index("bulk")
    other = lax.rem(me + (offset + count), count)
    return (lax.div(other, columns), lax.rem(other, columns))


def offsets():
    columns = lax.axis_size("bulk")
    return [u * columns + v for u, v in neighbour_steps()]


def meet():
    barrier = pltpu.get_barrier_semaphore()
    for o in offsets():
        pl.semaphore_signal(barrier, inc=1, device_id=place(o), device_id_type=MESH)
    pl.semaphore_wait(barrier, NEIGH)


def start_all(src, dst, send_sem, recv_sem, sign):
    copies = []
    for n, o in enumerate(offsets()):
        copy = pltpu.make_async_remote_copy(
            src_ref=src.at[n], dst_ref=dst.at[n], send_sem=send_sem.at[n], recv_sem=recv_sem.at[n],
            device_id=place(sign * o), device_id_type=MESH)
        copy.start()
        copies.append(copy)
    return copies


def split3(v):
    a = v.astype(bf16).astype(f32)
    r = v - a
    b = r.astype(bf16).astype(f32)
    return a, b, r - b


def hilo(v):
    hi = v.astype(bf16)
    return hi, (v - hi.astype(f32)).astype(bf16)


def split_dot(hot, v):
    a, b, c = [p.astype(bf16) for p in split3(v)]
    dot = functools.partial(jnp.dot, preferred_element_type=f32)
    return dot(hot, a) + (dot(hot, b) + dot(hot, c))


def inverse_cube_root(m):
    k = jnp.exp(jnp.log(m) * (-1.0 / 3.0))
    return k * (4.0 - m * (k * k * k)) * (1.0 / 3.0)


def tile_math(r2, hs):
    r2 = jnp.maximum(r2, 1e-30)
    s = pl.reciprocal(hs, approx=True)
    q = r2 * lax.rsqrt(r2) * s
    t = jnp.maximum(1.0 - q, 0.0)
    st = s * t
    c = st * st * st
    return c * (t * (q + 0.25)), c * (s * s)


def scaled_columns(x, y, z, m, h):
    k = inverse_cube_root(m)
    k2 = k * k
    return x * k2, y * k2, z * k2, k2, (x * x + y * y + z * z) * k2, (0.5 * h) * k, k


def fill_right(C, total, at, rows, v):
    for i, c in ((0, 0), (1, 1), (2, 2), (3, 3), (4, 4), (10, 5), (11, 6)):
        C[i * total + at:i * total + at + rows] = v[c]


def clear_right(C, total):
    zero = jnp.zeros((total, W128), f32)
    for i in (5, 6, 7, 8, 9, 12):
        C[i * total:(i + 1) * total] = zero


def fill_left(CA, v):
    for i, w in enumerate((-2.0 * v[0], -2.0 * v[1], -2.0 * v[2], v[4], v[3], v[6], v[5], jnp.zeros_like(v[0]))):
        CA[i * NB:(i + 1) * NB] = w


def right_features(C, total, b, BF, at):
    for w, c in ((0, 0), (5, W128)):
        p = split3(C[pl.ds(w * total + b, 8, stride=total), :])
        BF[at, :, c:c + W128] = jnp.concatenate([p[q] for _, q in CHUNKS], 0).astype(bf16)


def left_features(CA, b, AF, at):
    p = split3(CA[pl.ds(b, 8, stride=NB), :])
    AF[at] = jnp.concatenate([p[q] for q, _ in CHUNKS], 0).T.astype(bf16)


def pair_matrices(idx_v, hot_a, hot_b):
    for w in range(hot_a.shape[1] // W128):
        at = slice(w * W128, (w + 1) * W128)
        for matrix, row in ((hot_a, 2), (hot_b, 3)):
            which = idx_v[row:row + 1, at]
            blocks = lax.broadcasted_iota(jnp.int32, (matrix.shape[0], W128), 0)
            matrix[:, at] = jnp.where(blocks == which, 1.0, 0.0).astype(bf16)


def whole_kernel(send_list, count, pair_ends, pairs, pos_in, mass, smoothing, energy, level,
                 dens_o, acc_o, own_h, tiles_h,
                 ghost, idx, hot_o, pos, smooth, self_sum, gdens, buf, C, AF, BF, GB, T, RT, R, RS, MM, hot_a, hot_b,
                 gpress, ret, gacc, racc,
                 send_sem, recv_sem, own_sem, tile_sem, s1, r1, s2, r2, s3, r3):
    left = R.at[pl.ds(0, 8 * NB)]
    press, pbuf = smooth, gdens
    hot = R.at[pl.ds(8 * NB, 2 * W128)]
    right = R.at[pl.ds(R.shape[0] // 2, 13 * EXT)]
    lev = level[...]
    scale = jnp.where(lev == 0, 1.0, jnp.where(lev == 1, SHRINK, SHRINK * SHRINK)).astype(f32)
    smooth[...] = smoothing[...] * jnp.broadcast_to(scale, (NB, W128)).T
    for c in range(3):
        pos[c] = pos_in[:, c, :]
    lane = lax.broadcasted_iota(jnp.int32, (1, NB), 1)

    def gather(n, _):
        for g in range(SLOTS):
            t = send_list[0, g, n]
            for c in range(3):
                buf[n, c, g:g + 1, :] = pos[c, pl.ds(t, 1), :]
            buf[n, 3, g:g + 1, :] = mass[pl.ds(t, 1), :]
            buf[n, 4, g:g + 1, :] = smooth[pl.ds(t, 1), :]
            hot[pl.ds(n * SLOTS + g, 1), :] = jnp.where(lane == t, 1.0, 0.0)
        return 0

    hot[pl.ds(GHOSTS, 2 * W128 - GHOSTS), :] = jnp.zeros((2 * W128 - GHOSTS, W128), f32)
    lax.fori_loop(0, NEIGH, gather, 0)
    meet()
    copies = start_all(buf, ghost, send_sem, recv_sem, 1)

    npairs = pairs.shape[2]
    live = lax.broadcasted_iota(jnp.int32, (1, npairs), 1) < count[0]
    idx[...] = jnp.zeros_like(idx)
    idx[2:4, :] = jnp.full((2, idx.shape[1]), EXT, jnp.int32)
    first = pairs[0, 0:1, :]
    second = pairs[0, 1:2, :]
    idx[0:1, :npairs] = first
    idx[1:2, :npairs] = second
    idx[2:3, :npairs] = jnp.where(live, first, NB)
    idx[3:4, :npairs] = jnp.where(live, second, EXT)
    pair_matrices(idx, hot_a, hot_b)
    for i in range(2):
        hot_o[:, i * W128:(i + 1) * W128] = hot[i * W128:(i + 1) * W128].T.astype(bf16)
    slots = R.shape[0] // 16
    R[npairs * 8:slots * 8] = jnp.zeros(((slots - npairs) * 8, W128), f32)
    R[(slots + npairs) * 8:] = jnp.zeros(((slots - npairs) * 8, W128), f32)
    RT[...] = jnp.zeros_like(RT)
    clear_right(right, EXT)
    v = scaled_columns(pos[0], pos[1], pos[2], mass[...], smooth[...])
    fill_right(right, EXT, 0, NB, v)
    fill_left(left, v)

    own_first = (KEEP - 2) * CHUNK
    chunks = npairs // CHUNK

    def features(g):
        for j in range(SELF):
            b = g * SELF + j
            right_features(right, EXT, b, BF, b)
            left_features(left, b, AF, b)

    def product(a, b, j):
        GB[j] = jnp.dot(AF[a], BF[b], preferred_element_type=f32)

    def own_copy(g):
        return pltpu.make_async_copy(T.at[pl.ds(own_first + g * SELF, SELF)], own_h.at[pl.ds(g * SELF, SELF)], own_sem.at[g])

    features(0)
    for j in range(SELF):
        product(j, j, j)
    features(1)

    def own_body(g, _):
        after = jnp.minimum(g + 1, NB // SELF - 1)
        for j in range(SELF):
            part = jnp.zeros((8, W128), f32)
            for r in range(0, W128, 8):
                W, S = tile_math(GB[j, r:r + 8, :W128], GB[j, r:r + 8, W128:])
                T[own_first + g * SELF + j, r:r + 8] = S
                part = part + W
            self_sum[pl.ds(g * SELF + j, 1), :] = jnp.sum(part, axis=0, keepdims=True)
        own_copy(g).start()
        for j in range(SELF):
            product(after * SELF + j, after * SELF + j, j)
        features(jnp.minimum(g + 2, NB // SELF - 1))
        return 0

    lax.fori_loop(0, NB // SELF, own_body, 0)
    for copy in copies:
        copy.wait()

    for n in range(NEIGH):
        fill_right(right, EXT, NB + n * SLOTS, SLOTS, scaled_columns(*[ghost[n, c] for c in range(5)]))

    def ghost_features(i, _):
        for j in range(8):
            right_features(right, EXT, i * 8 + j, BF, i * 8 + j)
        return 0

    lax.fori_loop(NB // 8, EXT // 8, ghost_features, 0)
    for j in range(UNROLL):
        product(pair_ends[0, 0, j], pair_ends[0, 1, j], j)
    lanes = lax.broadcasted_iota(jnp.int32, (8, W128), 1)

    def spill_out(c):
        at = pl.ds(c * CHUNK, CHUNK)
        return pltpu.make_async_copy(T.at[at], tiles_h.at[at], tile_sem.at[c])

    def spill_back(c):
        at = pl.ds(c * CHUNK, CHUNK)
        return pltpu.make_async_copy(tiles_h.at[at], T.at[at], tile_sem.at[chunks - KEEP + c])

    def pair_body(c, u, _):
        k0 = c * CHUNK + u * UNROLL
        slot = lax.rem(c, KEEP) * CHUNK + u * UNROLL
        for j in range(UNROLL):
            here = lanes == lax.rem(k0 + j, W128)
            column = lax.div(k0 + j, W128)
            part = jnp.zeros((8, W128), f32)
            for r in range(0, W128, 8):
                W, S = tile_math(GB[j, r:r + 8, :W128], GB[j, r:r + 8, W128:])
                T[slot + j, r:r + 8] = S
                part = part + W
                RT[column, r:r + 8] = jnp.where(here, jnp.sum(W, axis=1, keepdims=True), RT[column, r:r + 8])
            R[pl.ds(pl.multiple_of((k0 + j) * 8, 8), 8), :] = part
            k = jnp.minimum(k0 + UNROLL + j, npairs - 1)
            product(pair_ends[0, 0, k], pair_ends[0, 1, k], j)
        return 0

    def own_landed(g, _):
        own_copy(g).wait()
        return 0

    def chunk_body(c, _):
        @pl.when(c == KEEP - 2)
        def _():
            lax.fori_loop(0, NB // SELF, own_landed, 0)

        @pl.when(c >= KEEP)
        def _():
            spill_out(c - KEEP).wait()

        lax.fori_loop(0, CHUNK // UNROLL, functools.partial(pair_body, c), 0)

        @pl.when(c < chunks - KEEP)
        def _():
            spill_out(c).start()

        return 0

    lax.fori_loop(0, chunks, chunk_body, 0)

    dot = functools.partial(jnp.dot, preferred_element_type=f32)
    rows = jnp.zeros((W128, NB), f32)
    for w in range(RT.shape[0]):
        for p in hilo(RT[w]):
            rows = rows + lax.dot_general(p, hot_a[:, w * W128:(w + 1) * W128], (((1,), (1,)), ((), ())),
                                          preferred_element_type=f32)
    part = R[pl.ds(0, slots, stride=8), :]
    for i in range(1, 8):
        part = part + R[pl.ds(i, slots, stride=8), :]
    hi, lo = hilo(part)
    sums = dot(hot_b[...], hi) + dot(hot_b[...], lo)
    for n in range(NEIGH):
        at = NB + n * SLOTS
        gdens[n] = sums[at:at + SLOTS] * (4.0 * NORM) / ghost[n, 3]
    copies = start_all(gdens, ret, s1, r1, -1)
    mine = (sums[:NB] + rows.T + self_sum[...]) * (4.0 * NORM) / mass[...]

    def weights(at, rows, x, y, z, m, p):
        k = inverse_cube_root(m)
        w = k * k
        pw = p * w
        for i, v in enumerate((w, w * x, w * y, w * z, pw, pw * x, pw * y, pw * z)):
            C[i * EXT + at:i * EXT + at + rows] = v

    def columns(i, _):
        for j in range(4):
            b = i * 4 + j
            v = C[pl.ds(b, 8, stride=EXT), :]
            hi = v.astype(bf16).astype(f32)
            mm = jnp.concatenate([hi, v - hi], 0).astype(bf16)
            MM[b, :, :W128] = mm
            MM[b, :, W128:] = mm
        return 0

    for copy in copies:
        copy.wait()
    dens = mine + split_dot(hot_o[:, :GHOSTS], ret[...].reshape(GHOSTS, W128))
    dens_o[...] = dens
    press[...] = GAMMA_LESS * energy[...] / dens

    def gather_press(n, _):
        for g in range(SLOTS):
            pbuf[n, g:g + 1, :] = press[pl.ds(send_list[0, g, n], 1), :]
        return 0

    lax.fori_loop(0, NEIGH, gather_press, 0)
    copies = start_all(pbuf, gpress, s2, r2, 1)

    weights(0, NB, pos[0], pos[1], pos[2], mass[...], press[...])
    lax.fori_loop(0, NB // 4, columns, 0)

    def to_b(k, hi, lo):
        return jnp.dot(MM[pair_ends[0, 0, k]], jnp.concatenate([hi, lo], 0), preferred_element_type=f32)

    def to_a(k, hi, lo):
        return lax.dot_general(MM[pair_ends[0, 1, k]], jnp.concatenate([hi, lo], 1), (((1,), (1,)), ((), ())),
                               preferred_element_type=f32)

    def put(ref, k, v):
        ref[pl.ds(pl.multiple_of(k * 8, 8), 8), :] = v[:8] + v[8:]

    def own_sums(u, _):
        out = []
        for j in range(16):
            a = u * 16 + j
            hi, lo = hilo(T[own_first + a])
            out.append((a, jnp.dot(MM[a], jnp.concatenate([hi, lo], 0), preferred_element_type=f32)))
        for a, v in out:
            put(RS, a, v)
        return 0

    def pair_sums(do_a, do_b, c, u, _):
        out = []
        for j in range(FORCE_UNROLL):
            k = c * CHUNK + u * FORCE_UNROLL + j
            hi, lo = hilo(T[lax.rem(c, KEEP) * CHUNK + u * FORCE_UNROLL + j])
            if do_b:
                out.append((slots + k, to_b(k, hi, lo)))
            if do_a:
                out.append((k, to_a(k, hi, lo)))
        for k, v in out:
            put(R, k, v)
        return 0

    def chunk_sums(do_a, do_b, c):
        lax.fori_loop(0, CHUNK // FORCE_UNROLL, functools.partial(pair_sums, do_a, do_b, c), 0)

    def early(do_a, do_b, i, _):
        chunk_sums(do_a, do_b, KEEP + i)
        return 0

    lax.fori_loop(0, chunks - KEEP, functools.partial(early, False, True), 0)
    for copy in copies:
        copy.wait()
    for n in range(NEIGH):
        weights(NB + n * SLOTS, SLOTS, *[ghost[n, c] for c in range(4)], gpress[n])
    lax.fori_loop(NB // 4, EXT // 4, columns, 0)
    lax.fori_loop(0, chunks - KEEP, functools.partial(early, True, False), 0)
    for c in range(chunks - KEEP):
        spill_back(c).start()
    own_back = pltpu.make_async_copy(own_h, T.at[pl.ds(own_first, NB)], tile_sem.at[2 * (chunks - KEEP)])

    def rest(i, _):
        c = lax.rem(chunks - KEEP + i, KEEP)

        @pl.when(i == 2)
        def _():
            own_back.start()

        @pl.when(i >= 2)
        def _():
            spill_back(c).wait()

        chunk_sums(True, True, c)
        return 0

    lax.fori_loop(0, KEEP, rest, 0)
    own_back.wait()
    lax.fori_loop(0, NB // 16, own_sums, 0)

    A = []
    for c in range(0, 8, 2):
        total = []
        for half, matrix in ((0, hot_a), (1, hot_b)):
            v = [R[pl.ds(half * slots * 8 + c + i, slots, stride=8), :] for i in range(2)]
            hi, lo = hilo(jnp.concatenate(v, 1))
            total.append(dot(matrix[...], hi) + dot(matrix[...], lo))
        own = total[1][:NB] + total[0]
        for i in range(2):
            at = slice(i * W128, (i + 1) * W128)
            A.append((own[:, at] + RS[pl.ds(c + i, NB, stride=8), :], total[1][NB:, at]))
    scale = -20.0 * NORM

    def final(p, m, spot, A):
        k = inverse_cube_root(m)
        k2 = k * k
        own = p * A[0] + A[4]
        return [(p * A[c + 1] + A[c + 5] - v * own) * (scale * (k2 * k2 * k)) for c, v in enumerate(spot)]

    for n in range(NEIGH):
        r = slice(n * SLOTS, (n + 1) * SLOTS)
        for c, v in enumerate(final(gpress[n], ghost[n, 3], [ghost[n, c] for c in range(3)], [x[1][r] for x in A])):
            gacc[n, c] = v
    copies = start_all(gacc, racc, s3, r3, -1)
    mine = final(press[...], mass[...], [pos[c] for c in range(3)], [x[0] for x in A])
    for copy in copies:
        copy.wait()
    for c in range(3):
        acc_o[:, c, :] = mine[c] + split_dot(hot_o[:, :GHOSTS], racc[:, c].reshape(GHOSTS, W128))


V = pl.BlockSpec(memory_space=pltpu.VMEM)
SM = pl.BlockSpec(memory_space=pltpu.SMEM)
sds = jax.ShapeDtypeStruct


def run_whole(send_list, pair_count, pair_list, pos, mass, smoothing, energy, level):
    D = pltpu.SemaphoreType.DMA((NEIGH,))
    vm = pltpu.VMEM
    A = pl.BlockSpec(memory_space=pl.ANY)
    pairs = pair_list.shape[2]
    slots = pairs + (-pairs) % (2 * W128)
    one = vm((NB, W128), f32)
    eight = vm((NEIGH, SLOTS, W128), f32)
    three = vm((NEIGH, 3, SLOTS, W128), f32)
    five = vm((NEIGH, 5, SLOTS, W128), f32)
    return pl.pallas_call(
        whole_kernel,
        out_shape=[sds((NB, W128), f32), sds((NB, 3, W128), f32), sds((NB, W128, W128), f32),
                   sds((pairs - KEEP * CHUNK, W128, W128), f32)],
        in_specs=[SM, SM, SM, V, V, V, V, V, V], out_specs=[V, V, A, A],
        scratch_shapes=[
            five, vm((4, slots), jnp.int32), vm((NB, 2 * W128), bf16), vm((3, NB, W128), f32), one, one, eight, five,
            vm((8 * EXT, W128), f32), vm((NB, W128, 64), bf16),
            vm((EXT, 64, 2 * W128), bf16), vm((UNROLL, W128, 2 * W128), f32), vm((KEEP * CHUNK, W128, W128), f32),
            vm((slots // W128, W128, W128), f32), vm((2 * slots * 8, W128), f32), vm((NB * 8, W128), f32),
            vm((EXT, 16, 2 * W128), bf16), vm((NB, slots), bf16), vm((EXT, slots), bf16),
            eight, eight, three, three,
            D, D, pltpu.SemaphoreType.DMA((NB // SELF,)), pltpu.SemaphoreType.DMA((2 * (pairs // CHUNK - KEEP) + 1,)), D, D, D, D, D, D],
        compiler_params=pltpu.CompilerParams(collective_id=0, has_side_effects=True, vmem_limit_bytes=VMEM),
        name="whole")(send_list, pair_count, pair_list, pair_list, pos, mass, smoothing, energy, level)


def per_device(positions, masses, smoothing, energy, level_ids, send_list, pair_list, pair_count):
    mass = masses.reshape(NB, W128)
    density, accel, _, _ = run_whole(
        send_list.transpose(0, 2, 1), pair_count, pair_list, positions.reshape(3, NB, W128).transpose(1, 0, 2), mass,
        smoothing.reshape(NB, W128), energy.reshape(NB, W128), level_ids.reshape(1, NB))
    return density.reshape(NB * W128), accel.transpose(1, 0, 2).reshape(3, NB * W128)


def solution(mesh):
    both = ("patch", "bulk")
    placed = (P(None, both), P(both), P(both), P(both), P(both), P(both, None, None), P(both, None, None), P(both))
    return jax.shard_map(per_device, mesh=mesh, in_specs=placed, out_specs=(P(both), P(None, both)), check_vma=False)
```

```python
import functools
import math

import jax
import jax.numpy as jnp
from jax import lax
from jax.experimental import pallas as pl
from jax.experimental.pallas import tpu as pltpu
from jax.sharding import PartitionSpec as P

MESH = pl.DeviceIdType.MESH
f32 = jnp.float32
bf16 = jnp.bfloat16
NORM = 21.0 / (2.0 * math.pi)
GAMMA_LESS = 2.0 / 3.0
SHRINK = 0.8
NB = 128
W128 = 128
NEIGH = 20
SLOTS = 8
GHOSTS = NEIGH * SLOTS
EXT = NB + GHOSTS
CHUNKS = [(0, 0), (0, 1), (1, 0), (1, 1), (0, 2), (2, 0), (1, 2), (2, 1)]
UNROLL = 28
CHUNK = 84
FORCE_UNROLL = 42
KEEP = 5
SELF = 8
VMEM = 63 * 2**20


def neighbour_steps():
    return [
        (step_patch, step_bulk)
        for step_patch in (-1, 0, 1)
        for step_bulk in range(-3, 4)
        if (step_patch, step_bulk) != (0, 0)
    ]


def place(offset):
    rows, columns = lax.axis_size("patch"), lax.axis_size("bulk")
    count = rows * columns
    me = lax.axis_index("patch") * columns + lax.axis_index("bulk")
    other = lax.rem(me + (offset + count), count)
    return (lax.div(other, columns), lax.rem(other, columns))


def offsets():
    columns = lax.axis_size("bulk")
    return [u * columns + v for u, v in neighbour_steps()]


def greet():
    barrier = pltpu.get_barrier_semaphore()
    for o in offsets():
        pl.semaphore_signal(barrier, inc=1, device_id=place(o), device_id_type=MESH)
    return barrier


def start_all(src, dst, send_sem, recv_sem, sign):
    copies = []
    for n, o in enumerate(offsets()):
        copy = pltpu.make_async_remote_copy(
            src_ref=src.at[n], dst_ref=dst.at[n], send_sem=send_sem.at[n], recv_sem=recv_sem.at[n],
            device_id=place(sign * o), device_id_type=MESH)
        copy.start()
        copies.append(copy)
    return copies


def split3(v):
    a = v.astype(bf16).astype(f32)
    r = v - a
    b = r.astype(bf16).astype(f32)
    return a, b, r - b


def hilo(v):
    hi = v.astype(bf16)
    return hi, (v - hi.astype(f32)).astype(bf16)


def split_dot(hot, v):
    a, b, c = [p.astype(bf16) for p in split3(v)]
    dot = functools.partial(jnp.dot, preferred_element_type=f32)
    return dot(hot, a) + (dot(hot, b) + dot(hot, c))


def inverse_cube_root(m):
    k = jnp.exp(jnp.log(m) * (-1.0 / 3.0))
    return k * (4.0 - m * (k * k * k)) * (1.0 / 3.0)


def tile_math(r2, hs):
    r2 = jnp.maximum(r2, 1e-30)
    s = pl.reciprocal(hs, approx=True)
    q = r2 * lax.rsqrt(r2) * s
    t = jnp.maximum(1.0 - q, 0.0)
    st = s * t
    c = st * st * st
    return c * (t * (q + 0.25)), c * (s * s)


def scaled_columns(x, y, z, m, h):
    k = inverse_cube_root(m)
    k2 = k * k
    return x * k2, y * k2, z * k2, k2, (x * x + y * y + z * z) * k2, (0.5 * h) * k, k


def fill_right(C, total, at, rows, v):
    for i, c in ((0, 0), (1, 1), (2, 2), (3, 3), (4, 4), (10, 5), (11, 6)):
        C[i * total + at:i * total + at + rows] = v[c]


def clear_right(C, total):
    zero = jnp.zeros((total, W128), f32)
    for i in (5, 6, 7, 8, 9, 12):
        C[i * total:(i + 1) * total] = zero


def fill_left(CA, v):
    for i, w in enumerate((-2.0 * v[0], -2.0 * v[1], -2.0 * v[2], v[4], v[3], v[6], v[5], jnp.zeros_like(v[0]))):
        CA[i * NB:(i + 1) * NB] = w


def right_features(C, total, b, BF, at):
    for w, c in ((0, 0), (5, W128)):
        p = split3(C[pl.ds(w * total + b, 8, stride=total), :])
        BF[at, :, c:c + W128] = jnp.concatenate([p[q] for _, q in CHUNKS], 0).astype(bf16)


def left_features(CA, b, AF, at):
    p = split3(CA[pl.ds(b, 8, stride=NB), :])
    AF[at] = jnp.concatenate([p[q] for q, _ in CHUNKS], 0).T.astype(bf16)


def pair_matrices(idx_v, hot_a, hot_b):
    for w in range(hot_a.shape[1] // W128):
        at = slice(w * W128, (w + 1) * W128)
        for matrix, row in ((hot_a, 2), (hot_b, 3)):
            which = idx_v[row:row + 1, at]
            blocks = lax.broadcasted_iota(jnp.int32, (matrix.shape[0], W128), 0)
            matrix[:, at] = jnp.where(blocks == which, 1.0, 0.0).astype(bf16)


def whole_kernel(send_list, count, pair_ends, pairs, pos_in, mass, smoothing, energy, level,
                 dens_o, acc_o, own_h, tiles_h,
                 ghost, idx, hot_o, pos, smooth, self_sum, gdens, buf, C, AF, BF, GB, T, RT, R, RS, MM, hot_a, hot_b,
                 gpress, ret, gacc, racc,
                 send_sem, recv_sem, own_sem, tile_sem, s1, r1, s2, r2, s3, r3):
    barrier = greet()
    left = R.at[pl.ds(0, 8 * NB)]
    press, pbuf = smooth, gdens
    hot = R.at[pl.ds(8 * NB, 2 * W128)]
    right = R.at[pl.ds(R.shape[0] // 2, 13 * EXT)]
    lev = level[...]
    scale = jnp.where(lev == 0, 1.0, jnp.where(lev == 1, SHRINK, SHRINK * SHRINK)).astype(f32)
    smooth[...] = smoothing[...] * jnp.broadcast_to(scale, (NB, W128)).T
    for c in range(3):
        pos[c] = pos_in[:, c, :]
    lane = lax.broadcasted_iota(jnp.int32, (1, NB), 1)

    def gather(n, _):
        for g in range(SLOTS):
            t = send_list[0, g, n]
            for c in range(3):
                buf[n, c, g:g + 1, :] = pos[c, pl.ds(t, 1), :]
            buf[n, 3, g:g + 1, :] = mass[pl.ds(t, 1), :]
            buf[n, 4, g:g + 1, :] = smooth[pl.ds(t, 1), :]
            hot[pl.ds(n * SLOTS + g, 1), :] = jnp.where(lane == t, 1.0, 0.0)
        return 0

    hot[pl.ds(GHOSTS, 2 * W128 - GHOSTS), :] = jnp.zeros((2 * W128 - GHOSTS, W128), f32)
    lax.fori_loop(0, NEIGH, gather, 0)
    pl.semaphore_wait(barrier, NEIGH)
    copies = start_all(buf, ghost, send_sem, recv_sem, 1)

    npairs = pairs.shape[2]
    live = lax.broadcasted_iota(jnp.int32, (1, npairs), 1) < count[0]
    idx[...] = jnp.zeros_like(idx)
    idx[2:4, :] = jnp.full((2, idx.shape[1]), EXT, jnp.int32)
    first = pairs[0, 0:1, :]
    second = pairs[0, 1:2, :]
    idx[0:1, :npairs] = first
    idx[1:2, :npairs] = second
    idx[2:3, :npairs] = jnp.where(live, first, NB)
    idx[3:4, :npairs] = jnp.where(live, second, EXT)
    pair_matrices(idx, hot_a, hot_b)
    for i in range(2):
        hot_o[:, i * W128:(i + 1) * W128] = hot[i * W128:(i + 1) * W128].T.astype(bf16)
    slots = R.shape[0] // 16
    R[npairs * 8:slots * 8] = jnp.zeros(((slots - npairs) * 8, W128), f32)
    R[(slots + npairs) * 8:] = jnp.zeros(((slots - npairs) * 8, W128), f32)
    RT[...] = jnp.zeros_like(RT)
    clear_right(right, EXT)
    v = scaled_columns(pos[0], pos[1], pos[2], mass[...], smooth[...])
    fill_right(right, EXT, 0, NB, v)
    fill_left(left, v)

    own_first = (KEEP - 2) * CHUNK
    chunks = npairs // CHUNK

    def features(g):
        for j in range(SELF):
            b = g * SELF + j
            right_features(right, EXT, b, BF, b)
            left_features(left, b, AF, b)

    def product(a, b, j):
        GB[j] = jnp.dot(AF[a], BF[b], preferred_element_type=f32)

    def own_copy(g):
        return pltpu.make_async_copy(T.at[pl.ds(own_first + g * SELF, SELF)], own_h.at[pl.ds(g * SELF, SELF)], own_sem.at[g])

    features(0)
    for j in range(SELF):
        product(j, j, j)
    features(1)

    def own_body(g, _):
        after = jnp.minimum(g + 1, NB // SELF - 1)
        for j in range(SELF):
            part = jnp.zeros((8, W128), f32)
            for r in range(0, W128, 8):
                W, S = tile_math(GB[j, r:r + 8, :W128], GB[j, r:r + 8, W128:])
                T[own_first + g * SELF + j, r:r + 8] = S
                part = part + W
            self_sum[pl.ds(g * SELF + j, 1), :] = jnp.sum(part, axis=0, keepdims=True)
        own_copy(g).start()
        for j in range(SELF):
            product(after * SELF + j, after * SELF + j, j)
        features(jnp.minimum(g + 2, NB // SELF - 1))
        return 0

    lax.fori_loop(0, NB // SELF, own_body, 0)
    for copy in copies:
        copy.wait()

    for n in range(NEIGH):
        fill_right(right, EXT, NB + n * SLOTS, SLOTS, scaled_columns(*[ghost[n, c] for c in range(5)]))

    def ghost_features(i, _):
        for j in range(8):
            right_features(right, EXT, i * 8 + j, BF, i * 8 + j)
        return 0

    lax.fori_loop(NB // 8, EXT // 8, ghost_features, 0)
    for j in range(UNROLL):
        product(pair_ends[0, 0, j], pair_ends[0, 1, j], j)
    lanes = lax.broadcasted_iota(jnp.int32, (8, W128), 1)

    def spill_out(c):
        at = pl.ds(c * CHUNK, CHUNK)
        return pltpu.make_async_copy(T.at[at], tiles_h.at[at], tile_sem.at[c])

    def spill_back(c):
        at = pl.ds(c * CHUNK, CHUNK)
        return pltpu.make_async_copy(tiles_h.at[at], T.at[at], tile_sem.at[chunks - KEEP + c])

    def pair_body(c, u, _):
        k0 = c * CHUNK + u * UNROLL
        slot = lax.rem(c, KEEP) * CHUNK + u * UNROLL
        for j in range(UNROLL):
            here = lanes == lax.rem(k0 + j, W128)
            column = lax.div(k0 + j, W128)
            part = jnp.zeros((8, W128), f32)
            for r in range(0, W128, 8):
                W, S = tile_math(GB[j, r:r + 8, :W128], GB[j, r:r + 8, W128:])
                T[slot + j, r:r + 8] = S
                part = part + W
                RT[column, r:r + 8] = jnp.where(here, jnp.sum(W, axis=1, keepdims=True), RT[column, r:r + 8])
            R[pl.ds(pl.multiple_of((k0 + j) * 8, 8), 8), :] = part
            k = jnp.minimum(k0 + UNROLL + j, npairs - 1)
            product(pair_ends[0, 0, k], pair_ends[0, 1, k], j)
        return 0

    def own_landed(g, _):
        own_copy(g).wait()
        return 0

    def chunk_body(c, _):
        @pl.when(c == KEEP - 2)
        def _():
            lax.fori_loop(0, NB // SELF, own_landed, 0)

        @pl.when(c >= KEEP)
        def _():
            spill_out(c - KEEP).wait()

        lax.fori_loop(0, CHUNK // UNROLL, functools.partial(pair_body, c), 0)

        @pl.when(c < chunks - KEEP)
        def _():
            spill_out(c).start()

        return 0

    lax.fori_loop(0, chunks, chunk_body, 0)

    dot = functools.partial(jnp.dot, preferred_element_type=f32)
    part = R[pl.ds(0, slots, stride=8), :]
    for i in range(1, 8):
        part = part + R[pl.ds(i, slots, stride=8), :]
    hi, lo = hilo(part)
    away = dot(hot_b[NB:], hi) + dot(hot_b[NB:], lo)
    for n in range(NEIGH):
        gdens[n] = away[n * SLOTS:(n + 1) * SLOTS] * (4.0 * NORM) / ghost[n, 3]
    copies = start_all(gdens, ret, s1, r1, -1)
    rows = jnp.zeros((W128, NB), f32)
    for w in range(RT.shape[0]):
        for p in hilo(RT[w]):
            rows = rows + lax.dot_general(p, hot_a[:, w * W128:(w + 1) * W128], (((1,), (1,)), ((), ())),
                                          preferred_element_type=f32)
    home = dot(hot_b[:NB], hi) + dot(hot_b[:NB], lo)
    mine = (home + rows.T + self_sum[...]) * (4.0 * NORM) / mass[...]

    def weights(at, rows, x, y, z, m, p):
        k = inverse_cube_root(m)
        w = k * k
        pw = p * w
        for i, v in enumerate((w, w * x, w * y, w * z, pw, pw * x, pw * y, pw * z)):
            C[i * EXT + at:i * EXT + at + rows] = v

    def columns(i, _):
        for j in range(4):
            b = i * 4 + j
            v = C[pl.ds(b, 8, stride=EXT), :]
            hi = v.astype(bf16).astype(f32)
            mm = jnp.concatenate([hi, v - hi], 0).astype(bf16)
            MM[b, :, :W128] = mm
            MM[b, :, W128:] = mm
        return 0

    for copy in copies:
        copy.wait()
    dens = mine + split_dot(hot_o[:, :GHOSTS], ret[...].reshape(GHOSTS, W128))
    dens_o[...] = dens
    press[...] = GAMMA_LESS * energy[...] / dens

    def gather_press(n, _):
        for g in range(SLOTS):
            pbuf[n, g:g + 1, :] = press[pl.ds(send_list[0, g, n], 1), :]
        return 0

    lax.fori_loop(0, NEIGH, gather_press, 0)
    copies = start_all(pbuf, gpress, s2, r2, 1)

    weights(0, NB, pos[0], pos[1], pos[2], mass[...], press[...])
    lax.fori_loop(0, NB // 4, columns, 0)

    def to_b(k, hi, lo):
        return jnp.dot(MM[pair_ends[0, 0, k]], jnp.concatenate([hi, lo], 0), preferred_element_type=f32)

    def to_a(k, hi, lo):
        return lax.dot_general(MM[pair_ends[0, 1, k]], jnp.concatenate([hi, lo], 1), (((1,), (1,)), ((), ())),
                               preferred_element_type=f32)

    def put(ref, k, v):
        ref[pl.ds(pl.multiple_of(k * 8, 8), 8), :] = v[:8] + v[8:]

    def own_sums(u, _):
        out = []
        for j in range(16):
            a = u * 16 + j
            hi, lo = hilo(T[own_first + a])
            out.append((a, jnp.dot(MM[a], jnp.concatenate([hi, lo], 0), preferred_element_type=f32)))
        for a, v in out:
            put(RS, a, v)
        return 0

    def pair_sums(do_a, do_b, c, u, _):
        out = []
        for j in range(FORCE_UNROLL):
            k = c * CHUNK + u * FORCE_UNROLL + j
            hi, lo = hilo(T[lax.rem(c, KEEP) * CHUNK + u * FORCE_UNROLL + j])
            if do_b:
                out.append((slots + k, to_b(k, hi, lo)))
            if do_a:
                out.append((k, to_a(k, hi, lo)))
        for k, v in out:
            put(R, k, v)
        return 0

    def chunk_sums(do_a, do_b, c):
        lax.fori_loop(0, CHUNK // FORCE_UNROLL, functools.partial(pair_sums, do_a, do_b, c), 0)

    def early(do_a, do_b, i, _):
        chunk_sums(do_a, do_b, KEEP + i)
        return 0

    lax.fori_loop(0, chunks - KEEP, functools.partial(early, False, True), 0)
    for copy in copies:
        copy.wait()
    for n in range(NEIGH):
        weights(NB + n * SLOTS, SLOTS, *[ghost[n, c] for c in range(4)], gpress[n])
    lax.fori_loop(NB // 4, EXT // 4, columns, 0)
    lax.fori_loop(0, chunks - KEEP, functools.partial(early, True, False), 0)
    for c in range(chunks - KEEP):
        spill_back(c).start()
    own_back = pltpu.make_async_copy(own_h, T.at[pl.ds(own_first, NB)], tile_sem.at[2 * (chunks - KEEP)])

    def rest(i, _):
        c = lax.rem(chunks - KEEP + i, KEEP)

        @pl.when(i == 2)
        def _():
            own_back.start()

        @pl.when(i >= 2)
        def _():
            spill_back(c).wait()

        chunk_sums(True, True, c)
        return 0

    lax.fori_loop(0, KEEP, rest, 0)
    own_back.wait()
    lax.fori_loop(0, NB // 16, own_sums, 0)

    def block_sums(halves):
        A = []
        for c in range(0, 8, 2):
            total = None
            for half, matrix in halves:
                v = [R[pl.ds(half * slots * 8 + c + i, slots, stride=8), :] for i in range(2)]
                hi, lo = hilo(jnp.concatenate(v, 1))
                term = dot(matrix, hi) + dot(matrix, lo)
                total = term if total is None else total + term
            A += [total[:, :W128], total[:, W128:]]
        return A

    scale = -20.0 * NORM

    def final(p, m, spot, A):
        k = inverse_cube_root(m)
        k2 = k * k
        own = p * A[0] + A[4]
        return [(p * A[c + 1] + A[c + 5] - v * own) * (scale * (k2 * k2 * k)) for c, v in enumerate(spot)]

    A = block_sums([(1, hot_b[NB:])])
    for n in range(NEIGH):
        r = slice(n * SLOTS, (n + 1) * SLOTS)
        for c, v in enumerate(final(gpress[n], ghost[n, 3], [ghost[n, c] for c in range(3)], [x[r] for x in A])):
            gacc[n, c] = v
    copies = start_all(gacc, racc, s3, r3, -1)
    A = [x + RS[pl.ds(c, NB, stride=8), :] for c, x in enumerate(block_sums([(0, hot_a[...]), (1, hot_b[:NB])]))]
    mine = final(press[...], mass[...], [pos[c] for c in range(3)], A)
    for copy in copies:
        copy.wait()
    for c in range(3):
        acc_o[:, c, :] = mine[c] + split_dot(hot_o[:, :GHOSTS], racc[:, c].reshape(GHOSTS, W128))


V = pl.BlockSpec(memory_space=pltpu.VMEM)
SM = pl.BlockSpec(memory_space=pltpu.SMEM)
sds = jax.ShapeDtypeStruct


def run_whole(send_list, pair_count, pair_list, pos, mass, smoothing, energy, level):
    D = pltpu.SemaphoreType.DMA((NEIGH,))
    vm = pltpu.VMEM
    A = pl.BlockSpec(memory_space=pl.ANY)
    pairs = pair_list.shape[2]
    slots = pairs + (-pairs) % (2 * W128)
    one = vm((NB, W128), f32)
    eight = vm((NEIGH, SLOTS, W128), f32)
    three = vm((NEIGH, 3, SLOTS, W128), f32)
    five = vm((NEIGH, 5, SLOTS, W128), f32)
    return pl.pallas_call(
        whole_kernel,
        out_shape=[sds((NB, W128), f32), sds((NB, 3, W128), f32), sds((NB, W128, W128), f32),
                   sds((pairs - KEEP * CHUNK, W128, W128), f32)],
        in_specs=[SM, SM, SM, V, V, V, V, V, V], out_specs=[V, V, A, A],
        scratch_shapes=[
            five, vm((4, slots), jnp.int32), vm((NB, 2 * W128), bf16), vm((3, NB, W128), f32), one, one, eight, five,
            vm((8 * EXT, W128), f32), vm((NB, W128, 64), bf16),
            vm((EXT, 64, 2 * W128), bf16), vm((UNROLL, W128, 2 * W128), f32), vm((KEEP * CHUNK, W128, W128), f32),
            vm((slots // W128, W128, W128), f32), vm((2 * slots * 8, W128), f32), vm((NB * 8, W128), f32),
            vm((EXT, 16, 2 * W128), bf16), vm((NB, slots), bf16), vm((EXT, slots), bf16),
            eight, eight, three, three,
            D, D, pltpu.SemaphoreType.DMA((NB // SELF,)), pltpu.SemaphoreType.DMA((2 * (pairs // CHUNK - KEEP) + 1,)), D, D, D, D, D, D],
        compiler_params=pltpu.CompilerParams(collective_id=0, has_side_effects=True, vmem_limit_bytes=VMEM),
        name="whole")(send_list, pair_count, pair_list, pair_list, pos, mass, smoothing, energy, level)


def leave_kernel(dens, acc, dens_o, acc_o):
    dens_o[...] = dens[...]
    acc_o[...] = acc[...]


def leave(dens, acc):
    return pl.pallas_call(
        leave_kernel, out_shape=[sds(dens.shape, f32), sds(acc.shape, f32)], in_specs=[V, V], out_specs=[V, V],
        compiler_params=pltpu.CompilerParams(vmem_limit_bytes=VMEM), name="leave")(dens, acc)


def per_device(positions, masses, smoothing, energy, level_ids, send_list, pair_list, pair_count):
    mass = masses.reshape(NB, W128)
    density, accel, _, _ = run_whole(
        send_list.transpose(0, 2, 1), pair_count, pair_list, positions.reshape(3, NB, W128).transpose(1, 0, 2), mass,
        smoothing.reshape(NB, W128), energy.reshape(NB, W128), level_ids.reshape(1, NB))
    density, accel = leave(density, accel)
    return density.reshape(NB * W128), accel.transpose(1, 0, 2).reshape(3, NB * W128)


def solution(mesh):
    both = ("patch", "bulk")
    placed = (P(None, both), P(both), P(both), P(both), P(both), P(both, None, None), P(both, None, None), P(both))
    return jax.shard_map(per_device, mesh=mesh, in_specs=placed, out_specs=(P(both), P(None, both)), check_vma=False)
```

```python
import functools
import math

import jax
import jax.numpy as jnp
from jax import lax
from jax.experimental import pallas as pl
from jax.experimental.pallas import tpu as pltpu
from jax.sharding import PartitionSpec as P

MESH = pl.DeviceIdType.MESH
f32 = jnp.float32
bf16 = jnp.bfloat16
NORM = 21.0 / (2.0 * math.pi)
GAMMA_LESS = 2.0 / 3.0
SHRINK = 0.8
NB = 128
W128 = 128
NEIGH = 20
SLOTS = 8
GHOSTS = NEIGH * SLOTS
EXT = NB + GHOSTS
CHUNKS = [(0, 0), (0, 1), (1, 0), (1, 1), (0, 2), (2, 0), (1, 2), (2, 1)]
UNROLL = 28
CHUNK = 84
FORCE_UNROLL = 42
KEEP = 5
SELF = 16
VMEM = 63 * 2**20


def neighbour_steps():
    return [
        (step_patch, step_bulk)
        for step_patch in (-1, 0, 1)
        for step_bulk in range(-3, 4)
        if (step_patch, step_bulk) != (0, 0)
    ]


def place(offset):
    rows, columns = lax.axis_size("patch"), lax.axis_size("bulk")
    count = rows * columns
    me = lax.axis_index("patch") * columns + lax.axis_index("bulk")
    other = lax.rem(me + (offset + count), count)
    return (lax.div(other, columns), lax.rem(other, columns))


def offsets():
    columns = lax.axis_size("bulk")
    return [u * columns + v for u, v in neighbour_steps()]


def greet():
    barrier = pltpu.get_barrier_semaphore()
    for o in offsets():
        pl.semaphore_signal(barrier, inc=1, device_id=place(o), device_id_type=MESH)
    return barrier


def start_all(src, dst, send_sem, recv_sem, sign):
    copies = []
    for n, o in enumerate(offsets()):
        copy = pltpu.make_async_remote_copy(
            src_ref=src.at[n], dst_ref=dst.at[n], send_sem=send_sem.at[n], recv_sem=recv_sem.at[n],
            device_id=place(sign * o), device_id_type=MESH)
        copy.start()
        copies.append(copy)
    return copies


def split3(v):
    a = v.astype(bf16).astype(f32)
    r = v - a
    b = r.astype(bf16).astype(f32)
    return a, b, r - b


def hilo(v):
    hi = v.astype(bf16)
    return hi, (v - hi.astype(f32)).astype(bf16)


def split_dot(hot, v):
    a, b, c = [p.astype(bf16) for p in split3(v)]
    dot = functools.partial(jnp.dot, preferred_element_type=f32)
    return dot(hot, a) + (dot(hot, b) + dot(hot, c))


def inverse_cube_root(m):
    k = jnp.exp(jnp.log(m) * (-1.0 / 3.0))
    return k * (4.0 - m * (k * k * k)) * (1.0 / 3.0)


def tile_math(r2, hs):
    r2 = jnp.maximum(r2, 1e-30)
    s = pl.reciprocal(hs, approx=True)
    q = r2 * lax.rsqrt(r2) * s
    t = jnp.maximum(1.0 - q, 0.0)
    st = s * t
    c = st * st * st
    return c * (t * (q + 0.25)), c * (s * s)


def scaled_columns(x, y, z, m, h):
    k = inverse_cube_root(m)
    k2 = k * k
    return x * k2, y * k2, z * k2, k2, (x * x + y * y + z * z) * k2, (0.5 * h) * k, k


def fill_right(C, total, at, rows, v):
    for i, c in ((0, 0), (1, 1), (2, 2), (3, 3), (4, 4), (10, 5), (11, 6)):
        C[i * total + at:i * total + at + rows] = v[c]


def clear_right(C, total):
    zero = jnp.zeros((total, W128), f32)
    for i in (5, 6, 7, 8, 9, 12):
        C[i * total:(i + 1) * total] = zero


def fill_left(CA, v):
    for i, w in enumerate((-2.0 * v[0], -2.0 * v[1], -2.0 * v[2], v[4], v[3], v[6], v[5], jnp.zeros_like(v[0]))):
        CA[i * NB:(i + 1) * NB] = w


def right_features(C, total, b, BF, at):
    for w, c in ((0, 0), (5, W128)):
        p = split3(C[pl.ds(w * total + b, 8, stride=total), :])
        BF[at, :, c:c + W128] = jnp.concatenate([p[q] for _, q in CHUNKS], 0).astype(bf16)


def left_features(CA, b, AF, at):
    p = split3(CA[pl.ds(b, 8, stride=NB), :])
    AF[at] = jnp.concatenate([p[q] for q, _ in CHUNKS], 0).T.astype(bf16)


def pair_matrices(idx_v, hot_a, hot_b):
    for w in range(hot_a.shape[1] // W128):
        at = slice(w * W128, (w + 1) * W128)
        for matrix, row in ((hot_a, 2), (hot_b, 3)):
            which = idx_v[row:row + 1, at]
            blocks = lax.broadcasted_iota(jnp.int32, (matrix.shape[0], W128), 0)
            matrix[:, at] = jnp.where(blocks == which, 1.0, 0.0).astype(bf16)


def whole_kernel(send_list, count, pair_ends, pairs, pos_in, mass, smoothing, energy, level,
                 dens_o, acc_o, own_h, tiles_h,
                 ghost, idx, hot_o, pos, smooth, self_sum, gdens, buf, C, AF, BF, GB, T, RT, R, RS, MM, hot_a, hot_b,
                 gpress, ret, gacc, racc,
                 send_sem, recv_sem, own_sem, tile_sem, s1, r1, s2, r2, s3, r3):
    barrier = greet()
    left = R.at[pl.ds(0, 8 * NB)]
    press, pbuf = smooth, gdens
    hot = R.at[pl.ds(8 * NB, 2 * W128)]
    right = R.at[pl.ds(R.shape[0] // 2, 13 * EXT)]
    lev = level[...]
    scale = jnp.where(lev == 0, 1.0, jnp.where(lev == 1, SHRINK, SHRINK * SHRINK)).astype(f32)
    smooth[...] = smoothing[...] * jnp.broadcast_to(scale, (NB, W128)).T
    for c in range(3):
        pos[c] = pos_in[:, c, :]
    lane = lax.broadcasted_iota(jnp.int32, (1, NB), 1)

    def gather(n, _):
        for g in range(SLOTS):
            t = send_list[0, g, n]
            for c in range(3):
                buf[n, c, g:g + 1, :] = pos[c, pl.ds(t, 1), :]
            buf[n, 3, g:g + 1, :] = mass[pl.ds(t, 1), :]
            buf[n, 4, g:g + 1, :] = smooth[pl.ds(t, 1), :]
            hot[pl.ds(n * SLOTS + g, 1), :] = jnp.where(lane == t, 1.0, 0.0)
        return 0

    hot[pl.ds(GHOSTS, 2 * W128 - GHOSTS), :] = jnp.zeros((2 * W128 - GHOSTS, W128), f32)
    lax.fori_loop(0, NEIGH, gather, 0)
    pl.semaphore_wait(barrier, NEIGH)
    copies = start_all(buf, ghost, send_sem, recv_sem, 1)

    npairs = pairs.shape[2]
    live = lax.broadcasted_iota(jnp.int32, (1, npairs), 1) < count[0]
    idx[...] = jnp.zeros_like(idx)
    idx[2:4, :] = jnp.full((2, idx.shape[1]), EXT, jnp.int32)
    first = pairs[0, 0:1, :]
    second = pairs[0, 1:2, :]
    idx[0:1, :npairs] = first
    idx[1:2, :npairs] = second
    idx[2:3, :npairs] = jnp.where(live, first, NB)
    idx[3:4, :npairs] = jnp.where(live, second, EXT)
    pair_matrices(idx, hot_a, hot_b)
    for i in range(2):
        hot_o[:, i * W128:(i + 1) * W128] = hot[i * W128:(i + 1) * W128].T.astype(bf16)
    slots = R.shape[0] // 16
    R[npairs * 8:slots * 8] = jnp.zeros(((slots - npairs) * 8, W128), f32)
    R[(slots + npairs) * 8:] = jnp.zeros(((slots - npairs) * 8, W128), f32)
    RT[...] = jnp.zeros_like(RT)
    clear_right(right, EXT)
    v = scaled_columns(pos[0], pos[1], pos[2], mass[...], smooth[...])
    fill_right(right, EXT, 0, NB, v)
    fill_left(left, v)

    own_first = (KEEP - 2) * CHUNK
    chunks = npairs // CHUNK

    def features(g):
        for j in range(SELF):
            b = g * SELF + j
            right_features(right, EXT, b, BF, b)
            left_features(left, b, AF, b)

    def product(a, b, j):
        GB[j] = jnp.dot(AF[a], BF[b], preferred_element_type=f32)

    def own_copy(g):
        return pltpu.make_async_copy(T.at[pl.ds(own_first + g * SELF, SELF)], own_h.at[pl.ds(g * SELF, SELF)], own_sem.at[g])

    features(0)
    for j in range(SELF):
        product(j, j, j)
    features(1)

    def own_body(g, _):
        after = jnp.minimum(g + 1, NB // SELF - 1)
        for j in range(SELF):
            part = jnp.zeros((8, W128), f32)
            for r in range(0, W128, 8):
                W, S = tile_math(GB[j, r:r + 8, :W128], GB[j, r:r + 8, W128:])
                T[own_first + g * SELF + j, r:r + 8] = S
                part = part + W
            self_sum[pl.ds(g * SELF + j, 1), :] = jnp.sum(part, axis=0, keepdims=True)
        own_copy(g).start()
        for j in range(SELF):
            product(after * SELF + j, after * SELF + j, j)
        features(jnp.minimum(g + 2, NB // SELF - 1))
        return 0

    lax.fori_loop(0, NB // SELF, own_body, 0)
    for copy in copies:
        copy.wait()

    for n in range(NEIGH):
        fill_right(right, EXT, NB + n * SLOTS, SLOTS, scaled_columns(*[ghost[n, c] for c in range(5)]))

    def ghost_features(i, _):
        for j in range(8):
            right_features(right, EXT, i * 8 + j, BF, i * 8 + j)
        return 0

    lax.fori_loop(NB // 8, EXT // 8, ghost_features, 0)
    for j in range(UNROLL):
        product(pair_ends[0, 0, j], pair_ends[0, 1, j], j)
    lanes = lax.broadcasted_iota(jnp.int32, (8, W128), 1)

    def spill_out(c):
        at = pl.ds(c * CHUNK, CHUNK)
        return pltpu.make_async_copy(T.at[at], tiles_h.at[at], tile_sem.at[c])

    def spill_back(c, place):
        return pltpu.make_async_copy(tiles_h.at[pl.ds(c * CHUNK, CHUNK)], T.at[pl.ds(place * CHUNK, CHUNK)],
                                     tile_sem.at[chunks - KEEP + c])

    def pair_body(c, u, _):
        k0 = c * CHUNK + u * UNROLL
        slot = lax.rem(c, KEEP) * CHUNK + u * UNROLL
        for j in range(UNROLL):
            here = lanes == lax.rem(k0 + j, W128)
            column = lax.div(k0 + j, W128)
            part = jnp.zeros((8, W128), f32)
            for r in range(0, W128, 8):
                W, S = tile_math(GB[j, r:r + 8, :W128], GB[j, r:r + 8, W128:])
                T[slot + j, r:r + 8] = S
                part = part + W
                RT[column, r:r + 8] = jnp.where(here, jnp.sum(W, axis=1, keepdims=True), RT[column, r:r + 8])
            R[pl.ds(pl.multiple_of((k0 + j) * 8, 8), 8), :] = part
            k = jnp.minimum(k0 + UNROLL + j, npairs - 1)
            product(pair_ends[0, 0, k], pair_ends[0, 1, k], j)
        return 0

    def own_landed(g, _):
        own_copy(g).wait()
        return 0

    def chunk_body(c, _):
        @pl.when(c == KEEP - 2)
        def _():
            lax.fori_loop(0, NB // SELF, own_landed, 0)

        @pl.when(c >= KEEP)
        def _():
            spill_out(c - KEEP).wait()

        lax.fori_loop(0, CHUNK // UNROLL, functools.partial(pair_body, c), 0)

        @pl.when(c < chunks - KEEP)
        def _():
            spill_out(c).start()

        return 0

    lax.fori_loop(0, chunks, chunk_body, 0)

    dot = functools.partial(jnp.dot, preferred_element_type=f32)
    part = R[pl.ds(0, slots, stride=8), :]
    for i in range(1, 8):
        part = part + R[pl.ds(i, slots, stride=8), :]
    hi, lo = hilo(part)
    away = dot(hot_b[NB:], hi) + dot(hot_b[NB:], lo)
    for n in range(NEIGH):
        gdens[n] = away[n * SLOTS:(n + 1) * SLOTS] * (4.0 * NORM) / ghost[n, 3]
    copies = start_all(gdens, ret, s1, r1, -1)
    rows = jnp.zeros((W128, NB), f32)
    for w in range(RT.shape[0]):
        for p in hilo(RT[w]):
            rows = rows + lax.dot_general(p, hot_a[:, w * W128:(w + 1) * W128], (((1,), (1,)), ((), ())),
                                          preferred_element_type=f32)
    home = dot(hot_b[:NB], hi) + dot(hot_b[:NB], lo)
    mine = (home + rows.T + self_sum[...]) * (4.0 * NORM) / mass[...]

    def weights(at, rows, x, y, z, m, p):
        k = inverse_cube_root(m)
        w = k * k
        pw = p * w
        for i, v in enumerate((w, w * x, w * y, w * z, pw, pw * x, pw * y, pw * z)):
            C[i * EXT + at:i * EXT + at + rows] = v

    def columns(i, _):
        for j in range(4):
            b = i * 4 + j
            v = C[pl.ds(b, 8, stride=EXT), :]
            hi = v.astype(bf16).astype(f32)
            mm = jnp.concatenate([hi, v - hi], 0).astype(bf16)
            MM[b, :, :W128] = mm
            MM[b, :, W128:] = mm
        return 0

    for copy in copies:
        copy.wait()
    dens = mine + split_dot(hot_o[:, :GHOSTS], ret[...].reshape(GHOSTS, W128))
    dens_o[...] = dens
    press[...] = GAMMA_LESS * energy[...] / dens

    def gather_press(n, _):
        for g in range(SLOTS):
            pbuf[n, g:g + 1, :] = press[pl.ds(send_list[0, g, n], 1), :]
        return 0

    lax.fori_loop(0, NEIGH, gather_press, 0)
    copies = start_all(pbuf, gpress, s2, r2, 1)

    weights(0, NB, pos[0], pos[1], pos[2], mass[...], press[...])
    lax.fori_loop(0, NB // 4, columns, 0)

    def to_b(k, hi, lo):
        return jnp.dot(MM[pair_ends[0, 0, k]], jnp.concatenate([hi, lo], 0), preferred_element_type=f32)

    def to_a(k, hi, lo):
        return lax.dot_general(MM[pair_ends[0, 1, k]], jnp.concatenate([hi, lo], 1), (((1,), (1,)), ((), ())),
                               preferred_element_type=f32)

    def put(ref, k, v):
        ref[pl.ds(pl.multiple_of(k * 8, 8), 8), :] = v[:8] + v[8:]

    def own_sums(u, _):
        out = []
        for j in range(16):
            a = u * 16 + j
            hi, lo = hilo(T[own_first + a])
            out.append((a, jnp.dot(MM[a], jnp.concatenate([hi, lo], 0), preferred_element_type=f32)))
        for a, v in out:
            put(RS, a, v)
        return 0

    def pair_sums(do_a, do_b, c, place, u, _):
        out = []
        for j in range(FORCE_UNROLL):
            k = c * CHUNK + u * FORCE_UNROLL + j
            hi, lo = hilo(T[place * CHUNK + u * FORCE_UNROLL + j])
            if do_b:
                out.append((slots + k, to_b(k, hi, lo)))
            if do_a:
                out.append((k, to_a(k, hi, lo)))
        for k, v in out:
            put(R, k, v)
        return 0

    def chunk_sums(do_a, do_b, c, place):
        lax.fori_loop(0, CHUNK // FORCE_UNROLL, functools.partial(pair_sums, do_a, do_b, c, place), 0)

    def early(do_a, do_b, i, _):
        chunk_sums(do_a, do_b, KEEP + i, i)
        return 0

    lax.fori_loop(0, chunks - KEEP, functools.partial(early, False, True), 0)
    for copy in copies:
        copy.wait()
    for n in range(NEIGH):
        weights(NB + n * SLOTS, SLOTS, *[ghost[n, c] for c in range(4)], gpress[n])
    lax.fori_loop(NB // 4, EXT // 4, columns, 0)
    own_back = pltpu.make_async_copy(own_h, T.at[pl.ds(own_first, NB)], tile_sem.at[2 * (chunks - KEEP)])

    def rest(i, _):
        c = lax.rem(chunks - KEEP + i, KEEP)
        place = KEEP - 2 + lax.rem(i, 2)

        @pl.when(i >= 2)
        def _():
            spill_back(c, place).wait()

        chunk_sums(True, True, c, place)

        @pl.when(i + 2 < KEEP)
        def _():
            spill_back(lax.rem(chunks - KEEP + i + 2, KEEP), place).start()

        return 0

    lax.fori_loop(0, KEEP, rest, 0)
    own_back.start()

    def block_sums(halves):
        A = []
        for c in range(0, 8, 2):
            total = None
            for half, matrix in halves:
                v = [R[pl.ds(half * slots * 8 + c + i, slots, stride=8), :] for i in range(2)]
                hi, lo = hilo(jnp.concatenate(v, 1))
                term = dot(matrix, hi) + dot(matrix, lo)
                total = term if total is None else total + term
            A += [total[:, :W128], total[:, W128:]]
        return A

    scale = -20.0 * NORM

    def final(p, m, spot, A):
        k = inverse_cube_root(m)
        k2 = k * k
        own = p * A[0] + A[4]
        return [(p * A[c + 1] + A[c + 5] - v * own) * (scale * (k2 * k2 * k)) for c, v in enumerate(spot)]

    A = block_sums([(1, hot_b[NB:])])
    for n in range(NEIGH):
        r = slice(n * SLOTS, (n + 1) * SLOTS)
        for c, v in enumerate(final(gpress[n], ghost[n, 3], [ghost[n, c] for c in range(3)], [x[r] for x in A])):
            gacc[n, c] = v
    copies = start_all(gacc, racc, s3, r3, -1)
    lax.fori_loop(0, chunks - KEEP, functools.partial(early, True, False), 0)
    own_back.wait()
    lax.fori_loop(0, NB // 16, own_sums, 0)
    A = [x + RS[pl.ds(c, NB, stride=8), :] for c, x in enumerate(block_sums([(0, hot_a[...]), (1, hot_b[:NB])]))]
    mine = final(press[...], mass[...], [pos[c] for c in range(3)], A)
    for copy in copies:
        copy.wait()
    for c in range(3):
        acc_o[:, c, :] = mine[c] + split_dot(hot_o[:, :GHOSTS], racc[:, c].reshape(GHOSTS, W128))


V = pl.BlockSpec(memory_space=pltpu.VMEM)
SM = pl.BlockSpec(memory_space=pltpu.SMEM)
sds = jax.ShapeDtypeStruct


def run_whole(send_list, pair_count, pair_list, pos, mass, smoothing, energy, level):
    D = pltpu.SemaphoreType.DMA((NEIGH,))
    vm = pltpu.VMEM
    A = pl.BlockSpec(memory_space=pl.ANY)
    pairs = pair_list.shape[2]
    slots = pairs + (-pairs) % (2 * W128)
    one = vm((NB, W128), f32)
    eight = vm((NEIGH, SLOTS, W128), f32)
    three = vm((NEIGH, 3, SLOTS, W128), f32)
    five = vm((NEIGH, 5, SLOTS, W128), f32)
    return pl.pallas_call(
        whole_kernel,
        out_shape=[sds((NB, W128), f32), sds((NB, 3, W128), f32), sds((NB, W128, W128), f32),
                   sds((pairs - KEEP * CHUNK, W128, W128), f32)],
        in_specs=[SM, SM, SM, V, V, V, V, V, V], out_specs=[V, V, A, A],
        scratch_shapes=[
            five, vm((4, slots), jnp.int32), vm((NB, 2 * W128), bf16), vm((3, NB, W128), f32), one, one, eight, five,
            vm((8 * EXT, W128), f32), vm((NB, W128, 64), bf16),
            vm((EXT, 64, 2 * W128), bf16), vm((UNROLL, W128, 2 * W128), f32), vm((KEEP * CHUNK, W128, W128), f32),
            vm((slots // W128, W128, W128), f32), vm((2 * slots * 8, W128), f32), vm((NB * 8, W128), f32),
            vm((EXT, 16, 2 * W128), bf16), vm((NB, slots), bf16), vm((EXT, slots), bf16),
            eight, eight, three, three,
            D, D, pltpu.SemaphoreType.DMA((NB // SELF,)), pltpu.SemaphoreType.DMA((2 * (pairs // CHUNK - KEEP) + 1,)), D, D, D, D, D, D],
        compiler_params=pltpu.CompilerParams(collective_id=0, has_side_effects=True, vmem_limit_bytes=VMEM),
        name="whole")(send_list, pair_count, pair_list, pair_list, pos, mass, smoothing, energy, level)


def leave_kernel(dens, acc, dens_o, acc_o):
    dens_o[...] = dens[...]
    acc_o[...] = acc[...]


def leave(dens, acc):
    return pl.pallas_call(
        leave_kernel, out_shape=[sds(dens.shape, f32), sds(acc.shape, f32)], in_specs=[V, V], out_specs=[V, V],
        compiler_params=pltpu.CompilerParams(vmem_limit_bytes=VMEM), name="leave")(dens, acc)


def per_device(positions, masses, smoothing, energy, level_ids, send_list, pair_list, pair_count):
    mass = masses.reshape(NB, W128)
    density, accel, _, _ = run_whole(
        send_list.transpose(0, 2, 1), pair_count, pair_list, positions.reshape(3, NB, W128).transpose(1, 0, 2), mass,
        smoothing.reshape(NB, W128), energy.reshape(NB, W128), level_ids.reshape(1, NB))
    density, accel = leave(density, accel)
    return density.reshape(NB * W128), accel.transpose(1, 0, 2).reshape(3, NB * W128)


def solution(mesh):
    both = ("patch", "bulk")
    placed = (P(None, both), P(both), P(both), P(both), P(both), P(both, None, None), P(both, None, None), P(both))
    return jax.shard_map(per_device, mesh=mesh, in_specs=placed, out_specs=(P(both), P(None, both)), check_vma=False)
```

```python
import functools
import math

import jax
import jax.numpy as jnp
from jax import lax
from jax.experimental import pallas as pl
from jax.experimental.pallas import tpu as pltpu
from jax.sharding import PartitionSpec as P

MESH = pl.DeviceIdType.MESH
f32 = jnp.float32
bf16 = jnp.bfloat16
NORM = 21.0 / (2.0 * math.pi)
GAMMA_LESS = 2.0 / 3.0
SHRINK = 0.8
NB = 128
W128 = 128
NEIGH = 20
SLOTS = 8
GHOSTS = NEIGH * SLOTS
EXT = NB + GHOSTS
CHUNKS = [(0, 0), (0, 1), (1, 0), (1, 1), (0, 2), (2, 0), (1, 2), (2, 1)]
UNROLL = 42
CHUNK = 84
FORCE_UNROLL = 42
KEEP = 5
SELF = 16
VMEM = 63 * 2**20


def neighbour_steps():
    return [
        (step_patch, step_bulk)
        for step_patch in (-1, 0, 1)
        for step_bulk in range(-3, 4)
        if (step_patch, step_bulk) != (0, 0)
    ]


def place(offset):
    rows, columns = lax.axis_size("patch"), lax.axis_size("bulk")
    count = rows * columns
    me = lax.axis_index("patch") * columns + lax.axis_index("bulk")
    other = lax.rem(me + (offset + count), count)
    return (lax.div(other, columns), lax.rem(other, columns))


def offsets():
    columns = lax.axis_size("bulk")
    return [u * columns + v for u, v in neighbour_steps()]


def greet():
    barrier = pltpu.get_barrier_semaphore()
    for o in offsets():
        pl.semaphore_signal(barrier, inc=1, device_id=place(o), device_id_type=MESH)
    return barrier


def start_all(src, dst, send_sem, recv_sem, sign):
    copies = []
    for n, o in enumerate(offsets()):
        copy = pltpu.make_async_remote_copy(
            src_ref=src.at[n], dst_ref=dst.at[n], send_sem=send_sem.at[n], recv_sem=recv_sem.at[n],
            device_id=place(sign * o), device_id_type=MESH)
        copy.start()
        copies.append(copy)
    return copies


def split3(v):
    a = v.astype(bf16).astype(f32)
    r = v - a
    b = r.astype(bf16).astype(f32)
    return a, b, r - b


def hilo(v):
    hi = v.astype(bf16)
    return hi, (v - hi.astype(f32)).astype(bf16)


def split_dot(hot, v):
    a, b, c = [p.astype(bf16) for p in split3(v)]
    dot = functools.partial(jnp.dot, preferred_element_type=f32)
    return dot(hot, a) + (dot(hot, b) + dot(hot, c))


def inverse_cube_root(m):
    k = jnp.exp(jnp.log(m) * (-1.0 / 3.0))
    return k * (4.0 - m * (k * k * k)) * (1.0 / 3.0)


def tile_math(r2, hs):
    r2 = jnp.maximum(r2, 1e-30)
    s = pl.reciprocal(hs, approx=True)
    q = r2 * lax.rsqrt(r2) * s
    t = jnp.maximum(1.0 - q, 0.0)
    st = s * t
    c = st * st * st
    return c * (t * (q + 0.25)), c * (s * s)


def scaled_columns(x, y, z, m, h):
    k = inverse_cube_root(m)
    k2 = k * k
    return x * k2, y * k2, z * k2, k2, (x * x + y * y + z * z) * k2, (0.5 * h) * k, k


def fill_right(C, total, at, rows, v):
    for i, c in ((0, 0), (1, 1), (2, 2), (3, 3), (4, 4), (10, 5), (11, 6)):
        C[i * total + at:i * total + at + rows] = v[c]


def clear_right(C, total):
    zero = jnp.zeros((total, W128), f32)
    for i in (5, 6, 7, 8, 9, 12):
        C[i * total:(i + 1) * total] = zero


def fill_left(CA, v):
    for i, w in enumerate((-2.0 * v[0], -2.0 * v[1], -2.0 * v[2], v[4], v[3], v[6], v[5], jnp.zeros_like(v[0]))):
        CA[i * NB:(i + 1) * NB] = w


def right_features(C, total, b, BF, at):
    for w, c in ((0, 0), (5, W128)):
        p = split3(C[pl.ds(w * total + b, 8, stride=total), :])
        BF[at, :, c:c + W128] = jnp.concatenate([p[q] for _, q in CHUNKS], 0).astype(bf16)


def left_features(CA, b, AF, at):
    p = split3(CA[pl.ds(b, 8, stride=NB), :])
    AF[at] = jnp.concatenate([p[q] for q, _ in CHUNKS], 0).T.astype(bf16)


def pair_matrices(idx_v, hot_a, hot_b):
    for w in range(hot_a.shape[1] // W128):
        at = slice(w * W128, (w + 1) * W128)
        for matrix, row in ((hot_a, 2), (hot_b, 3)):
            which = idx_v[row:row + 1, at]
            blocks = lax.broadcasted_iota(jnp.int32, (matrix.shape[0], W128), 0)
            matrix[:, at] = jnp.where(blocks == which, 1.0, 0.0).astype(bf16)


def whole_kernel(send_list, count, pair_ends, pairs, pos_in, mass, smoothing, energy, level,
                 dens_o, acc_o, own_h, tiles_h,
                 ghost, idx, hot_o, pos, smooth, self_sum, gdens, buf, C, AF, BF, GB, T, RT, R, RS, MM, hot_a, hot_b,
                 gpress, ret, gacc, racc,
                 send_sem, recv_sem, own_sem, tile_sem, s1, r1, s2, r2, s3, r3):
    barrier = greet()
    left = R.at[pl.ds(0, 8 * NB)]
    press, pbuf = smooth, gdens
    hot = R.at[pl.ds(8 * NB, 2 * W128)]
    right = R.at[pl.ds(R.shape[0] // 2, 13 * EXT)]
    lev = level[...]
    scale = jnp.where(lev == 0, 1.0, jnp.where(lev == 1, SHRINK, SHRINK * SHRINK)).astype(f32)
    smooth[...] = smoothing[...] * jnp.broadcast_to(scale, (NB, W128)).T
    for c in range(3):
        pos[c] = pos_in[:, c, :]
    lane = lax.broadcasted_iota(jnp.int32, (1, NB), 1)

    def gather(n, _):
        for g in range(SLOTS):
            t = send_list[0, g, n]
            for c in range(3):
                buf[n, c, g:g + 1, :] = pos[c, pl.ds(t, 1), :]
            buf[n, 3, g:g + 1, :] = mass[pl.ds(t, 1), :]
            buf[n, 4, g:g + 1, :] = smooth[pl.ds(t, 1), :]
            hot[pl.ds(n * SLOTS + g, 1), :] = jnp.where(lane == t, 1.0, 0.0)
        return 0

    hot[pl.ds(GHOSTS, 2 * W128 - GHOSTS), :] = jnp.zeros((2 * W128 - GHOSTS, W128), f32)
    lax.fori_loop(0, NEIGH, gather, 0)
    pl.semaphore_wait(barrier, NEIGH)
    copies = start_all(buf, ghost, send_sem, recv_sem, 1)

    npairs = pairs.shape[2]
    live = lax.broadcasted_iota(jnp.int32, (1, npairs), 1) < count[0]
    idx[...] = jnp.zeros_like(idx)
    idx[2:4, :] = jnp.full((2, idx.shape[1]), EXT, jnp.int32)
    first = pairs[0, 0:1, :]
    second = pairs[0, 1:2, :]
    idx[0:1, :npairs] = first
    idx[1:2, :npairs] = second
    idx[2:3, :npairs] = jnp.where(live, first, NB)
    idx[3:4, :npairs] = jnp.where(live, second, EXT)
    pair_matrices(idx, hot_a, hot_b)
    for i in range(2):
        hot_o[:, i * W128:(i + 1) * W128] = hot[i * W128:(i + 1) * W128].T.astype(bf16)
    slots = R.shape[0] // 16
    R[npairs * 8:slots * 8] = jnp.zeros(((slots - npairs) * 8, W128), f32)
    R[(slots + npairs) * 8:] = jnp.zeros(((slots - npairs) * 8, W128), f32)
    RT[...] = jnp.zeros_like(RT)
    clear_right(right, EXT)
    v = scaled_columns(pos[0], pos[1], pos[2], mass[...], smooth[...])
    fill_right(right, EXT, 0, NB, v)
    fill_left(left, v)

    own_first = (KEEP - 2) * CHUNK
    chunks = npairs // CHUNK

    def features(g):
        for j in range(SELF):
            b = g * SELF + j
            right_features(right, EXT, b, BF, b)
            left_features(left, b, AF, b)

    def product(a, b, j):
        GB[j] = jnp.dot(AF[a], BF[b], preferred_element_type=f32)

    def own_copy(g):
        return pltpu.make_async_copy(T.at[pl.ds(own_first + g * SELF, SELF)], own_h.at[pl.ds(g * SELF, SELF)], own_sem.at[g])

    features(0)
    for j in range(SELF):
        product(j, j, j)
    features(1)

    def own_body(g, _):
        after = jnp.minimum(g + 1, NB // SELF - 1)
        for j in range(SELF):
            part = jnp.zeros((8, W128), f32)
            for r in range(0, W128, 8):
                W, S = tile_math(GB[j, r:r + 8, :W128], GB[j, r:r + 8, W128:])
                T[own_first + g * SELF + j, r:r + 8] = S
                part = part + W
            self_sum[pl.ds(g * SELF + j, 1), :] = jnp.sum(part, axis=0, keepdims=True)
        own_copy(g).start()
        for j in range(SELF):
            product(after * SELF + j, after * SELF + j, j)
        features(jnp.minimum(g + 2, NB // SELF - 1))
        return 0

    lax.fori_loop(0, NB // SELF, own_body, 0)
    for copy in copies:
        copy.wait()

    for n in range(NEIGH):
        fill_right(right, EXT, NB + n * SLOTS, SLOTS, scaled_columns(*[ghost[n, c] for c in range(5)]))

    def ghost_features(i, _):
        for j in range(8):
            right_features(right, EXT, i * 8 + j, BF, i * 8 + j)
        return 0

    lax.fori_loop(NB // 8, EXT // 8, ghost_features, 0)
    for j in range(UNROLL):
        product(pair_ends[0, 0, j], pair_ends[0, 1, j], j)
    lanes = lax.broadcasted_iota(jnp.int32, (8, W128), 1)

    def spill_out(c):
        at = pl.ds(c * CHUNK, CHUNK)
        return pltpu.make_async_copy(T.at[at], tiles_h.at[at], tile_sem.at[c])

    def spill_back(c, place):
        return pltpu.make_async_copy(tiles_h.at[pl.ds(c * CHUNK, CHUNK)], T.at[pl.ds(place * CHUNK, CHUNK)],
                                     tile_sem.at[chunks - KEEP + c])

    def pair_body(c, u, _):
        k0 = c * CHUNK + u * UNROLL
        slot = lax.rem(c, KEEP) * CHUNK + u * UNROLL
        for j in range(UNROLL):
            here = lanes == lax.rem(k0 + j, W128)
            column = lax.div(k0 + j, W128)
            part = jnp.zeros((8, W128), f32)
            for r in range(0, W128, 8):
                W, S = tile_math(GB[j, r:r + 8, :W128], GB[j, r:r + 8, W128:])
                T[slot + j, r:r + 8] = S
                part = part + W
                RT[column, r:r + 8] = jnp.where(here, jnp.sum(W, axis=1, keepdims=True), RT[column, r:r + 8])
            R[pl.ds(pl.multiple_of((k0 + j) * 8, 8), 8), :] = part
            k = jnp.minimum(k0 + UNROLL + j, npairs - 1)
            product(pair_ends[0, 0, k], pair_ends[0, 1, k], j)
        return 0

    def own_landed(g, _):
        own_copy(g).wait()
        return 0

    def chunk_body(c, _):
        @pl.when(c == KEEP - 2)
        def _():
            lax.fori_loop(0, NB // SELF, own_landed, 0)

        @pl.when(c >= KEEP)
        def _():
            spill_out(c - KEEP).wait()

        lax.fori_loop(0, CHUNK // UNROLL, functools.partial(pair_body, c), 0)

        @pl.when(c < chunks - KEEP)
        def _():
            spill_out(c).start()

        return 0

    lax.fori_loop(0, chunks, chunk_body, 0)

    dot = functools.partial(jnp.dot, preferred_element_type=f32)
    part = R[pl.ds(0, slots, stride=8), :]
    for i in range(1, 8):
        part = part + R[pl.ds(i, slots, stride=8), :]
    hi, lo = hilo(part)
    away = dot(hot_b[NB:], hi) + dot(hot_b[NB:], lo)
    for n in range(NEIGH):
        gdens[n] = away[n * SLOTS:(n + 1) * SLOTS] * (4.0 * NORM) / ghost[n, 3]
    copies = start_all(gdens, ret, s1, r1, -1)
    rows = jnp.zeros((W128, NB), f32)
    for w in range(RT.shape[0]):
        for p in hilo(RT[w]):
            rows = rows + lax.dot_general(p, hot_a[:, w * W128:(w + 1) * W128], (((1,), (1,)), ((), ())),
                                          preferred_element_type=f32)
    home = dot(hot_b[:NB], hi) + dot(hot_b[:NB], lo)
    mine = (home + rows.T + self_sum[...]) * (4.0 * NORM) / mass[...]

    def weights(at, rows, x, y, z, m, p):
        k = inverse_cube_root(m)
        w = k * k
        pw = p * w
        for i, v in enumerate((w, w * x, w * y, w * z, pw, pw * x, pw * y, pw * z)):
            C[i * EXT + at:i * EXT + at + rows] = v

    def columns(i, _):
        for j in range(4):
            b = i * 4 + j
            v = C[pl.ds(b, 8, stride=EXT), :]
            hi = v.astype(bf16).astype(f32)
            mm = jnp.concatenate([hi, v - hi], 0).astype(bf16)
            MM[b, :, :W128] = mm
            MM[b, :, W128:] = mm
        return 0

    for copy in copies:
        copy.wait()
    dens = mine + split_dot(hot_o[:, :GHOSTS], ret[...].reshape(GHOSTS, W128))
    dens_o[...] = dens
    press[...] = GAMMA_LESS * energy[...] / dens

    def gather_press(n, _):
        for g in range(SLOTS):
            pbuf[n, g:g + 1, :] = press[pl.ds(send_list[0, g, n], 1), :]
        return 0

    lax.fori_loop(0, NEIGH, gather_press, 0)
    copies = start_all(pbuf, gpress, s2, r2, 1)

    weights(0, NB, pos[0], pos[1], pos[2], mass[...], press[...])
    lax.fori_loop(0, NB // 4, columns, 0)

    def to_b(k, hi, lo):
        return jnp.dot(MM[pair_ends[0, 0, k]], jnp.concatenate([hi, lo], 0), preferred_element_type=f32)

    def to_a(k, hi, lo):
        return lax.dot_general(MM[pair_ends[0, 1, k]], jnp.concatenate([hi, lo], 1), (((1,), (1,)), ((), ())),
                               preferred_element_type=f32)

    def put(ref, k, v):
        ref[pl.ds(pl.multiple_of(k * 8, 8), 8), :] = v[:8] + v[8:]

    def own_sums(u, _):
        out = []
        for j in range(16):
            a = u * 16 + j
            hi, lo = hilo(T[own_first + a])
            out.append((a, jnp.dot(MM[a], jnp.concatenate([hi, lo], 0), preferred_element_type=f32)))
        for a, v in out:
            put(RS, a, v)
        return 0

    def pair_sums(do_a, do_b, c, place, u, _):
        out = []
        for j in range(FORCE_UNROLL):
            k = c * CHUNK + u * FORCE_UNROLL + j
            hi, lo = hilo(T[place * CHUNK + u * FORCE_UNROLL + j])
            if do_b:
                out.append((slots + k, to_b(k, hi, lo)))
            if do_a:
                out.append((k, to_a(k, hi, lo)))
        for k, v in out:
            put(R, k, v)
        return 0

    def chunk_sums(do_a, do_b, c, place):
        lax.fori_loop(0, CHUNK // FORCE_UNROLL, functools.partial(pair_sums, do_a, do_b, c, place), 0)

    def early(do_a, do_b, i, _):
        chunk_sums(do_a, do_b, KEEP + i, i)
        return 0

    lax.fori_loop(0, chunks - KEEP, functools.partial(early, False, True), 0)
    for copy in copies:
        copy.wait()
    for n in range(NEIGH):
        weights(NB + n * SLOTS, SLOTS, *[ghost[n, c] for c in range(4)], gpress[n])
    lax.fori_loop(NB // 4, EXT // 4, columns, 0)
    own_back = pltpu.make_async_copy(own_h, T.at[pl.ds(own_first, NB)], tile_sem.at[2 * (chunks - KEEP)])

    def rest(i, _):
        c = lax.rem(chunks - KEEP + i, KEEP)
        place = KEEP - 2 + lax.rem(i, 2)

        @pl.when(i >= 2)
        def _():
            spill_back(c, place).wait()

        chunk_sums(True, True, c, place)

        @pl.when(i + 2 < KEEP)
        def _():
            spill_back(lax.rem(chunks - KEEP + i + 2, KEEP), place).start()

        return 0

    lax.fori_loop(0, KEEP, rest, 0)
    own_back.start()

    def block_sums(halves):
        A = []
        for c in range(0, 8, 2):
            total = None
            for half, matrix in halves:
                v = [R[pl.ds(half * slots * 8 + c + i, slots, stride=8), :] for i in range(2)]
                hi, lo = hilo(jnp.concatenate(v, 1))
                term = dot(matrix, hi) + dot(matrix, lo)
                total = term if total is None else total + term
            A += [total[:, :W128], total[:, W128:]]
        return A

    scale = -20.0 * NORM

    def final(p, m, spot, A):
        k = inverse_cube_root(m)
        k2 = k * k
        own = p * A[0] + A[4]
        return [(p * A[c + 1] + A[c + 5] - v * own) * (scale * (k2 * k2 * k)) for c, v in enumerate(spot)]

    A = block_sums([(1, hot_b[NB:])])
    for n in range(NEIGH):
        r = slice(n * SLOTS, (n + 1) * SLOTS)
        for c, v in enumerate(final(gpress[n], ghost[n, 3], [ghost[n, c] for c in range(3)], [x[r] for x in A])):
            gacc[n, c] = v
    copies = start_all(gacc, racc, s3, r3, -1)
    lax.fori_loop(0, chunks - KEEP, functools.partial(early, True, False), 0)
    own_back.wait()
    lax.fori_loop(0, NB // 16, own_sums, 0)
    A = [x + RS[pl.ds(c, NB, stride=8), :] for c, x in enumerate(block_sums([(0, hot_a[...]), (1, hot_b[:NB])]))]
    mine = final(press[...], mass[...], [pos[c] for c in range(3)], A)
    for copy in copies:
        copy.wait()
    for c in range(3):
        acc_o[:, c, :] = mine[c] + split_dot(hot_o[:, :GHOSTS], racc[:, c].reshape(GHOSTS, W128))


V = pl.BlockSpec(memory_space=pltpu.VMEM)
SM = pl.BlockSpec(memory_space=pltpu.SMEM)
sds = jax.ShapeDtypeStruct


def run_whole(send_list, pair_count, pair_list, pos, mass, smoothing, energy, level):
    D = pltpu.SemaphoreType.DMA((NEIGH,))
    vm = pltpu.VMEM
    A = pl.BlockSpec(memory_space=pl.ANY)
    pairs = pair_list.shape[2]
    slots = pairs + (-pairs) % (2 * W128)
    one = vm((NB, W128), f32)
    eight = vm((NEIGH, SLOTS, W128), f32)
    three = vm((NEIGH, 3, SLOTS, W128), f32)
    five = vm((NEIGH, 5, SLOTS, W128), f32)
    return pl.pallas_call(
        whole_kernel,
        out_shape=[sds((NB, W128), f32), sds((NB, 3, W128), f32), sds((NB, W128, W128), f32),
                   sds((pairs - KEEP * CHUNK, W128, W128), f32)],
        in_specs=[SM, SM, SM, V, V, V, V, V, V], out_specs=[V, V, A, A],
        scratch_shapes=[
            five, vm((4, slots), jnp.int32), vm((NB, 2 * W128), bf16), vm((3, NB, W128), f32), one, one, eight, five,
            vm((8 * EXT, W128), f32), vm((NB, W128, 64), bf16),
            vm((EXT, 64, 2 * W128), bf16), vm((UNROLL, W128, 2 * W128), f32), vm((KEEP * CHUNK, W128, W128), f32),
            vm((slots // W128, W128, W128), f32), vm((2 * slots * 8, W128), f32), vm((NB * 8, W128), f32),
            vm((EXT, 16, 2 * W128), bf16), vm((NB, slots), bf16), vm((EXT, slots), bf16),
            eight, eight, three, three,
            D, D, pltpu.SemaphoreType.DMA((NB // SELF,)), pltpu.SemaphoreType.DMA((2 * (pairs // CHUNK - KEEP) + 1,)), D, D, D, D, D, D],
        compiler_params=pltpu.CompilerParams(collective_id=0, has_side_effects=True, vmem_limit_bytes=VMEM),
        name="whole")(send_list, pair_count, pair_list, pair_list, pos, mass, smoothing, energy, level)


def leave_kernel(dens, acc, dens_o, acc_o):
    dens_o[...] = dens[...]
    acc_o[...] = acc[...]


def leave(dens, acc):
    return pl.pallas_call(
        leave_kernel, out_shape=[sds(dens.shape, f32), sds(acc.shape, f32)], in_specs=[V, V], out_specs=[V, V],
        compiler_params=pltpu.CompilerParams(vmem_limit_bytes=VMEM), name="leave")(dens, acc)


def per_device(positions, masses, smoothing, energy, level_ids, send_list, pair_list, pair_count):
    mass = masses.reshape(NB, W128)
    density, accel, _, _ = run_whole(
        send_list.transpose(0, 2, 1), pair_count, pair_list, positions.reshape(3, NB, W128).transpose(1, 0, 2), mass,
        smoothing.reshape(NB, W128), energy.reshape(NB, W128), level_ids.reshape(1, NB))
    density, accel = leave(density, accel)
    return density.reshape(NB * W128), accel.transpose(1, 0, 2).reshape(3, NB * W128)


def solution(mesh):
    both = ("patch", "bulk")
    placed = (P(None, both), P(both), P(both), P(both), P(both), P(both, None, None), P(both, None, None), P(both))
    return jax.shard_map(per_device, mesh=mesh, in_specs=placed, out_specs=(P(both), P(None, both)), check_vma=False)
```
